128 devices in a mesh: section: 2 (over z_hi), dp: 16 (over z_lo, x, core), tensor: 4 (over y).
Axes of the slice: x: 4, y: 4, z: 4 (z_hi: 2, z_lo: 2; z = z_hi * 2 + z_lo), core: 2. Of those that a mesh axis runs over, the one named last changes fastest.
Arguments:
- tokens: bfloat16 [2, 8192, 1024], P(None, ('dp', 'tensor')), may hold values from -6 to 6
- cotangent: bfloat16 [2, 8192, 1024], P(None, ('dp', 'tensor')), may hold values from -6 to 6
- lengths: int32 [2, 16, 4], P(None, 'dp'), may hold values from 1 to 386, 512 in all within a row
- gains: float32 [2, 2, 1024], P('section'), may hold values from 0.25 to 1.75
- w_qkv: bfloat16 [2, 1024, 3, 1024], P('section', None, None, 'tensor'), may hold values from -0.1875 to 0.1875
- w_out: bfloat16 [2, 1024, 1024], P('section', 'tensor'), may hold values from -1.5 to 1.5
- w_up: bfloat16 [2, 1024, 2, 2624], P('section', None, None, 'tensor'), may hold values from -0.1875 to 0.1875
- w_down: bfloat16 [2, 2624, 1024], P('section', 'tensor'), may hold values from -0.125 to 0.125
Outputs:
- section_out: bfloat16 [2, 2, 8192, 1024], P('section', None, ('dp', 'tensor'))
- input_grads: bfloat16 [2, 2, 8192, 1024], P('section', None, ('dp', 'tensor'))
- grad_gains: float32 [2, 2, 1024], P('section')
- grad_qkv: float32 [2, 1024, 3, 1024], P('section', None, None, 'tensor')
- grad_out: float32 [2, 1024, 1024], P('section', 'tensor')
- grad_up: float32 [2, 1024, 2, 2624], P('section', None, None, 'tensor')
- grad_down: float32 [2, 2624, 1024], P('section', 'tensor')
The draws below stay inside these ranges and needn't reach their ends.
Inputs may be any that keep to these rules, and one draw needn't show every extreme that they name: `lengths`: in each group's micro-batch the 4 documents fill all 512 rows; the longest has exactly 386 rows.
All inputs are finite; a program needn't handle non-finite values.
Results may differ from the reference program's by a relative error of at most 0.03.
Values may be sent and summed in bfloat16 or wider, within the bound.
No kernel may reach another device: no remote copies, remote signals or barrier semaphores. Data moves between devices by JAX's collectives and lax.ppermute only.
A program may use at most 192 MiB of HBM per device.

```python
import math
import jax
import jax.numpy as jnp
import numpy as np
from jax import lax

D = 1024
HEADS = 16
HEAD_DIM = 64
FF = 2624
WINDOW = 128
MICRO = 2
NDOC = 4
SEQ_TOK = 512
TOKENS_MB = 8192
LONGEST = 386
N_DP = 16


def level_of(key, extent, shards, least, high):
    def one(position, shards_of):
        steps = jax.random.uniform(jax.random.fold_in(jax.random.fold_in(key, 6), position), (shards_of,), jnp.float32, least / len(shards), high / len(shards))
        return jnp.repeat(jnp.exp(steps), extent[position] // shards_of).reshape((-1,) + (1,) * (len(extent) - position - 1))

    level = one(*shards[0])
    for cut in shards[1:]:
        level = level * one(*cut)
    return level


def split_up(number_of, total, most, skew):
    portions = [(1 << 20) // math.isqrt(grade ** skew) + 1 for grade in range(2, number_of + 1)]
    surplus, given = total - most - (number_of - 1), [1] * (number_of - 1)
    while surplus > 0:
        movable = [i for i in range(number_of - 1) if given[i] < most]
        mass, budget = sum([portions[i] for i in movable]), surplus
        for i in movable:
            more = min(most - given[i], max(1, budget * portions[i] // mass), surplus)
            given[i] = given[i] + more
            surplus = surplus - more
    return np.array([most] + given)


def uneven_parts(stream_key, count, total, most, lean):
    if count == 2:
        one = jax.random.randint(stream_key, (), max(1, total - most), min(most, total - 1) + 1)
        return jnp.stack([one, total - one])
    sizes = jnp.asarray(split_up(count, total, most, lean), jnp.int32)
    couples = (count - 1) // 2
    source_of, sink = sizes[1:1 + 2 * couples:2], sizes[2:2 + 2 * couples:2]
    room = jnp.minimum(source_of - 1, most - sink)
    moved = jax.random.randint(jax.random.fold_in(stream_key, 1), (couples,), 0, 1 << 20) % (room + 1)
    sizes = sizes.at[1:1 + 2 * couples:2].set(source_of - moved).at[2:2 + 2 * couples:2].set(sink + moved)
    return sizes[jax.random.permutation(jax.random.fold_in(stream_key, 2), count)]


def bell_draw(key, dims, spread, limit, cuts=(), kind=jnp.bfloat16):
    array = spread * jax.random.normal(key, dims, jnp.float32)
    if cuts:
        array = array * level_of(key, dims, cuts, -0.22, 0.18)
    return jnp.clip(array, -limit, limit).astype(kind)


def setup_inputs(seed: int = 0) -> dict:
    keys = jax.random.split(jax.random.key(seed), 9)
    return {
        "tokens": bell_draw(keys[0], (MICRO, TOKENS_MB, D), 1.0, 6.0, ((1, 64),)),
        "cotangent": bell_draw(keys[1], (MICRO, TOKENS_MB, D), 1.0, 6.0, ((1, 64),)),
        "lengths": jax.vmap(lambda own: uneven_parts(own, NDOC, SEQ_TOK, LONGEST, 2))(jax.random.split(keys[2], MICRO * N_DP)).reshape((MICRO, N_DP, NDOC)).astype(jnp.int32),
        "gains": jnp.clip(1.0 + 0.15 * jax.random.normal(keys[3], (2, 2, D), jnp.float32), 0.25, 1.75),
        "w_qkv": bell_draw(keys[4], (2, D, 3, D), D ** -0.5, 0.1875, ((0, 2), (3, 4))),
        "w_out": bell_draw(keys[5], (2, D, D), (max(D // 64, 4)) ** -0.5, 1.5, ((0, 2), (1, 4))),
        "w_up": bell_draw(keys[6], (2, D, 2, FF), D ** -0.5, 0.1875, ((0, 2), (3, 4))),
        "w_down": bell_draw(keys[7], (2, FF, D), FF ** -0.5, 0.125, ((0, 2), (1, 4))),
    }


@jax.custom_vjp
def low(v):
    return lax.optimization_barrier(v.astype(jnp.bfloat16)).astype(jnp.float32)

@jax.custom_vjp
def low_back(v):
    return v

def low_keep(v):
    return (low(v), None)

def low_pass(kept, grad):
    return (grad,)

def back_keep(v):
    return (v, None)

def back_low(kept, grad):
    return (low(grad),)
low.defvjp(low_keep, low_pass)
low_back.defvjp(back_keep, back_low)
epsilon = 1e-05
highest = lax.Precision.HIGHEST

def layer_norm(values, gain_scale):
    centered = values - lax.optimization_barrier(jnp.mean(values, axis=-1, keepdims=True))
    variance = lax.optimization_barrier(jnp.mean(centered * centered, axis=-1, keepdims=True))
    return centered * lax.rsqrt(variance + epsilon) * gain_scale

def doc_layout(doc_lengths, total_rows):
    indices = jnp.arange(total_rows, dtype=jnp.int32)
    doc_ends = jnp.cumsum(doc_lengths).astype(jnp.int32)
    passed = indices[:, None] >= doc_ends[None, :]
    doc_ids = lax.optimization_barrier(jnp.sum(passed.astype(jnp.int32), axis=1)).astype(jnp.int32)
    starts = lax.optimization_barrier(jnp.sum(jnp.where(passed, doc_lengths[None, :], 0), axis=1)).astype(jnp.int32)
    return (doc_ids, (indices - starts).astype(jnp.int32))

def rope_tables(positions, rope_base):
    half_dim = HEAD_DIM // 2
    inverse = rope_base ** (-2.0 * jnp.arange(half_dim, dtype=jnp.float32) / HEAD_DIM)
    angles = positions.astype(jnp.float32)[..., None] * inverse
    angles = jnp.concatenate([angles, angles], axis=-1)
    return (jnp.cos(angles), jnp.sin(angles))

def rotate(values, cosine_table, sine_table):
    half_dim = values.shape[-1] // 2
    turned = jnp.concatenate([-values[..., half_dim:], values[..., :half_dim]], axis=-1)
    return values * cosine_table[..., None, :] + turned * sine_table[..., None, :]

def section_layer(inputs, gain_pair, w_qkv, w_out, w_up, w_down, doc_ids, positions, reach_rows, rope_base):
    blocks, length_rows, model_width = inputs.shape
    normed = low(layer_norm(inputs, gain_pair[0]))
    projected = low_back(jnp.einsum('bsd,dce->bsce', normed, w_qkv, precision=highest))
    projected = projected.reshape(blocks, length_rows, 3, HEADS, HEAD_DIM)
    cosine_table, sine_table = rope_tables(positions, rope_base)
    queries = low(rotate(projected[:, :, 0], cosine_table, sine_table))
    keys_rot = low(rotate(projected[:, :, 1], cosine_table, sine_table))
    values_in = low(projected[:, :, 2])
    indices = jnp.arange(length_rows, dtype=jnp.int32)
    near_pairs = jnp.abs(indices[:, None] - indices[None, :]) <= reach_rows

    def attend(pieces):
        block_queries, block_keys, block_values, block_docs = pieces
        allowed = (block_docs[:, None] == block_docs[None, :]) & near_pairs
        scores = low_back(jnp.einsum('qhd,khd->hqk', block_queries, block_keys, precision=highest) * HEAD_DIM ** (-0.5))
        scores = jnp.where(allowed[None], scores, -1e+30)
        soft_weights = low(jax.nn.softmax(scores, axis=-1))
        return jnp.einsum('hqk,khd->qhd', soft_weights, block_values, precision=highest)
    attended = lax.map(jax.checkpoint(attend), (queries, keys_rot, values_in, doc_ids))
    attended = low(low_back(attended.reshape(blocks, length_rows, model_width)))
    resid_mid = inputs + low_back(jnp.einsum('bse,ed->bsd', attended, w_out, precision=highest))
    normed_mid = low(layer_norm(resid_mid, gain_pair[1]))
    hidden = low_back(jnp.einsum('bsd,dcf->bscf', normed_mid, w_up, precision=highest))
    mixed_rows = low(jax.nn.gelu(hidden[:, :, 0], approximate=False) * hidden[:, :, 1])
    return resid_mid + low_back(jnp.einsum('bsf,fd->bsd', mixed_rows, w_down, precision=highest))

def reference(tokens, cotangent, lengths, gains, w_qkv, w_out, w_up, w_down):
    blocks = MICRO * N_DP
    doc_ids, positions = jax.vmap(lambda row_lengths: doc_layout(row_lengths, SEQ_TOK))(lengths.reshape(blocks, NDOC))
    start_rows = tokens.astype(jnp.float32).reshape(blocks, SEQ_TOK, D)
    probe_rows = jnp.zeros_like(start_rows)

    def forward(start_in, gains_all, qkv_all, out_all, up_all, down_all, probe_in):
        first_out = section_layer(start_in, gains_all[0], qkv_all[0], out_all[0], up_all[0], down_all[0], doc_ids, positions, WINDOW // 2, 10000.0)
        handed = low_back(low(first_out) + probe_in)
        second = section_layer(handed, gains_all[1], qkv_all[1], out_all[1], up_all[1], down_all[1], doc_ids, positions, SEQ_TOK, 160000.0)
        return (second, first_out)
    second, pull_back, first_out = jax.vjp(forward, start_rows, gains.astype(jnp.float32), w_qkv.astype(jnp.float32), w_out.astype(jnp.float32), w_up.astype(jnp.float32), w_down.astype(jnp.float32), probe_rows, has_aux=True)
    gradients = pull_back(cotangent.astype(jnp.float32).reshape(blocks, SEQ_TOK, D))
    shape_out = (2, MICRO, TOKENS_MB, D)
    section_out = jnp.stack([low(first_out), second]).reshape(shape_out).astype(jnp.bfloat16)
    input_grads = jnp.stack([gradients[0], gradients[6]]).reshape(shape_out).astype(jnp.bfloat16)
    return (section_out, input_grads, gradients[1], gradients[2], gradients[3], gradients[4], gradients[5])
```

```python
import jax
import jax.numpy as jnp
from jax import lax
from jax.sharding import Mesh
from jax.sharding import PartitionSpec as P

HEAD_DIM = 64
WINDOW = 128

epsilon = 1e-05
bf16 = jnp.bfloat16
f32 = jnp.float32

DP = ("zlo", "x", "core")


def around(block, axis, distance):
    count = lax.axis_size(axis)
    return lax.ppermute(block, axis, [(i, (i + distance) % count) for i in range(count)])


def swap_core(block):
    return lax.ppermute(block, "core", [(0, 1), (1, 0)])


def swap_section(block):
    return lax.ppermute(block, "section", [(0, 1), (1, 0)])


def swap_layer(block):
    return lax.ppermute(block, ("section", "zlo"), [(0, 3), (1, 2), (2, 1), (3, 0)])


def gather_rows(block):
    ahead2 = around(block, "tensor", 2)
    ahead1 = around(block, "tensor", -1)
    ahead3 = around(block, "tensor", 1)
    return jnp.concatenate([block, ahead1, ahead2, ahead3], axis=0)


def scatter_rows(terms, row_count):
    parts = [terms[k * row_count : (k + 1) * row_count] for k in range(4)]
    sent2 = around(parts[2].astype(bf16), "tensor", 2)
    sent1 = around(parts[1].astype(bf16), "tensor", 1)
    sent3 = around(parts[3].astype(bf16), "tensor", -1)
    return (
        parts[0].astype(f32) + sent2.astype(f32) + sent1.astype(f32) + sent3.astype(f32)
    )


def sum_tensor(block):
    return (
        block
        + around(block, "tensor", 2)
        + around(block, "tensor", 1)
        + around(block, "tensor", -1)
    )


def layer_norm(values, gain_scale):
    centered = values - jnp.mean(values, axis=-1, keepdims=True)
    variance = jnp.mean(centered * centered, axis=-1, keepdims=True)
    return centered * lax.rsqrt(variance + epsilon) * gain_scale


def doc_layout(doc_lengths, indices):
    doc_ends = jnp.cumsum(doc_lengths)
    passed = indices[:, None] >= doc_ends[None, :]
    doc_ids = jnp.sum(passed.astype(jnp.int32), axis=1)
    starts = jnp.sum(jnp.where(passed, doc_lengths[None, :], 0), axis=1)
    return (doc_ids, indices - starts)


def rope_tables(positions, rope_base):
    half_dim = HEAD_DIM // 2
    inverse = rope_base ** (-2.0 * jnp.arange(half_dim, dtype=f32) / HEAD_DIM)
    angles = positions.astype(f32)[..., None] * inverse
    angles = jnp.concatenate([angles, angles], axis=-1)
    return (jnp.cos(angles), jnp.sin(angles))


def rotate(values, cosine_table, sine_table):
    half_dim = values.shape[-1] // 2
    turned = jnp.concatenate([-values[..., half_dim:], values[..., :half_dim]], axis=-1)
    return values * cosine_table[..., None, :] + turned * sine_table[..., None, :]


def rotate_back(gradients, cosine_table, sine_table):
    half_dim = gradients.shape[-1] // 2
    scaled = gradients * sine_table[..., None, :]
    turned = jnp.concatenate([scaled[..., half_dim:], -scaled[..., :half_dim]], axis=-1)
    return gradients * cosine_table[..., None, :] + turned


def masked_scores(queries, keys_rot, allowed):
    scores = jnp.einsum(
        "qhd,khd->hqk", queries, keys_rot, preferred_element_type=f32
    ) * HEAD_DIM ** (-0.5)
    return jnp.where(allowed[None], scores, -1e30)


def contract_rows(left_rows, right_rows):
    return lax.dot_general(
        left_rows, right_rows, (((0,), (0,)), ((), ())), preferred_element_type=f32
    )


def contract_last(left_rows, weight):
    return lax.dot_general(
        left_rows, weight, (((1,), (1,)), ((), ())), preferred_element_type=f32
    )


def times(left_rows, weight):
    return jnp.dot(left_rows, weight, preferred_element_type=f32)


def forward_layer(inputs, gain_pair, weights, allowed, tables):
    w_qkv, w_out, w_up, w_down = weights
    row_count = inputs.shape[0]
    normed_all = gather_rows(layer_norm(inputs, gain_pair[0]).astype(bf16))
    full_rows = normed_all.shape[0]
    local_width = w_out.shape[0]
    projected = times(normed_all, w_qkv).reshape(full_rows, 3, -1, HEAD_DIM)
    queries = rotate(projected[:, 0], *tables).astype(bf16)
    keys_rot = rotate(projected[:, 1], *tables).astype(bf16)
    values_in = projected[:, 2].astype(bf16)
    scores = masked_scores(queries, keys_rot, allowed)
    largest = jnp.max(scores, axis=2, keepdims=True)
    exp_scores = jnp.exp(scores - largest)
    totals = jnp.sum(exp_scores, axis=2, keepdims=True)
    soft_weights = (exp_scores / totals).astype(bf16)
    log_totals = largest + jnp.log(totals)
    attended = jnp.einsum("hqk,khd->qhd", soft_weights, values_in, preferred_element_type=f32)
    attended = attended.reshape(full_rows, local_width).astype(bf16)
    resid_mid = inputs + scatter_rows(times(attended, w_out), row_count)
    normed_mid_all = gather_rows(layer_norm(resid_mid, gain_pair[1]).astype(bf16))
    hidden = times(normed_mid_all, w_up)
    local_hidden = hidden.shape[1] // 2
    gelu_in = hidden[:, :local_hidden]
    gate_mult = hidden[:, local_hidden:]
    mixed_rows = (jax.nn.gelu(gelu_in, approximate=False) * gate_mult).astype(bf16)
    result = resid_mid + scatter_rows(times(mixed_rows, w_down), row_count)
    kept = (
        inputs,
        resid_mid,
        normed_all,
        queries,
        keys_rot,
        values_in,
        log_totals,
        attended,
        normed_mid_all,
        gelu_in,
        gate_mult,
        mixed_rows,
    )
    return (result, kept)


def gelu_product(first_half, second_half):
    return jax.nn.gelu(first_half, approximate=False) * second_half


def backward_ffn(grad_result, kept, gain_pair, weights):
    w_up, w_down = weights[2], weights[3]
    resid_mid, normed_mid_all = kept[1], kept[8]
    gelu_in, gate_mult, mixed_rows = kept[9], kept[10], kept[11]
    row_count = grad_result.shape[0]
    grad_ffn_all = gather_rows(grad_result.astype(bf16))
    grad_mixed = contract_last(grad_ffn_all, w_down)
    unused, pull_gelu = jax.vjp(gelu_product, gelu_in, gate_mult)
    grad_gelu, grad_gate = pull_gelu(grad_mixed)
    grad_hidden = jnp.concatenate([grad_gelu, grad_gate], axis=1).astype(bf16)
    grad_normed_mid = scatter_rows(contract_last(grad_hidden, w_up), row_count)
    unused, pull_norm = jax.vjp(layer_norm, resid_mid, gain_pair[1])
    grad_resid, grad_gain = pull_norm(grad_normed_mid)
    grad_w_down = contract_rows(mixed_rows, grad_ffn_all).astype(bf16)
    grad_w_up = contract_rows(normed_mid_all, grad_hidden).astype(bf16)
    return (grad_result + grad_resid, grad_w_up, grad_w_down, grad_gain)


def backward_attn(grad_mid, kept, gain_pair, weights, allowed, tables):
    w_qkv, w_out = weights[0], weights[1]
    inputs, normed_all = kept[0], kept[2]
    queries, keys_rot, values_in, log_totals, attended = kept[3:8]
    row_count = grad_mid.shape[0]
    full_rows = normed_all.shape[0]
    grad_att_all = gather_rows(grad_mid.astype(bf16))
    grad_attended = contract_last(grad_att_all, w_out).astype(bf16).reshape(queries.shape)
    scores = masked_scores(queries, keys_rot, allowed)
    soft_exact = jnp.exp(scores - log_totals)
    soft_weights = soft_exact.astype(bf16)
    grad_values = jnp.einsum(
        "hqk,qhd->khd", soft_weights, grad_attended, preferred_element_type=f32
    )
    grad_soft = jnp.einsum("qhd,khd->hqk", grad_attended, values_in, preferred_element_type=f32)
    row_dots = jnp.sum(soft_exact * grad_soft, axis=2, keepdims=True)
    grad_scores = (soft_exact * (grad_soft - row_dots)).astype(bf16)
    grad_queries = jnp.einsum(
        "hqk,khd->qhd", grad_scores, keys_rot, preferred_element_type=f32
    ) * HEAD_DIM ** (-0.5)
    grad_keys = jnp.einsum(
        "hqk,qhd->khd", grad_scores, queries, preferred_element_type=f32
    ) * HEAD_DIM ** (-0.5)
    grad_projected = jnp.stack(
        [
            rotate_back(grad_queries, *tables),
            rotate_back(grad_keys, *tables),
            grad_values,
        ],
        axis=1,
    )
    grad_projected = grad_projected.astype(bf16).reshape(full_rows, -1)
    grad_normed = scatter_rows(contract_last(grad_projected, w_qkv), row_count)
    unused, pull_norm = jax.vjp(layer_norm, inputs, gain_pair[0])
    grad_resid, grad_gain = pull_norm(grad_normed)
    grad_w_out = contract_rows(attended, grad_att_all).astype(bf16)
    grad_w_qkv = contract_rows(normed_all, grad_projected).astype(bf16)
    return (grad_mid + grad_resid, grad_w_qkv, grad_w_out, grad_gain)


def other_layer(own, core_index):
    half = own.shape[0] // 2
    sent = jnp.where(core_index == 0, own[:half], own[half:])
    got = swap_layer(sent)
    beside = swap_core(got)
    low = jnp.where(core_index == 0, got, beside)
    high = jnp.where(core_index == 0, beside, got)
    return jnp.concatenate([low, high], axis=0)


def reduce_part(grads):
    core_index = lax.axis_index("core")
    half = grads.shape[0] // 2
    sent = jnp.where(core_index == 0, grads[half:], grads[:half])
    held = jnp.where(core_index == 0, grads[:half], grads[half:])
    both = (held.astype(f32) + swap_core(sent).astype(f32)).astype(bf16)
    return lax.psum_scatter(both, ("zlo", "x"), scatter_dimension=0, tiled=True)


def reduce_part_now(grads):
    core_index = lax.axis_index("core")
    half = grads.shape[0] // 2
    sent = jnp.where(core_index == 0, grads[half:], grads[:half])
    held = jnp.where(core_index == 0, grads[:half], grads[half:])
    both = (held.astype(f32) + swap_core(sent).astype(f32)).astype(bf16)
    pieces = lax.all_to_all(both, ("zlo", "x"), 0, 0, tiled=True)
    pieces = pieces.reshape(8, -1, pieces.shape[1])
    return jnp.sum(pieces.astype(f32), axis=0).astype(bf16)


def spread_part(part):
    core_index = lax.axis_index("core")
    half = lax.all_gather(part, ("zlo", "x"), axis=0, tiled=True)
    beside = swap_core(half)
    low = jnp.where(core_index == 0, half, beside)
    high = jnp.where(core_index == 0, beside, half)
    return jnp.concatenate([low, high], axis=0)


def pad_rows(block, rows):
    return jnp.concatenate([block, jnp.zeros((rows - block.shape[0], block.shape[1]), block.dtype)])


def join_sections(is_first, part_first, part_second):
    own = jnp.where(is_first, part_first, part_second)
    sent = jnp.where(is_first, part_second, part_first)
    return (own.astype(f32) + swap_section(sent).astype(f32)).astype(bf16)


def local(tokens, cotangent, lengths, gains, w_qkv, w_out, w_up, w_down):
    section_index = lax.axis_index("section")
    core_index = lax.axis_index("core")
    is_first = section_index == 0
    row_count = tokens.shape[1]
    full_rows = row_count * lax.axis_size("tensor")
    own = (
        w_qkv[0].reshape(w_qkv.shape[1], -1),
        w_out[0],
        w_up[0].reshape(w_up.shape[1], -1),
        w_down[0],
    )
    others = tuple(other_layer(weight, core_index) for weight in own)
    gains_other = swap_layer(gains[0])
    layer0 = tuple(jnp.where(is_first, a, b) for a, b in zip(own, others))
    layer1 = tuple(jnp.where(is_first, b, a) for a, b in zip(own, others))
    gains0 = jnp.where(is_first, gains[0], gains_other)
    gains1 = jnp.where(is_first, gains_other, gains[0])
    start_rows = jnp.where(is_first, tokens[0], tokens[1])
    end_grads = jnp.where(is_first, cotangent[0], cotangent[1])
    doc_lengths = jnp.where(is_first, lengths[0, 0], lengths[1, 0])
    indices = jnp.arange(full_rows, dtype=jnp.int32)
    indices = (indices + lax.axis_index("tensor") * row_count) % full_rows
    doc_ids, positions = doc_layout(doc_lengths, indices)
    same_doc = doc_ids[:, None] == doc_ids[None, :]
    near = jnp.abs(indices[:, None] - indices[None, :]) <= WINDOW // 2
    allowed0 = same_doc & near
    allowed1 = same_doc
    tables0 = rope_tables(positions, 10000.0)
    tables1 = rope_tables(positions, 160000.0)

    out0, kept0 = forward_layer(start_rows.astype(f32), gains0, layer0, allowed0, tables0)
    out0 = out0.astype(bf16)
    out1, kept1 = forward_layer(out0.astype(f32), gains1, layer1, allowed1, tables1)
    out1 = out1.astype(bf16)
    mid1, up1, down1, gain_mid1 = backward_ffn(end_grads.astype(f32), kept1, gains1, layer1)
    in1, qkv1, wout1, gain_first1 = backward_attn(mid1, kept1, gains1, layer1, allowed1, tables1)
    in1 = in1.astype(bf16)
    mid0, up0, down0, gain_mid0 = backward_ffn(in1.astype(f32), kept0, gains0, layer0)
    in0, qkv0, wout0, gain_first0 = backward_attn(mid0, kept0, gains0, layer0, allowed0, tables0)
    in0 = in0.astype(bf16)

    down_rows = down1.shape[0]
    padded = -(-down_rows // 256) * 256
    part_up1 = reduce_part(up1)
    part_down1 = reduce_part(pad_rows(down1, padded))
    part_qkv1 = reduce_part(qkv1)
    part_out1 = reduce_part(wout1)
    part_up0 = reduce_part(up0)
    part_down0 = reduce_part(pad_rows(down0, padded))
    up_sum = spread_part(join_sections(is_first, part_up0, part_up1))
    down_sum = spread_part(join_sections(is_first, part_down0, part_down1))[:down_rows]
    part_qkv0 = reduce_part_now(qkv0)
    part_out0 = reduce_part_now(wout0)
    qkv_sum = spread_part(join_sections(is_first, part_qkv0, part_qkv1))
    out_sum = spread_part(join_sections(is_first, part_out0, part_out1))

    gain0 = jnp.stack([gain_first0, gain_mid0])
    gain1 = jnp.stack([gain_first1, gain_mid1])
    gain_own = jnp.where(is_first, gain0, gain1)
    gain_sent = jnp.where(is_first, gain1, gain0)
    gain_total = gain_own + swap_section(gain_sent)
    gain_total = sum_tensor(gain_total)
    gain_total = gain_total + swap_core(gain_total)
    gain_total = (
        gain_total
        + around(gain_total, "x", 1)
        + around(gain_total, "x", 2)
        + around(gain_total, "x", 3)
    )
    gain_total = gain_total + around(gain_total, "zlo", 1)

    got_out = swap_section(jnp.where(is_first, out1, out0))
    section_out = jnp.stack(
        [jnp.where(is_first, out0, got_out), jnp.where(is_first, got_out, out1)]
    )
    got_in = swap_section(jnp.where(is_first, in1, in0))
    input_grads = jnp.stack(
        [jnp.where(is_first, in0, got_in), jnp.where(is_first, got_in, in1)]
    )
    return (
        section_out[None],
        input_grads[None],
        gain_total[None],
        qkv_sum.astype(f32).reshape(w_qkv.shape),
        out_sum.astype(f32)[None],
        up_sum.astype(f32).reshape(w_up.shape),
        down_sum.astype(f32)[None],
    )


def solution(mesh):
    sizes = dict(zip(mesh.axis_names, mesh.devices.shape))
    fine = Mesh(
        mesh.devices.reshape(sizes["section"], 2, sizes["dp"] // 4, 2, sizes["tensor"]),
        ("section", "zlo", "x", "core", "tensor"),
    )
    rows = ("zlo", "x", "core", "tensor")
    in_specs = (
        P(None, rows, None),
        P(None, rows, None),
        P(None, DP, None),
        P("section", None, None),
        P("section", None, None, "tensor"),
        P("section", "tensor", None),
        P("section", None, None, "tensor"),
        P("section", "tensor", None),
    )
    out_specs = (
        P("section", None, rows, None),
        P("section", None, rows, None),
        P("section", None, None),
        P("section", None, None, "tensor"),
        P("section", "tensor", None),
        P("section", None, None, "tensor"),
        P("section", "tensor", None),
    )
    return jax.shard_map(local, mesh=fine, in_specs=in_specs, out_specs=out_specs, check_vma=False)
```

```python
import jax
import jax.numpy as jnp
from jax import lax
from jax.sharding import Mesh
from jax.sharding import PartitionSpec as P

HEAD_DIM = 64
WINDOW = 128

epsilon = 1e-05
bf16 = jnp.bfloat16
f32 = jnp.float32

DP = ("zlo", "x", "core")


def around(block, axis, distance):
    count = lax.axis_size(axis)
    return lax.ppermute(block, axis, [(i, (i + distance) % count) for i in range(count)])


def swap_core(block):
    return lax.ppermute(block, "core", [(0, 1), (1, 0)])


def swap_section(block):
    return lax.ppermute(block, "section", [(0, 1), (1, 0)])


def swap_layer(block):
    return lax.ppermute(block, ("section", "zlo"), [(0, 3), (1, 2), (2, 1), (3, 0)])


def gather_rows(block):
    ahead2 = around(block, "tensor", 2)
    ahead1 = around(block, "tensor", -1)
    ahead3 = around(block, "tensor", 1)
    return jnp.concatenate([block, ahead1, ahead2, ahead3], axis=0)


def scatter_rows(terms, row_count):
    parts = [terms[k * row_count : (k + 1) * row_count] for k in range(4)]
    sent2 = around(parts[2].astype(bf16), "tensor", 2)
    sent1 = around(parts[1].astype(bf16), "tensor", 1)
    sent3 = around(parts[3].astype(bf16), "tensor", -1)
    return (
        parts[0].astype(f32) + sent2.astype(f32) + sent1.astype(f32) + sent3.astype(f32)
    )


def sum_tensor(block):
    return (
        block
        + around(block, "tensor", 2)
        + around(block, "tensor", 1)
        + around(block, "tensor", -1)
    )


def layer_norm(values, gain_scale):
    centered = values - jnp.mean(values, axis=-1, keepdims=True)
    variance = jnp.mean(centered * centered, axis=-1, keepdims=True)
    return centered * lax.rsqrt(variance + epsilon) * gain_scale


def doc_layout(doc_lengths, indices):
    doc_ends = jnp.cumsum(doc_lengths)
    passed = indices[:, None] >= doc_ends[None, :]
    doc_ids = jnp.sum(passed.astype(jnp.int32), axis=1)
    starts = jnp.sum(jnp.where(passed, doc_lengths[None, :], 0), axis=1)
    return (doc_ids, indices - starts)


def rope_tables(positions, rope_base):
    half_dim = HEAD_DIM // 2
    inverse = rope_base ** (-2.0 * jnp.arange(half_dim, dtype=f32) / HEAD_DIM)
    angles = positions.astype(f32)[..., None] * inverse
    angles = jnp.concatenate([angles, angles], axis=-1)
    return (jnp.cos(angles), jnp.sin(angles))


def rotate(values, cosine_table, sine_table):
    half_dim = values.shape[-1] // 2
    turned = jnp.concatenate([-values[..., half_dim:], values[..., :half_dim]], axis=-1)
    return values * cosine_table[..., None, :] + turned * sine_table[..., None, :]


def rotate_back(gradients, cosine_table, sine_table):
    half_dim = gradients.shape[-1] // 2
    scaled = gradients * sine_table[..., None, :]
    turned = jnp.concatenate([scaled[..., half_dim:], -scaled[..., :half_dim]], axis=-1)
    return gradients * cosine_table[..., None, :] + turned


def masked_scores(queries, keys_rot, allowed):
    scores = jnp.einsum(
        "qhd,khd->hqk", queries, keys_rot, preferred_element_type=f32
    ) * HEAD_DIM ** (-0.5)
    return jnp.where(allowed[None], scores, -1e30)


def contract_rows(left_rows, right_rows):
    return lax.dot_general(
        left_rows, right_rows, (((0,), (0,)), ((), ())), preferred_element_type=f32
    )


def contract_last(left_rows, weight):
    return lax.dot_general(
        left_rows, weight, (((1,), (1,)), ((), ())), preferred_element_type=f32
    )


def times(left_rows, weight):
    return jnp.dot(left_rows, weight, preferred_element_type=f32)


def forward_layer(inputs, gain_pair, weights, allowed, tables):
    w_qkv, w_out, w_up, w_down = weights
    row_count = inputs.shape[0]
    normed_all = gather_rows(layer_norm(inputs, gain_pair[0]).astype(bf16))
    full_rows = normed_all.shape[0]
    local_width = w_out.shape[0]
    projected = times(normed_all, w_qkv).reshape(full_rows, 3, -1, HEAD_DIM)
    queries = rotate(projected[:, 0], *tables).astype(bf16)
    keys_rot = rotate(projected[:, 1], *tables).astype(bf16)
    values_in = projected[:, 2].astype(bf16)
    scores = masked_scores(queries, keys_rot, allowed)
    largest = jnp.max(scores, axis=2, keepdims=True)
    exp_scores = jnp.exp(scores - largest)
    totals = jnp.sum(exp_scores, axis=2, keepdims=True)
    soft_weights = (exp_scores / totals).astype(bf16)
    log_totals = largest + jnp.log(totals)
    attended = jnp.einsum("hqk,khd->qhd", soft_weights, values_in, preferred_element_type=f32)
    attended = attended.reshape(full_rows, local_width).astype(bf16)
    resid_mid = inputs + scatter_rows(times(attended, w_out), row_count)
    normed_mid_all = gather_rows(layer_norm(resid_mid, gain_pair[1]).astype(bf16))
    hidden = times(normed_mid_all, w_up)
    local_hidden = hidden.shape[1] // 2
    gelu_in = hidden[:, :local_hidden]
    gate_mult = hidden[:, local_hidden:]
    mixed_rows = (jax.nn.gelu(gelu_in, approximate=False) * gate_mult).astype(bf16)
    result = resid_mid + scatter_rows(times(mixed_rows, w_down), row_count)
    kept = (
        inputs,
        resid_mid,
        normed_all,
        queries,
        keys_rot,
        values_in,
        log_totals,
        attended,
        normed_mid_all,
        gelu_in,
        gate_mult,
        mixed_rows,
    )
    return (result, kept)


def gelu_product(first_half, second_half):
    return jax.nn.gelu(first_half, approximate=False) * second_half


def backward_ffn(grad_result, kept, gain_pair, weights):
    w_up, w_down = weights[2], weights[3]
    resid_mid, normed_mid_all = kept[1], kept[8]
    gelu_in, gate_mult, mixed_rows = kept[9], kept[10], kept[11]
    row_count = grad_result.shape[0]
    grad_ffn_all = gather_rows(grad_result.astype(bf16))
    grad_mixed = contract_last(grad_ffn_all, w_down)
    unused, pull_gelu = jax.vjp(gelu_product, gelu_in, gate_mult)
    grad_gelu, grad_gate = pull_gelu(grad_mixed)
    grad_hidden = jnp.concatenate([grad_gelu, grad_gate], axis=1).astype(bf16)
    grad_normed_mid = scatter_rows(contract_last(grad_hidden, w_up), row_count)
    unused, pull_norm = jax.vjp(layer_norm, resid_mid, gain_pair[1])
    grad_resid, grad_gain = pull_norm(grad_normed_mid)
    grad_w_down = contract_rows(grad_ffn_all, mixed_rows).astype(bf16)
    grad_w_up = contract_rows(normed_mid_all, grad_hidden).astype(bf16)
    grad_w = jnp.concatenate([grad_w_up, grad_w_down], axis=1)
    return (grad_result + grad_resid, grad_w, grad_gain)


def backward_attn(grad_mid, kept, gain_pair, weights, allowed, tables):
    w_qkv, w_out = weights[0], weights[1]
    inputs, normed_all = kept[0], kept[2]
    queries, keys_rot, values_in, log_totals, attended = kept[3:8]
    row_count = grad_mid.shape[0]
    full_rows = normed_all.shape[0]
    grad_att_all = gather_rows(grad_mid.astype(bf16))
    grad_attended = contract_last(grad_att_all, w_out).astype(bf16).reshape(queries.shape)
    scores = masked_scores(queries, keys_rot, allowed)
    soft_exact = jnp.exp(scores - log_totals)
    soft_weights = soft_exact.astype(bf16)
    grad_values = jnp.einsum(
        "hqk,qhd->khd", soft_weights, grad_attended, preferred_element_type=f32
    )
    grad_soft = jnp.einsum("qhd,khd->hqk", grad_attended, values_in, preferred_element_type=f32)
    row_dots = jnp.sum(soft_exact * grad_soft, axis=2, keepdims=True)
    grad_scores = (soft_exact * (grad_soft - row_dots)).astype(bf16)
    grad_queries = jnp.einsum(
        "hqk,khd->qhd", grad_scores, keys_rot, preferred_element_type=f32
    ) * HEAD_DIM ** (-0.5)
    grad_keys = jnp.einsum(
        "hqk,qhd->khd", grad_scores, queries, preferred_element_type=f32
    ) * HEAD_DIM ** (-0.5)
    grad_projected = jnp.stack(
        [
            rotate_back(grad_queries, *tables),
            rotate_back(grad_keys, *tables),
            grad_values,
        ],
        axis=1,
    )
    grad_projected = grad_projected.astype(bf16).reshape(full_rows, -1)
    grad_normed = scatter_rows(contract_last(grad_projected, w_qkv), row_count)
    unused, pull_norm = jax.vjp(layer_norm, inputs, gain_pair[0])
    grad_resid, grad_gain = pull_norm(grad_normed)
    grad_w_out = contract_rows(grad_att_all, attended).astype(bf16)
    grad_w_qkv = contract_rows(normed_all, grad_projected).astype(bf16)
    grad_w = jnp.concatenate([grad_w_qkv, grad_w_out], axis=1)
    return (grad_mid + grad_resid, grad_w, grad_gain)


def other_layer(own, after, pair_x):
    core_index = lax.axis_index("core")
    parity = lax.axis_index("x") % 2
    own, unused = lax.optimization_barrier((own, after))
    rows = own.shape[0]
    if pair_x:
        piece = rows // 4
        sent = lax.dynamic_slice_in_dim(own, (core_index * 2 + parity) * piece, piece)
        got = swap_layer(sent)
        beside = lax.ppermute(got, "x", [(0, 1), (1, 0), (2, 3), (3, 2)])
        half = in_order(parity, got, beside)
    else:
        piece = rows // 2
        sent = lax.dynamic_slice_in_dim(own, core_index * piece, piece)
        got = half = swap_layer(sent)
    return in_order(core_index, half, swap_core(half)), got


def in_order(index, mine, other):
    low = jnp.where(index == 0, mine, other)
    high = jnp.where(index == 0, other, mine)
    return jnp.concatenate([low, high], axis=0)


def add_core(grads):
    core_index = lax.axis_index("core")
    half = grads.shape[0] // 2
    sent = lax.dynamic_slice_in_dim(grads, (1 - core_index) * half, half)
    held = lax.dynamic_slice_in_dim(grads, core_index * half, half)
    return (held.astype(f32) + swap_core(sent).astype(f32)).astype(bf16)


def reduce_part(grads):
    return lax.psum_scatter(add_core(grads), ("zlo", "x"), scatter_dimension=0, tiled=True)


def reduce_part_now(grads):
    pieces = lax.all_to_all(add_core(grads), ("zlo", "x"), 0, 0, tiled=True)
    pieces = pieces.reshape(8, -1, pieces.shape[1])
    return jnp.sum(pieces.astype(f32), axis=0).astype(bf16)


def spread_part(part):
    copies = jnp.broadcast_to(part[None], (8,) + part.shape).reshape(-1, part.shape[1])
    half = lax.all_to_all(copies, ("zlo", "x"), 0, 0, tiled=True)
    return in_order(lax.axis_index("core"), half, swap_core(half))


def join_sections(is_first, part_first, part_second):
    own = jnp.where(is_first, part_first, part_second)
    sent = jnp.where(is_first, part_second, part_first)
    return (own.astype(f32) + swap_section(sent).astype(f32)).astype(bf16)


def local(tokens, cotangent, lengths, gains, w_qkv, w_out, w_up, w_down):
    section_index = lax.axis_index("section")
    is_first = section_index == 0
    row_count = tokens.shape[1]
    full_rows = row_count * lax.axis_size("tensor")
    own = (
        w_qkv[0].reshape(w_qkv.shape[1], -1),
        w_out[0],
        w_up[0].reshape(w_up.shape[1], -1),
        w_down[0],
    )
    other_qkv, after = other_layer(own[0], tokens[0, 0, 0], False)
    other_out, after = other_layer(own[1], after, False)
    other_up, after = other_layer(own[2], after, True)
    other_down, after = other_layer(own[3], after, True)
    others = (other_qkv, other_out, other_up, other_down)
    gains_other = swap_layer(gains[0])
    layer0 = tuple(jnp.where(is_first, a, b) for a, b in zip(own, others))
    layer1 = tuple(jnp.where(is_first, b, a) for a, b in zip(own, others))
    gains0 = jnp.where(is_first, gains[0], gains_other)
    gains1 = jnp.where(is_first, gains_other, gains[0])
    start_rows = jnp.where(is_first, tokens[0], tokens[1])
    end_grads = jnp.where(is_first, cotangent[0], cotangent[1])
    doc_lengths = jnp.where(is_first, lengths[0, 0], lengths[1, 0])
    indices = jnp.arange(full_rows, dtype=jnp.int32)
    indices = (indices + lax.axis_index("tensor") * row_count) % full_rows
    doc_ids, positions = doc_layout(doc_lengths, indices)
    same_doc = doc_ids[:, None] == doc_ids[None, :]
    near = jnp.abs(indices[:, None] - indices[None, :]) <= WINDOW // 2
    allowed0 = same_doc & near
    allowed1 = same_doc
    tables0 = rope_tables(positions, 10000.0)
    tables1 = rope_tables(positions, 160000.0)

    out0, kept0 = forward_layer(start_rows.astype(f32), gains0, layer0, allowed0, tables0)
    out0 = out0.astype(bf16)
    out1, kept1 = forward_layer(out0.astype(f32), gains1, layer1, allowed1, tables1)
    out1 = out1.astype(bf16)
    mid1, ffn1, gain_mid1 = backward_ffn(end_grads.astype(f32), kept1, gains1, layer1)
    in1, attn1, gain_first1 = backward_attn(mid1, kept1, gains1, layer1, allowed1, tables1)
    in1 = in1.astype(bf16)
    mid0, ffn0, gain_mid0 = backward_ffn(in1.astype(f32), kept0, gains0, layer0)
    in0, attn0, gain_first0 = backward_attn(mid0, kept0, gains0, layer0, allowed0, tables0)
    in0 = in0.astype(bf16)

    both1 = reduce_part(jnp.concatenate([attn1, ffn1], axis=1))
    attn_width = attn1.shape[1]
    part_ffn0 = reduce_part(ffn0)
    ffn_sum = spread_part(join_sections(is_first, part_ffn0, both1[:, attn_width:]))
    part_attn0 = reduce_part_now(attn0)
    attn_sum = spread_part(join_sections(is_first, part_attn0, both1[:, :attn_width]))
    up_width = own[2].shape[1]
    qkv_width = own[0].shape[1]

    gain0 = jnp.stack([gain_first0, gain_mid0])
    gain1 = jnp.stack([gain_first1, gain_mid1])
    gain_own = jnp.where(is_first, gain0, gain1)
    gain_sent = jnp.where(is_first, gain1, gain0)
    gain_total = gain_own + swap_section(gain_sent)
    gain_total = sum_tensor(gain_total)
    gain_total = gain_total + swap_core(gain_total)
    gain_total = (
        gain_total
        + around(gain_total, "x", 1)
        + around(gain_total, "x", 2)
        + around(gain_total, "x", 3)
    )
    gain_total = gain_total + around(gain_total, "zlo", 1)

    got_out = swap_section(jnp.where(is_first, out1, out0))
    section_out = jnp.stack(
        [jnp.where(is_first, out0, got_out), jnp.where(is_first, got_out, out1)]
    )
    got_in = swap_section(jnp.where(is_first, in1, in0))
    input_grads = jnp.stack(
        [jnp.where(is_first, in0, got_in), jnp.where(is_first, got_in, in1)]
    )
    return (
        section_out[None],
        input_grads[None],
        gain_total[None],
        attn_sum[:, :qkv_width].astype(f32).reshape(w_qkv.shape),
        attn_sum[:, qkv_width:].T.astype(f32)[None],
        ffn_sum[:, :up_width].astype(f32).reshape(w_up.shape),
        ffn_sum[:, up_width:].T.astype(f32)[None],
    )


def solution(mesh):
    sizes = dict(zip(mesh.axis_names, mesh.devices.shape))
    fine = Mesh(
        mesh.devices.reshape(sizes["section"], 2, sizes["dp"] // 4, 2, sizes["tensor"]),
        ("section", "zlo", "x", "core", "tensor"),
    )
    rows = ("zlo", "x", "core", "tensor")
    in_specs = (
        P(None, rows, None),
        P(None, rows, None),
        P(None, DP, None),
        P("section", None, None),
        P("section", None, None, "tensor"),
        P("section", "tensor", None),
        P("section", None, None, "tensor"),
        P("section", "tensor", None),
    )
    out_specs = (
        P("section", None, rows, None),
        P("section", None, rows, None),
        P("section", None, None),
        P("section", None, None, "tensor"),
        P("section", "tensor", None),
        P("section", None, None, "tensor"),
        P("section", "tensor", None),
    )
    return jax.shard_map(local, mesh=fine, in_specs=in_specs, out_specs=out_specs, check_vma=False)
```

```python
import jax
import jax.numpy as jnp
from jax import lax
from jax.sharding import Mesh
from jax.sharding import PartitionSpec as P

HEAD_DIM = 64
WINDOW = 128

epsilon = 1e-05
bf16 = jnp.bfloat16
f32 = jnp.float32

DP = ("zlo", "x", "core")


def around(block, axis, distance):
    count = lax.axis_size(axis)
    return lax.ppermute(block, axis, [(i, (i + distance) % count) for i in range(count)])


def swap_core(block):
    return lax.ppermute(block, "core", [(0, 1), (1, 0)])


def swap_section(block):
    return lax.ppermute(block, "section", [(0, 1), (1, 0)])


def swap_layer(block):
    return lax.ppermute(block, ("section", "zlo"), [(0, 3), (1, 2), (2, 1), (3, 0)])


def gather_parts(block):
    ahead2 = around(block, "tensor", 2)
    ahead1 = around(block, "tensor", -1)
    ahead3 = around(block, "tensor", 1)
    return [block, ahead1, ahead2, ahead3]


def scatter_parts(term_of):
    sent2 = around(term_of(2).astype(bf16), "tensor", 2)
    sent1 = around(term_of(1).astype(bf16), "tensor", 1)
    sent3 = around(term_of(3).astype(bf16), "tensor", -1)
    kept = term_of(0).astype(f32)
    return kept + sent2.astype(f32) + sent1.astype(f32) + sent3.astype(f32)


def joined(parts, axis=0):
    return jnp.concatenate(parts, axis=axis)


def after_all(values, *others):
    return lax.optimization_barrier((values,) + others)[0]


def sum_tensor(block):
    return (
        block
        + around(block, "tensor", 2)
        + around(block, "tensor", 1)
        + around(block, "tensor", -1)
    )


def layer_norm(values, gain_scale):
    centered = values - jnp.mean(values, axis=-1, keepdims=True)
    variance = jnp.mean(centered * centered, axis=-1, keepdims=True)
    return centered * lax.rsqrt(variance + epsilon) * gain_scale


def doc_layout(doc_lengths, indices):
    doc_ends = jnp.cumsum(doc_lengths)
    passed = indices[:, None] >= doc_ends[None, :]
    doc_ids = jnp.sum(passed.astype(jnp.int32), axis=1)
    starts = jnp.sum(jnp.where(passed, doc_lengths[None, :], 0), axis=1)
    return (doc_ids, indices - starts)


def rope_tables(positions, rope_base):
    half_dim = HEAD_DIM // 2
    inverse = rope_base ** (-2.0 * jnp.arange(half_dim, dtype=f32) / HEAD_DIM)
    angles = positions.astype(f32)[..., None] * inverse
    angles = jnp.concatenate([angles, angles], axis=-1)
    return (jnp.cos(angles), jnp.sin(angles))


def rotate(values, cosine_table, sine_table):
    half_dim = values.shape[-1] // 2
    turned = jnp.concatenate([-values[..., half_dim:], values[..., :half_dim]], axis=-1)
    return values * cosine_table[..., None, :] + turned * sine_table[..., None, :]


def rotate_back(gradients, cosine_table, sine_table):
    half_dim = gradients.shape[-1] // 2
    scaled = gradients * sine_table[..., None, :]
    turned = jnp.concatenate([scaled[..., half_dim:], -scaled[..., :half_dim]], axis=-1)
    return gradients * cosine_table[..., None, :] + turned


def masked_scores(queries, keys_rot, allowed):
    scores = jnp.einsum(
        "qhd,khd->hqk", queries, keys_rot, preferred_element_type=f32
    ) * HEAD_DIM ** (-0.5)
    return jnp.where(allowed[None], scores, -1e30)


def contract_rows(left_rows, right_rows):
    return lax.dot_general(
        left_rows, right_rows, (((0,), (0,)), ((), ())), preferred_element_type=f32
    )


def contract_last(left_rows, weight):
    return lax.dot_general(
        left_rows, weight, (((1,), (1,)), ((), ())), preferred_element_type=f32
    )


def times(left_rows, weight):
    return jnp.dot(left_rows, weight, preferred_element_type=f32)


def gelu_product(first_half, second_half):
    return jax.nn.gelu(first_half, approximate=False) * second_half


def forward_layer(inputs, normed_parts, gain_mid, weights, allowed, tables):
    w_qkv, w_out, w_up, w_down = weights
    row_count = inputs.shape[0]
    local_width = w_out.shape[0]
    queries, keys_rot, values_in = [], [], []
    for k, part in enumerate(normed_parts):
        projected = times(part, w_qkv).reshape(row_count, 3, -1, HEAD_DIM)
        rows = slice(k * row_count, (k + 1) * row_count)
        turns = (tables[0][rows], tables[1][rows])
        queries.append(rotate(projected[:, 0], *turns).astype(bf16))
        keys_rot.append(rotate(projected[:, 1], *turns).astype(bf16))
        values_in.append(projected[:, 2].astype(bf16))
    keys_all = joined(keys_rot)
    values_all = joined(values_in)
    attended = [None] * 4
    log_totals = [None] * 4

    def attend(k):
        rows = slice(k * row_count, (k + 1) * row_count)
        scores = masked_scores(queries[k], keys_all, allowed[rows])
        largest = jnp.max(scores, axis=2, keepdims=True)
        exp_scores = jnp.exp(scores - largest)
        totals = jnp.sum(exp_scores, axis=2, keepdims=True)
        soft_weights = (exp_scores / totals).astype(bf16)
        log_totals[k] = largest + jnp.log(totals)
        mixed = jnp.einsum("hqk,khd->qhd", soft_weights, values_all, preferred_element_type=f32)
        attended[k] = mixed.reshape(row_count, local_width).astype(bf16)
        return times(attended[k], w_out)

    resid_mid = inputs + scatter_parts(attend)
    mid_parts = gather_parts(layer_norm(resid_mid, gain_mid).astype(bf16))
    gelu_in = [None] * 4
    gate_mult = [None] * 4
    mixed_rows = [None] * 4

    def feed(k):
        hidden = times(mid_parts[k], w_up)
        local_hidden = hidden.shape[1] // 2
        gelu_in[k] = hidden[:, :local_hidden]
        gate_mult[k] = hidden[:, local_hidden:]
        mixed_rows[k] = gelu_product(gelu_in[k], gate_mult[k]).astype(bf16)
        return times(mixed_rows[k], w_down)

    result = resid_mid + scatter_parts(feed)
    kept = dict(
        inputs=inputs,
        resid_mid=resid_mid,
        normed=normed_parts,
        queries=joined(queries),
        keys=keys_all,
        values=values_all,
        log_totals=joined(log_totals, 1),
        attended=attended,
        normed_mid=mid_parts,
        gelu_in=gelu_in,
        gate_mult=gate_mult,
        mixed=mixed_rows,
    )
    return (result, kept)


def backward_ffn(grad_result, kept, gain_mid, weights):
    w_up, w_down = weights[2], weights[3]
    grad_parts = gather_parts(grad_result.astype(bf16))
    grad_hidden = [None] * 4

    def feed_back(k):
        grad_mixed = contract_last(grad_parts[k], w_down)
        unused, pull_gelu = jax.vjp(gelu_product, kept["gelu_in"][k], kept["gate_mult"][k])
        grad_hidden[k] = joined(pull_gelu(grad_mixed), 1).astype(bf16)
        return contract_last(grad_hidden[k], w_up)

    grad_normed_mid = scatter_parts(feed_back)
    unused, pull_norm = jax.vjp(layer_norm, kept["resid_mid"], gain_mid)
    grad_resid, grad_gain = pull_norm(grad_normed_mid)
    grad_mid = grad_result + grad_resid

    def weight_grads(gate):
        outer, inner, left, right = after_all(
            (grad_parts, kept["mixed"], kept["normed_mid"], grad_hidden), gate
        )
        grad_down = contract_rows(joined(outer), joined(inner)).astype(bf16)
        grad_up = contract_rows(joined(left), joined(right)).astype(bf16)
        return joined([grad_up, grad_down], 1)

    return (grad_mid, weight_grads, grad_gain)


def backward_attn(grad_mid, kept, gain_first, weights, allowed, tables):
    w_qkv, w_out = weights[0], weights[1]
    queries, keys_rot, values_in = kept["queries"], kept["keys"], kept["values"]
    row_count = grad_mid.shape[0]
    grad_parts = gather_parts(grad_mid.astype(bf16))
    grad_attended = joined([contract_last(part, w_out).astype(bf16) for part in grad_parts])
    grad_attended = grad_attended.reshape(queries.shape)
    scores = masked_scores(queries, keys_rot, allowed)
    soft_exact = jnp.exp(scores - kept["log_totals"])
    soft_weights = soft_exact.astype(bf16)
    grad_values = jnp.einsum(
        "hqk,qhd->khd", soft_weights, grad_attended, preferred_element_type=f32
    )
    grad_soft = jnp.einsum("qhd,khd->hqk", grad_attended, values_in, preferred_element_type=f32)
    row_dots = jnp.sum(soft_exact * grad_soft, axis=2, keepdims=True)
    grad_scores = (soft_exact * (grad_soft - row_dots)).astype(bf16)
    grad_queries = jnp.einsum(
        "hqk,khd->qhd", grad_scores, keys_rot, preferred_element_type=f32
    ) * HEAD_DIM ** (-0.5)
    grad_keys = jnp.einsum(
        "hqk,qhd->khd", grad_scores, queries, preferred_element_type=f32
    ) * HEAD_DIM ** (-0.5)
    grad_projected = jnp.stack(
        [
            rotate_back(grad_queries, *tables),
            rotate_back(grad_keys, *tables),
            grad_values,
        ],
        axis=1,
    )
    grad_projected = grad_projected.astype(bf16).reshape(4 * row_count, -1)

    def project_back(k):
        return contract_last(grad_projected[k * row_count : (k + 1) * row_count], w_qkv)

    grad_normed = scatter_parts(project_back)
    unused, pull_norm = jax.vjp(layer_norm, kept["inputs"], gain_first)
    grad_resid, grad_gain = pull_norm(grad_normed)

    def weight_grads(gate):
        outer, inner, left, right = (grad_parts, kept["attended"], kept["normed"], grad_projected)
        if gate is not None:
            outer, inner, left, right = after_all((outer, inner, left, right), gate)
        grad_out = contract_rows(joined(outer), joined(inner)).astype(bf16)
        grad_qkv = contract_rows(joined(left), right).astype(bf16)
        return joined([grad_qkv, grad_out], 1)

    return (grad_mid + grad_resid, weight_grads, grad_gain)


def other_layer(own, after, pair_x, before_core=()):
    core_index = lax.axis_index("core")
    parity = lax.axis_index("x") % 2
    own, unused = lax.optimization_barrier((own, after))
    rows = own.shape[0]
    if pair_x:
        piece = rows // 4
        sent = lax.dynamic_slice_in_dim(own, (core_index * 2 + parity) * piece, piece)
        got = swap_layer(sent)
        beside = lax.ppermute(got, "x", [(0, 1), (1, 0), (2, 3), (3, 2)])
        half = in_order(parity, got, beside)
    else:
        piece = rows // 2
        sent = lax.dynamic_slice_in_dim(own, core_index * piece, piece)
        got = half = swap_layer(sent)
    half = after_all(half, *before_core)
    return in_order(core_index, half, swap_core(half)), got


def in_order(index, mine, other):
    low = jnp.where(index == 0, mine, other)
    high = jnp.where(index == 0, other, mine)
    return jnp.concatenate([low, high], axis=0)


def add_core(grads):
    core_index = lax.axis_index("core")
    half = grads.shape[0] // 2
    sent = lax.dynamic_slice_in_dim(grads, (1 - core_index) * half, half)
    held = lax.dynamic_slice_in_dim(grads, core_index * half, half)
    return (held.astype(f32) + swap_core(sent).astype(f32)).astype(bf16)


def reduce_part(grads):
    return lax.psum_scatter(add_core(grads), ("zlo", "x"), scatter_dimension=0, tiled=True)


def reduce_part_now(grads):
    pieces = lax.all_to_all(add_core(grads), ("zlo", "x"), 0, 0, tiled=True)
    pieces = pieces.reshape(8, -1, pieces.shape[1])
    return jnp.sum(pieces.astype(f32), axis=0).astype(bf16)


def spread_part(part):
    copies = jnp.broadcast_to(part[None], (8,) + part.shape).reshape(-1, part.shape[1])
    half = lax.all_to_all(copies, ("zlo", "x"), 0, 0, tiled=True)
    return in_order(lax.axis_index("core"), half, swap_core(half))


def join_sections(is_first, part_first, part_second):
    own = jnp.where(is_first, part_first, part_second)
    sent = jnp.where(is_first, part_second, part_first)
    return (own.astype(f32) + swap_section(sent).astype(f32)).astype(bf16)


def local(tokens, cotangent, lengths, gains, w_qkv, w_out, w_up, w_down):
    section_index = lax.axis_index("section")
    is_first = section_index == 0
    row_count = tokens.shape[1]
    full_rows = row_count * lax.axis_size("tensor")
    start_rows = jnp.where(is_first, tokens[0], tokens[1]).astype(f32)
    end_grads = jnp.where(is_first, cotangent[0], cotangent[1])
    gains_other = swap_layer(gains[0])
    gains0 = jnp.where(is_first, gains[0], gains_other)
    gains1 = jnp.where(is_first, gains_other, gains[0])
    first_parts = gather_parts(layer_norm(start_rows, gains0[0]).astype(bf16))
    own = (
        w_qkv[0].reshape(w_qkv.shape[1], -1),
        w_out[0],
        w_up[0].reshape(w_up.shape[1], -1),
        w_down[0],
    )
    other_qkv, after = other_layer(own[0], tokens[0, 0, 0], False, first_parts)
    other_out, after = other_layer(own[1], after, False)
    other_up, after = other_layer(own[2], after, True)
    other_down, after = other_layer(own[3], after, True)
    others = (other_qkv, other_out, other_up, other_down)
    layer0 = tuple(jnp.where(is_first, a, b) for a, b in zip(own, others))
    layer1 = tuple(jnp.where(is_first, b, a) for a, b in zip(own, others))
    doc_lengths = jnp.where(is_first, lengths[0, 0], lengths[1, 0])
    indices = jnp.arange(full_rows, dtype=jnp.int32)
    indices = (indices + lax.axis_index("tensor") * row_count) % full_rows
    doc_ids, positions = doc_layout(doc_lengths, indices)
    same_doc = doc_ids[:, None] == doc_ids[None, :]
    near = jnp.abs(indices[:, None] - indices[None, :]) <= WINDOW // 2
    allowed0 = same_doc & near
    allowed1 = same_doc
    tables0 = rope_tables(positions, 10000.0)
    tables1 = rope_tables(positions, 160000.0)

    out0, kept0 = forward_layer(
        start_rows, first_parts, gains0[1], layer0, allowed0, tables0
    )
    out0 = out0.astype(bf16)
    second_rows = out0.astype(f32)
    second_parts = gather_parts(layer_norm(second_rows, gains1[0]).astype(bf16))
    out1, kept1 = forward_layer(
        second_rows, second_parts, gains1[1], layer1, allowed1, tables1
    )
    out1 = out1.astype(bf16)
    mid1, ffn_grads1, gain_mid1 = backward_ffn(end_grads.astype(f32), kept1, gains1[1], layer1)
    ffn1 = reduce_part(ffn_grads1(mid1))
    in1, attn_grads1, gain_first1 = backward_attn(
        mid1, kept1, gains1[0], layer1, allowed1, tables1
    )
    in1 = in1.astype(bf16)
    attn1 = reduce_part(attn_grads1(in1))
    mid0, ffn_grads0, gain_mid0 = backward_ffn(in1.astype(f32), kept0, gains0[1], layer0)
    ffn0 = reduce_part_now(ffn_grads0(mid0))
    ffn_sum = spread_part(join_sections(is_first, ffn0, ffn1))
    in0, attn_grads0, gain_first0 = backward_attn(
        mid0, kept0, gains0[0], layer0, allowed0, tables0
    )
    in0 = in0.astype(bf16)
    attn0 = reduce_part_now(attn_grads0(None))
    attn_sum = spread_part(join_sections(is_first, attn0, attn1))
    up_width = own[2].shape[1]
    qkv_width = own[0].shape[1]

    gain0 = jnp.stack([gain_first0, gain_mid0])
    gain1 = jnp.stack([gain_first1, gain_mid1])
    gain_own = jnp.where(is_first, gain0, gain1)
    gain_sent = jnp.where(is_first, gain1, gain0)
    gain_total = gain_own + swap_section(gain_sent)
    gain_total = sum_tensor(gain_total)
    gain_total = gain_total + swap_core(gain_total)
    gain_total = (
        gain_total
        + around(gain_total, "x", 1)
        + around(gain_total, "x", 2)
        + around(gain_total, "x", 3)
    )
    gain_total = gain_total + around(gain_total, "zlo", 1)

    got_out = swap_section(jnp.where(is_first, out1, out0))
    section_out = jnp.stack(
        [jnp.where(is_first, out0, got_out), jnp.where(is_first, got_out, out1)]
    )
    got_in = swap_section(jnp.where(is_first, in1, in0))
    input_grads = jnp.stack(
        [jnp.where(is_first, in0, got_in), jnp.where(is_first, got_in, in1)]
    )
    return (
        section_out[None],
        input_grads[None],
        gain_total[None],
        attn_sum[:, :qkv_width].astype(f32).reshape(w_qkv.shape),
        attn_sum[:, qkv_width:].T.astype(f32)[None],
        ffn_sum[:, :up_width].astype(f32).reshape(w_up.shape),
        ffn_sum[:, up_width:].T.astype(f32)[None],
    )


def solution(mesh):
    sizes = dict(zip(mesh.axis_names, mesh.devices.shape))
    fine = Mesh(
        mesh.devices.reshape(sizes["section"], 2, sizes["dp"] // 4, 2, sizes["tensor"]),
        ("section", "zlo", "x", "core", "tensor"),
    )
    rows = ("zlo", "x", "core", "tensor")
    in_specs = (
        P(None, rows, None),
        P(None, rows, None),
        P(None, DP, None),
        P("section", None, None),
        P("section", None, None, "tensor"),
        P("section", "tensor", None),
        P("section", None, None, "tensor"),
        P("section", "tensor", None),
    )
    out_specs = (
        P("section", None, rows, None),
        P("section", None, rows, None),
        P("section", None, None),
        P("section", None, None, "tensor"),
        P("section", "tensor", None),
        P("section", None, None, "tensor"),
        P("section", "tensor", None),
    )
    return jax.shard_map(local, mesh=fine, in_specs=in_specs, out_specs=out_specs, check_vma=False)
```

```python
import jax
import jax.numpy as jnp
from jax import lax
from jax.sharding import Mesh
from jax.sharding import PartitionSpec as P

HEAD_DIM = 64
WINDOW = 128

epsilon = 1e-05
bf16 = jnp.bfloat16
f32 = jnp.float32

DP = ("zlo", "x", "core")


def around(block, axis, distance):
    count = lax.axis_size(axis)
    return lax.ppermute(block, axis, [(i, (i + distance) % count) for i in range(count)])


def swap_core(block):
    return lax.ppermute(block, "core", [(0, 1), (1, 0)])


def swap_section(block):
    return lax.ppermute(block, "section", [(0, 1), (1, 0)])


def swap_layer(block):
    return lax.ppermute(block, ("section", "zlo"), [(0, 3), (1, 2), (2, 1), (3, 0)])


def gather_parts(block):
    ahead2 = around(block, "tensor", 2)
    ahead1 = around(block, "tensor", -1)
    ahead3 = around(block, "tensor", 1)
    return [block, ahead1, ahead2, ahead3]


def scatter_parts(term_of):
    sent2 = around(term_of(2).astype(bf16), "tensor", 2)
    sent1 = around(term_of(1).astype(bf16), "tensor", 1)
    sent3 = around(term_of(3).astype(bf16), "tensor", -1)
    kept = term_of(0).astype(f32)
    return kept + sent2.astype(f32) + sent1.astype(f32) + sent3.astype(f32)


def joined(parts, axis=0):
    return jnp.concatenate(parts, axis=axis)


def after_all(values, *others):
    return lax.optimization_barrier((values,) + others)[0]


def sum_tensor(block):
    return (
        block
        + around(block, "tensor", 2)
        + around(block, "tensor", 1)
        + around(block, "tensor", -1)
    )


def layer_norm(values, gain_scale):
    centered = values - jnp.mean(values, axis=-1, keepdims=True)
    variance = jnp.mean(centered * centered, axis=-1, keepdims=True)
    return centered * lax.rsqrt(variance + epsilon) * gain_scale


def doc_layout(doc_lengths, indices):
    doc_ends = jnp.cumsum(doc_lengths)
    passed = indices[:, None] >= doc_ends[None, :]
    doc_ids = jnp.sum(passed.astype(jnp.int32), axis=1)
    starts = jnp.sum(jnp.where(passed, doc_lengths[None, :], 0), axis=1)
    return (doc_ids, indices - starts)


def rope_tables(positions, rope_base):
    half_dim = HEAD_DIM // 2
    inverse = rope_base ** (-2.0 * jnp.arange(half_dim, dtype=f32) / HEAD_DIM)
    angles = positions.astype(f32)[..., None] * inverse
    angles = jnp.concatenate([angles, angles], axis=-1)
    return (jnp.cos(angles), jnp.sin(angles))


def rotate(values, cosine_table, sine_table):
    half_dim = values.shape[-1] // 2
    turned = jnp.concatenate([-values[..., half_dim:], values[..., :half_dim]], axis=-1)
    return values * cosine_table[..., None, :] + turned * sine_table[..., None, :]


def rotate_back(gradients, cosine_table, sine_table):
    half_dim = gradients.shape[-1] // 2
    scaled = gradients * sine_table[..., None, :]
    turned = jnp.concatenate([scaled[..., half_dim:], -scaled[..., :half_dim]], axis=-1)
    return gradients * cosine_table[..., None, :] + turned


def masked_scores(queries, keys_rot, allowed):
    scores = jnp.einsum(
        "qhd,khd->hqk", queries, keys_rot, preferred_element_type=f32
    ) * HEAD_DIM ** (-0.5)
    return jnp.where(allowed[None], scores, -1e30)


def contract_rows(left_rows, right_rows):
    return lax.dot_general(
        left_rows, right_rows, (((0,), (0,)), ((), ())), preferred_element_type=f32
    )


def contract_last(left_rows, weight):
    return lax.dot_general(
        left_rows, weight, (((1,), (1,)), ((), ())), preferred_element_type=f32
    )


def times(left_rows, weight):
    return jnp.dot(left_rows, weight, preferred_element_type=f32)


def gelu_product(first_half, second_half):
    return jax.nn.gelu(first_half, approximate=False) * second_half


def forward_layer(inputs, normed_parts, gain_mid, weights, allowed, tables):
    w_qkv, w_out, w_up, w_down = weights
    row_count = inputs.shape[0]
    local_width = w_out.shape[0]
    queries, keys_rot, values_in = [], [], []
    for k, part in enumerate(normed_parts):
        projected = times(part, w_qkv).reshape(row_count, 3, -1, HEAD_DIM)
        rows = slice(k * row_count, (k + 1) * row_count)
        turns = (tables[0][rows], tables[1][rows])
        queries.append(rotate(projected[:, 0], *turns).astype(bf16))
        keys_rot.append(rotate(projected[:, 1], *turns).astype(bf16))
        values_in.append(projected[:, 2].astype(bf16))
    keys_all = joined(keys_rot)
    values_all = joined(values_in)
    attended = [None] * 4
    log_totals = [None] * 4

    def attend(k):
        rows = slice(k * row_count, (k + 1) * row_count)
        scores = masked_scores(queries[k], keys_all, allowed[rows])
        largest = jnp.max(scores, axis=2, keepdims=True)
        exp_scores = jnp.exp(scores - largest)
        totals = jnp.sum(exp_scores, axis=2, keepdims=True)
        soft_weights = (exp_scores / totals).astype(bf16)
        log_totals[k] = largest + jnp.log(totals)
        mixed = jnp.einsum("hqk,khd->qhd", soft_weights, values_all, preferred_element_type=f32)
        attended[k] = mixed.reshape(row_count, local_width).astype(bf16)
        return times(attended[k], w_out)

    resid_mid = inputs + scatter_parts(attend)
    mid_parts = gather_parts(layer_norm(resid_mid, gain_mid).astype(bf16))
    gelu_in = [None] * 4
    gate_mult = [None] * 4
    mixed_rows = [None] * 4

    def feed(k):
        hidden = contract_last(mid_parts[k], w_up)
        local_hidden = hidden.shape[1] // 2
        gelu_in[k] = hidden[:, :local_hidden]
        gate_mult[k] = hidden[:, local_hidden:]
        mixed_rows[k] = gelu_product(gelu_in[k], gate_mult[k]).astype(bf16)
        return times(mixed_rows[k], w_down)

    result = resid_mid + scatter_parts(feed)
    kept = dict(
        inputs=inputs,
        resid_mid=resid_mid,
        normed=normed_parts,
        queries=joined(queries),
        keys=keys_all,
        values=values_all,
        log_totals=joined(log_totals, 1),
        attended=attended,
        normed_mid=mid_parts,
        gelu_in=gelu_in,
        gate_mult=gate_mult,
        mixed=mixed_rows,
    )
    return (result, kept)


def backward_ffn(grad_result, kept, gain_mid, weights, before):
    w_up, w_down = weights[2], weights[3]
    grad_parts = gather_parts(grad_result.astype(bf16))
    grad_hidden = [None] * 4

    def feed_back(k):
        grad_mixed = contract_last(grad_parts[k], w_down)
        unused, pull_gelu = jax.vjp(gelu_product, kept["gelu_in"][k], kept["gate_mult"][k])
        grad_hidden[k] = tuple(term.astype(bf16) for term in pull_gelu(grad_mixed))
        return times(joined(grad_hidden[k], 1), w_up)

    grad_normed_mid = after_all(scatter_parts(feed_back), *before)
    unused, pull_norm = jax.vjp(layer_norm, kept["resid_mid"], gain_mid)
    grad_resid, grad_gain = pull_norm(grad_normed_mid)
    grad_mid = grad_result + grad_resid

    def weight_grads(gate):
        outer, inner, left, right = after_all(
            (grad_parts, kept["mixed"], kept["normed_mid"], grad_hidden), gate
        )
        outer, inner, left = joined(outer), joined(inner), joined(left)
        first = joined([term[0] for term in right])
        second = joined([term[1] for term in right])
        half = inner.shape[1] // 2
        front, back = inner[:, :half], inner[:, half:]
        up = add_core(lambda core: contract_rows(core(first, second), left))
        down = add_core(lambda core: contract_rows(core(front, back), outer))
        rows = up.shape[0] + down.shape[0]
        blank = jnp.zeros((-rows % 128, up.shape[1]), bf16)
        return joined([up, down, blank])

    return (grad_mid, weight_grads, grad_gain)


def backward_attn(grad_mid, kept, gain_first, weights, allowed, tables, before, before_end):
    w_qkv, w_out = weights[0], weights[1]
    queries, keys_rot, values_in = kept["queries"], kept["keys"], kept["values"]
    row_count = grad_mid.shape[0]
    grad_parts = after_all(gather_parts(grad_mid.astype(bf16)), *before)
    grad_attended = joined([contract_last(part, w_out).astype(bf16) for part in grad_parts])
    grad_attended = grad_attended.reshape(queries.shape)
    scores = masked_scores(queries, keys_rot, allowed)
    soft_exact = jnp.exp(scores - kept["log_totals"])
    soft_weights = soft_exact.astype(bf16)
    grad_values = jnp.einsum(
        "hqk,qhd->khd", soft_weights, grad_attended, preferred_element_type=f32
    )
    grad_soft = jnp.einsum("qhd,khd->hqk", grad_attended, values_in, preferred_element_type=f32)
    row_dots = jnp.sum(soft_exact * grad_soft, axis=2, keepdims=True)
    grad_scores = (soft_exact * (grad_soft - row_dots)).astype(bf16)
    grad_queries = jnp.einsum(
        "hqk,khd->qhd", grad_scores, keys_rot, preferred_element_type=f32
    ) * HEAD_DIM ** (-0.5)
    grad_keys = jnp.einsum(
        "hqk,qhd->khd", grad_scores, queries, preferred_element_type=f32
    ) * HEAD_DIM ** (-0.5)
    grad_projected = jnp.stack(
        [
            rotate_back(grad_queries, *tables),
            rotate_back(grad_keys, *tables),
            grad_values,
        ],
        axis=1,
    )
    grad_projected = grad_projected.astype(bf16).reshape(4 * row_count, -1)

    def project_back(k):
        return contract_last(grad_projected[k * row_count : (k + 1) * row_count], w_qkv)

    grad_normed = after_all(scatter_parts(project_back), *before_end)
    unused, pull_norm = jax.vjp(layer_norm, kept["inputs"], gain_first)
    grad_resid, grad_gain = pull_norm(grad_normed)

    def weight_grads(gate):
        outer, inner, left, right = (grad_parts, kept["attended"], kept["normed"], grad_projected)
        if gate is not None:
            outer, inner, left, right = after_all((outer, inner, left, right), gate)
        outer, inner, left = joined(outer), joined(inner), joined(left)
        width = inner.shape[1]
        of_q, of_k, of_v = (right[:, i * width : (i + 1) * width] for i in range(3))
        one = add_core(lambda core: contract_rows(left, core(of_q, of_v)))
        two = add_core(lambda core: contract_rows(core(left, outer), core(of_k, inner)))
        return joined([one, two])

    return (grad_mid + grad_resid, weight_grads, grad_gain)


def other_layer(own, after, pair_x, before_core=()):
    core_index = lax.axis_index("core")
    parity = lax.axis_index("x") % 2
    own, unused = lax.optimization_barrier((own, after))
    rows = own.shape[0]
    if pair_x:
        piece = rows // 4
        sent = lax.dynamic_slice_in_dim(own, (core_index * 2 + parity) * piece, piece)
        got = swap_layer(sent)
        beside = lax.ppermute(got, "x", [(0, 1), (1, 0), (2, 3), (3, 2)])
        half = in_order(parity, got, beside)
    else:
        piece = rows // 2
        sent = lax.dynamic_slice_in_dim(own, core_index * piece, piece)
        got = half = swap_layer(sent)
    half = after_all(half, *before_core)
    return in_order(core_index, half, swap_core(half)), got


def in_order(index, mine, other):
    low = jnp.where(index == 0, mine, other)
    high = jnp.where(index == 0, other, mine)
    return jnp.concatenate([low, high], axis=0)


def add_core(product):
    is_core0 = lax.axis_index("core") == 0
    sent = product(lambda one, two: jnp.where(is_core0, two, one)).astype(bf16)
    held = product(lambda one, two: jnp.where(is_core0, one, two))
    return (held + swap_core(sent).astype(f32)).astype(bf16)


def reduce_part(grads):
    pieces = lax.all_to_all(grads, ("zlo", "x"), 0, 0, tiled=True)
    pieces = pieces.reshape(8, -1, pieces.shape[1])
    return jnp.sum(pieces.astype(f32), axis=0).astype(bf16)


def spread_part(part):
    copies = jnp.broadcast_to(part[None], (8,) + part.shape).reshape(-1, part.shape[1])
    half = lax.all_to_all(copies, ("zlo", "x"), 0, 0, tiled=True)
    beside = swap_core(half)
    is_core0 = lax.axis_index("core") == 0
    return jnp.where(is_core0, half, beside), jnp.where(is_core0, beside, half)


def join_sections(is_first, part_first, part_second):
    own = jnp.where(is_first, part_first, part_second)
    sent = jnp.where(is_first, part_second, part_first)
    return (own.astype(f32) + swap_section(sent).astype(f32)).astype(bf16)


def local(tokens, cotangent, lengths, gains, w_qkv, w_out, w_up, w_down):
    section_index = lax.axis_index("section")
    is_first = section_index == 0
    row_count = tokens.shape[1]
    full_rows = row_count * lax.axis_size("tensor")
    start_rows = jnp.where(is_first, tokens[0], tokens[1])
    end_grads = jnp.where(is_first, cotangent[0], cotangent[1])
    start_parts = gather_parts(start_rows)
    gains_other = swap_layer(gains[0])
    gains0 = jnp.where(is_first, gains[0], gains_other)
    gains1 = jnp.where(is_first, gains_other, gains[0])
    first_parts = [layer_norm(part.astype(f32), gains0[0]).astype(bf16) for part in start_parts]
    start_rows = start_rows.astype(f32)
    own = (
        jnp.transpose(w_qkv[0], (1, 0, 2)).reshape(-1, w_qkv.shape[3]),
        w_out[0],
        jnp.transpose(w_up[0], (1, 2, 0)).reshape(-1, w_up.shape[1]),
        w_down[0],
    )
    other_qkv, after = other_layer(own[0], tokens[0, 0, 0], False, start_parts)
    other_out, after = other_layer(own[1], after, False)
    other_up, after = other_layer(own[2], after, True)
    other_down, after = other_layer(own[3], after, False)
    others = (other_qkv, other_out, other_up, other_down)
    layer0 = [jnp.where(is_first, a, b) for a, b in zip(own, others)]
    layer1 = [jnp.where(is_first, b, a) for a, b in zip(own, others)]
    layer0[0] = joined(jnp.split(layer0[0], 3), 1)
    layer1[0] = joined(jnp.split(layer1[0], 3), 1)
    doc_lengths = jnp.where(is_first, lengths[0, 0], lengths[1, 0])
    indices = jnp.arange(full_rows, dtype=jnp.int32)
    indices = (indices + lax.axis_index("tensor") * row_count) % full_rows
    doc_ids, positions = doc_layout(doc_lengths, indices)
    same_doc = doc_ids[:, None] == doc_ids[None, :]
    near = jnp.abs(indices[:, None] - indices[None, :]) <= WINDOW // 2
    allowed0 = same_doc & near
    allowed1 = same_doc
    tables0 = rope_tables(positions, 10000.0)
    tables1 = rope_tables(positions, 160000.0)

    out0, kept0 = forward_layer(
        start_rows, first_parts, gains0[1], layer0, allowed0, tables0
    )
    out0 = out0.astype(bf16)
    second_rows = out0.astype(f32)
    second_parts = gather_parts(layer_norm(second_rows, gains1[0]).astype(bf16))
    out1, kept1 = forward_layer(
        second_rows, second_parts, gains1[1], layer1, allowed1, tables1
    )
    out1 = out1.astype(bf16)
    mid1, ffn_grads1, gain_mid1 = backward_ffn(
        end_grads.astype(f32), kept1, gains1[1], layer1, ()
    )
    ffn1 = reduce_part(ffn_grads1(mid1))
    in1, attn_grads1, gain_first1 = backward_attn(
        mid1, kept1, gains1[0], layer1, allowed1, tables1, (), ()
    )
    in1 = in1.astype(bf16)
    attn1 = reduce_part(attn_grads1(in1))
    mid0, ffn_grads0, gain_mid0 = backward_ffn(
        in1.astype(f32), kept0, gains0[1], layer0, (ffn1,)
    )
    ffn0 = reduce_part(ffn_grads0(mid0))
    in0, attn_grads0, gain_first0 = backward_attn(
        mid0, kept0, gains0[0], layer0, allowed0, tables0, (attn1,), (ffn0,)
    )
    in0 = in0.astype(bf16)
    attn0 = reduce_part(attn_grads0(None))
    ffn_halves = spread_part(join_sections(is_first, ffn0, ffn1))
    attn_halves = spread_part(join_sections(is_first, attn0, attn1))
    hidden_width = w_up.shape[3]
    grad_up = jnp.stack([half[:hidden_width] for half in ffn_halves])
    down_rows = w_down.shape[1] // 2
    grad_down = joined([half[hidden_width : hidden_width + down_rows] for half in ffn_halves])
    model_width = w_qkv.shape[1]
    grad_qkv = jnp.stack(
        [
            attn_halves[0][:model_width],
            attn_halves[0][model_width:],
            attn_halves[1][:model_width],
        ]
    )
    grad_out = attn_halves[1][model_width:].T

    gain0 = jnp.stack([gain_first0, gain_mid0])
    gain1 = jnp.stack([gain_first1, gain_mid1])
    gain_own = jnp.where(is_first, gain0, gain1)
    gain_sent = jnp.where(is_first, gain1, gain0)
    gain_total = gain_own + swap_section(gain_sent)
    gain_total = sum_tensor(gain_total)
    gain_total = gain_total + swap_core(gain_total)
    gain_total = (
        gain_total
        + around(gain_total, "x", 1)
        + around(gain_total, "x", 2)
        + around(gain_total, "x", 3)
    )
    gain_total = gain_total + around(gain_total, "zlo", 1)

    got_out = swap_section(jnp.where(is_first, out1, out0))
    section_out = jnp.stack(
        [jnp.where(is_first, out0, got_out), jnp.where(is_first, got_out, out1)]
    )
    got_in = swap_section(jnp.where(is_first, in1, in0))
    input_grads = jnp.stack(
        [jnp.where(is_first, in0, got_in), jnp.where(is_first, got_in, in1)]
    )
    return (
        section_out[None],
        input_grads[None],
        gain_total[None],
        jnp.transpose(grad_qkv.astype(f32), (1, 0, 2))[None],
        grad_out.astype(f32)[None],
        jnp.transpose(grad_up.astype(f32), (2, 0, 1))[None],
        grad_down.astype(f32)[None],
    )


def solution(mesh):
    sizes = dict(zip(mesh.axis_names, mesh.devices.shape))
    fine = Mesh(
        mesh.devices.reshape(sizes["section"], 2, sizes["dp"] // 4, 2, sizes["tensor"]),
        ("section", "zlo", "x", "core", "tensor"),
    )
    rows = ("zlo", "x", "core", "tensor")
    in_specs = (
        P(None, rows, None),
        P(None, rows, None),
        P(None, DP, None),
        P("section", None, None),
        P("section", None, None, "tensor"),
        P("section", "tensor", None),
        P("section", None, None, "tensor"),
        P("section", "tensor", None),
    )
    out_specs = (
        P("section", None, rows, None),
        P("section", None, rows, None),
        P("section", None, None),
        P("section", None, None, "tensor"),
        P("section", "tensor", None),
        P("section", None, None, "tensor"),
        P("section", "tensor", None),
    )
    return jax.shard_map(local, mesh=fine, in_specs=in_specs, out_specs=out_specs, check_vma=False)
```

```python
import jax
import jax.numpy as jnp
from jax import lax
from jax.sharding import Mesh
from jax.sharding import PartitionSpec as P

HEAD_DIM = 64
WINDOW = 128

epsilon = 1e-05
bf16 = jnp.bfloat16
f32 = jnp.float32

DP = ("zlo", "x", "core")


def around(block, axis, distance):
    count = lax.axis_size(axis)
    return lax.ppermute(block, axis, [(i, (i + distance) % count) for i in range(count)])


def swap_core(block):
    return lax.ppermute(block, "core", [(0, 1), (1, 0)])


def swap_section(block):
    return lax.ppermute(block, "section", [(0, 1), (1, 0)])


def swap_layer(block):
    return lax.ppermute(block, ("section", "zlo"), [(0, 3), (1, 2), (2, 1), (3, 0)])


def gather_parts(block):
    ahead2 = around(block, "tensor", 2)
    ahead1 = around(block, "tensor", -1)
    ahead3 = around(block, "tensor", 1)
    return [block, ahead1, ahead2, ahead3]


def scatter_parts(term_of, beside=None):
    sent2 = around(term_of(2).astype(bf16), "tensor", 2)
    sent1 = around(term_of(1).astype(bf16), "tensor", 1)
    sent3 = around(term_of(3).astype(bf16), "tensor", -1)
    kept = term_of(0).astype(f32)
    if beside is not None:
        kept = after_all(kept, beside(kept))
    return kept + sent2.astype(f32) + sent1.astype(f32) + sent3.astype(f32)


def joined(parts, axis=0):
    return jnp.concatenate(parts, axis=axis)


def after_all(values, *others):
    return lax.optimization_barrier((values,) + others)[0]


def sum_tensor(block):
    return (
        block
        + around(block, "tensor", 2)
        + around(block, "tensor", 1)
        + around(block, "tensor", -1)
    )


def layer_norm(values, gain_scale):
    centered = values - jnp.mean(values, axis=-1, keepdims=True)
    variance = jnp.mean(centered * centered, axis=-1, keepdims=True)
    return centered * lax.rsqrt(variance + epsilon) * gain_scale


def doc_layout(doc_lengths, indices):
    doc_ends = jnp.cumsum(doc_lengths)
    passed = indices[:, None] >= doc_ends[None, :]
    doc_ids = jnp.sum(passed.astype(jnp.int32), axis=1)
    starts = jnp.sum(jnp.where(passed, doc_lengths[None, :], 0), axis=1)
    return (doc_ids, indices - starts)


def rope_tables(positions, rope_base):
    half_dim = HEAD_DIM // 2
    inverse = rope_base ** (-2.0 * jnp.arange(half_dim, dtype=f32) / HEAD_DIM)
    angles = positions.astype(f32)[..., None] * inverse
    angles = jnp.concatenate([angles, angles], axis=-1)
    return (jnp.cos(angles), jnp.sin(angles))


def rotate(values, cosine_table, sine_table):
    half_dim = values.shape[-1] // 2
    turned = jnp.concatenate([-values[..., half_dim:], values[..., :half_dim]], axis=-1)
    return values * cosine_table[..., None, :] + turned * sine_table[..., None, :]


def rotate_back(gradients, cosine_table, sine_table):
    half_dim = gradients.shape[-1] // 2
    scaled = gradients * sine_table[..., None, :]
    turned = jnp.concatenate([scaled[..., half_dim:], -scaled[..., :half_dim]], axis=-1)
    return gradients * cosine_table[..., None, :] + turned


def masked_scores(queries, keys_rot, allowed):
    scores = jnp.einsum(
        "qhd,khd->hqk", queries, keys_rot, preferred_element_type=f32
    ) * HEAD_DIM ** (-0.5)
    return jnp.where(allowed[None], scores, -1e30)


def contract_rows(left_rows, right_rows):
    return lax.dot_general(
        left_rows, right_rows, (((0,), (0,)), ((), ())), preferred_element_type=f32
    )


def contract_last(left_rows, weight):
    return lax.dot_general(
        left_rows, weight, (((1,), (1,)), ((), ())), preferred_element_type=f32
    )


def times(left_rows, weight):
    return jnp.dot(left_rows, weight, preferred_element_type=f32)


def gelu_product(first_half, second_half):
    return jax.nn.gelu(first_half, approximate=False) * second_half


def forward_layer(inputs, normed_parts, gain_mid, weights, allowed, tables, late, points):
    w_qkv, w_out = weights[0], weights[1]
    row_count = inputs.shape[0]
    local_width = w_out.shape[0]
    queries, keys_rot, values_in = [], [], []
    for k, part in enumerate(normed_parts):
        projected = times(part, w_qkv).reshape(row_count, 3, -1, HEAD_DIM)
        rows = slice(k * row_count, (k + 1) * row_count)
        turns = (tables[0][rows], tables[1][rows])
        queries.append(rotate(projected[:, 0], *turns).astype(bf16))
        keys_rot.append(rotate(projected[:, 1], *turns).astype(bf16))
        values_in.append(projected[:, 2].astype(bf16))
    keys_all = joined(keys_rot)
    values_all = joined(values_in)
    attended = [None] * 4
    log_totals = [None] * 4

    def attend(k):
        rows = slice(k * row_count, (k + 1) * row_count)
        scores = masked_scores(queries[k], keys_all, allowed[rows])
        largest = jnp.max(scores, axis=2, keepdims=True)
        exp_scores = jnp.exp(scores - largest)
        totals = jnp.sum(exp_scores, axis=2, keepdims=True)
        soft_weights = (exp_scores / totals).astype(bf16)
        log_totals[k] = largest + jnp.log(totals)
        mixed = jnp.einsum("hqk,khd->qhd", soft_weights, values_all, preferred_element_type=f32)
        attended[k] = mixed.reshape(row_count, local_width).astype(bf16)
        return times(attended[k], w_out)

    resid_mid = inputs + scatter_parts(attend)
    points(attended[0], resid_mid)
    w_up, w_down = weights[2], weights[3]
    mid_parts = gather_parts(layer_norm(resid_mid, gain_mid).astype(bf16))
    gelu_in = [None] * 4
    gate_mult = [None] * 4
    mixed_rows = [None] * 4

    def feed(k):
        hidden = contract_last(mid_parts[k], w_up)
        local_hidden = hidden.shape[1] // 2
        gelu_in[k] = hidden[:, :local_hidden]
        gate_mult[k] = hidden[:, local_hidden:]
        mixed_rows[k] = gelu_product(gelu_in[k], gate_mult[k]).astype(bf16)
        return times(mixed_rows[k], w_down)

    if late:
        for k in range(4):
            feed(k)

        def result(gate):
            held = after_all(mixed_rows, gate)
            return resid_mid + scatter_parts(lambda k: times(held[k], w_down))

    else:
        result = resid_mid + scatter_parts(feed)
    kept = dict(
        inputs=inputs,
        resid_mid=resid_mid,
        normed=normed_parts,
        queries=joined(queries),
        keys=keys_all,
        values=values_all,
        log_totals=joined(log_totals, 1),
        attended=attended,
        normed_mid=mid_parts,
        gelu_in=gelu_in,
        gate_mult=gate_mult,
        mixed=mixed_rows,
    )
    return (result, kept)


def backward_ffn(grad_result, kept, gain_mid, weights, gather_gate):
    w_up, w_down = weights[2], weights[3]
    grad_parts = gather_parts(grad_result.astype(bf16))
    if gather_gate is not None:
        grad_parts = after_all(grad_parts, gather_gate)
    grad_hidden = [None] * 4
    finish = []

    def feed_back(k):
        grad_mixed = contract_last(grad_parts[k], w_down)
        unused, pull_gelu = jax.vjp(gelu_product, kept["gelu_in"][k], kept["gate_mult"][k])
        grad_hidden[k] = tuple(term.astype(bf16) for term in pull_gelu(grad_mixed))
        return times(joined(grad_hidden[k], 1), w_up)

    def weight_grads(gate):
        outer, inner, left, right = after_all(
            (grad_parts, kept["mixed"], kept["normed_mid"], grad_hidden), gate
        )
        outer, inner, left = joined(outer), joined(inner), joined(left)
        first = joined([term[0] for term in right])
        second = joined([term[1] for term in right])
        half = inner.shape[1] // 2
        front, back = inner[:, :half], inner[:, half:]
        sent_up, add_up = add_core(lambda core: contract_rows(core(first, second), left))
        sent_down, add_down = add_core(lambda core: contract_rows(core(front, back), outer))

        def add(gate):
            up, down = add_up(gate), add_down(gate)
            rows = up.shape[0] + down.shape[0]
            blank = jnp.zeros((-rows % 128, up.shape[1]), bf16)
            return joined([up, down, blank])

        finish.append(add)
        return (sent_up, sent_down)

    grad_normed_mid = scatter_parts(feed_back, weight_grads)
    unused, pull_norm = jax.vjp(layer_norm, kept["resid_mid"], gain_mid)
    grad_resid, grad_gain = pull_norm(grad_normed_mid)
    grad_mid = grad_result + grad_resid
    return (grad_mid, finish[0], grad_gain)


def backward_attn(grad_mid, kept, gain_first, weights, allowed, tables, gather_gate, last):
    w_qkv, w_out = weights[0], weights[1]
    queries, keys_rot, values_in = kept["queries"], kept["keys"], kept["values"]
    row_count = grad_mid.shape[0]
    grad_parts = after_all(gather_parts(grad_mid.astype(bf16)), gather_gate)
    finish = []
    grad_attended = joined([contract_last(part, w_out).astype(bf16) for part in grad_parts])
    grad_attended = grad_attended.reshape(queries.shape)
    scores = masked_scores(queries, keys_rot, allowed)
    soft_exact = jnp.exp(scores - kept["log_totals"])
    soft_weights = soft_exact.astype(bf16)
    grad_values = jnp.einsum(
        "hqk,qhd->khd", soft_weights, grad_attended, preferred_element_type=f32
    )
    grad_soft = jnp.einsum("qhd,khd->hqk", grad_attended, values_in, preferred_element_type=f32)
    row_dots = jnp.sum(soft_exact * grad_soft, axis=2, keepdims=True)
    grad_scores = (soft_exact * (grad_soft - row_dots)).astype(bf16)
    grad_queries = jnp.einsum(
        "hqk,khd->qhd", grad_scores, keys_rot, preferred_element_type=f32
    ) * HEAD_DIM ** (-0.5)
    grad_keys = jnp.einsum(
        "hqk,qhd->khd", grad_scores, queries, preferred_element_type=f32
    ) * HEAD_DIM ** (-0.5)
    grad_projected = jnp.stack(
        [
            rotate_back(grad_queries, *tables),
            rotate_back(grad_keys, *tables),
            grad_values,
        ],
        axis=1,
    )
    grad_projected = grad_projected.astype(bf16).reshape(4 * row_count, -1)

    def project_back(k):
        return contract_last(grad_projected[k * row_count : (k + 1) * row_count], w_qkv)

    def weight_grads(gate):
        outer, inner, left, right = after_all(
            (grad_parts, kept["attended"], kept["normed"], grad_projected), gate
        )
        outer, inner, left = joined(outer), joined(inner), joined(left)
        width = inner.shape[1]
        of_q, of_k, of_v = (right[:, i * width : (i + 1) * width] for i in range(3))
        sent_one, add_one = add_core(lambda core: contract_rows(left, core(of_q, of_v)))
        sent_two, add_two = add_core(
            lambda core: contract_rows(core(left, outer), core(of_k, inner))
        )

        def add(gate):
            return joined([add_one(gate), add_two(gate)])

        finish.append(add)
        return add(()) if last else (sent_one, sent_two)

    grad_normed = scatter_parts(project_back, weight_grads)
    unused, pull_norm = jax.vjp(layer_norm, kept["inputs"], gain_first)
    grad_resid, grad_gain = pull_norm(grad_normed)
    return (grad_mid + grad_resid, finish[0], grad_gain)


def other_layer(own, after, pair_x, before_x, before_core):
    core_index = lax.axis_index("core")
    parity = lax.axis_index("x") % 2
    own = after_all(own, after)
    rows = own.shape[0]
    if pair_x:
        piece = rows // 4
        sent = lax.dynamic_slice_in_dim(own, (core_index * 2 + parity) * piece, piece)
        got = swap_layer(sent)
        kept = after_all(got, before_x)
        beside = lax.ppermute(kept, "x", [(0, 1), (1, 0), (2, 3), (3, 2)])
        half = in_order(parity, kept, beside)
    else:
        piece = rows // 2
        sent = lax.dynamic_slice_in_dim(own, core_index * piece, piece)
        got = half = swap_layer(sent)
    half = after_all(half, before_core)
    return in_order(core_index, half, swap_core(half)), got


def in_order(index, mine, other):
    low = jnp.where(index == 0, mine, other)
    high = jnp.where(index == 0, other, mine)
    return jnp.concatenate([low, high], axis=0)


def add_core(product):
    is_core0 = lax.axis_index("core") == 0
    sent = product(lambda one, two: jnp.where(is_core0, two, one)).astype(bf16)
    got = swap_core(sent)

    def add(gate):
        held = product(lambda one, two: after_all(jnp.where(is_core0, one, two), gate))
        return (held + got.astype(f32)).astype(bf16)

    return sent, add


def reduce_part(grads):
    return lax.psum_scatter(grads, ("zlo", "x"), scatter_dimension=0, tiled=True)


def reduce_part_now(grads):
    pieces = lax.all_to_all(grads, ("zlo", "x"), 0, 0, tiled=True)
    pieces = pieces.reshape(8, -1, pieces.shape[1])
    return jnp.sum(pieces.astype(f32), axis=0).astype(bf16)


def spread_part(part):
    copies = jnp.broadcast_to(part[None], (8,) + part.shape).reshape(-1, part.shape[1])
    half = lax.all_to_all(copies, ("zlo", "x"), 0, 0, tiled=True)
    beside = swap_core(half)
    is_core0 = lax.axis_index("core") == 0
    return jnp.where(is_core0, half, beside), jnp.where(is_core0, beside, half)


def join_sections(is_first, part_first, part_second):
    own = jnp.where(is_first, part_first, part_second)
    sent = jnp.where(is_first, part_second, part_first)
    return (own.astype(f32) + swap_section(sent).astype(f32)).astype(bf16)


def local(tokens, cotangent, lengths, gains, w_qkv, w_out, w_up, w_down):
    section_index = lax.axis_index("section")
    is_first = section_index == 0
    row_count = tokens.shape[1]
    full_rows = row_count * lax.axis_size("tensor")
    start_rows = jnp.where(is_first, tokens[0], tokens[1])
    end_grads = jnp.where(is_first, cotangent[0], cotangent[1])
    start_parts = gather_parts(start_rows)
    gains_other = swap_layer(gains[0])
    gains0 = jnp.where(is_first, gains[0], gains_other)
    gains1 = jnp.where(is_first, gains_other, gains[0])
    first_parts = [layer_norm(part.astype(f32), gains0[0]).astype(bf16) for part in start_parts]
    start_rows = start_rows.astype(f32)
    own = (
        jnp.transpose(w_qkv[0], (1, 0, 2)).reshape(-1, w_qkv.shape[3]),
        w_out[0],
        jnp.transpose(w_up[0], (1, 2, 0)).reshape(-1, w_up.shape[1]),
        w_down[0],
    )
    other_qkv, after = other_layer(own[0], (), False, (), start_parts)
    other_out, after_out = other_layer(own[1], after, False, (), ())
    layer0 = [jnp.where(is_first, own[0], other_qkv), jnp.where(is_first, own[1], other_out)]
    layer1 = [jnp.where(is_first, other_qkv, own[0]), jnp.where(is_first, other_out, own[1])]
    layer0[0] = joined(jnp.split(layer0[0], 3), 1)
    layer1[0] = joined(jnp.split(layer1[0], 3), 1)

    def feed_weights(attended, resid_mid):
        other_up, after = other_layer(own[2], after_out, True, attended, resid_mid)
        other_down, unused = other_layer(own[3], after, False, (), resid_mid)
        layer0.extend([jnp.where(is_first, own[2], other_up), jnp.where(is_first, own[3], other_down)])
        layer1.extend([jnp.where(is_first, other_up, own[2]), jnp.where(is_first, other_down, own[3])])

    doc_lengths = jnp.where(is_first, lengths[0, 0], lengths[1, 0])
    indices = jnp.arange(full_rows, dtype=jnp.int32)
    indices = (indices + lax.axis_index("tensor") * row_count) % full_rows
    doc_ids, positions = doc_layout(doc_lengths, indices)
    same_doc = doc_ids[:, None] == doc_ids[None, :]
    near = jnp.abs(indices[:, None] - indices[None, :]) <= WINDOW // 2
    allowed0 = same_doc & near
    allowed1 = same_doc
    tables0 = rope_tables(positions, 10000.0)
    tables1 = rope_tables(positions, 160000.0)

    out0, kept0 = forward_layer(
        start_rows, first_parts, gains0[1], layer0, allowed0, tables0, False, feed_weights
    )
    out0 = out0.astype(bf16)
    second_rows = out0.astype(f32)
    second_parts = gather_parts(layer_norm(second_rows, gains1[0]).astype(bf16))
    out1_of, kept1 = forward_layer(
        second_rows, second_parts, gains1[1], layer1, allowed1, tables1, True, lambda *points: None
    )
    mid1, add_ffn1, gain_mid1 = backward_ffn(
        end_grads.astype(f32), kept1, gains1[1], layer1, None
    )
    ffn1 = add_ffn1(mid1)
    in1, add_attn1, gain_first1 = backward_attn(
        mid1, kept1, gains1[0], layer1, allowed1, tables1, ffn1, False
    )
    ffn1 = reduce_part(ffn1)
    in1 = in1.astype(bf16)
    attn1 = add_attn1(in1)
    mid0, add_ffn0, gain_mid0 = backward_ffn(
        in1.astype(f32), kept0, gains0[1], layer0, attn1
    )
    attn1 = reduce_part(attn1)
    mid0 = after_all(mid0, ffn1)
    ffn0 = add_ffn0(mid0)
    in0, add_attn0, gain_first0 = backward_attn(
        mid0, kept0, gains0[0], layer0, allowed0, tables0, (ffn0, attn1), True
    )
    ffn0 = reduce_part_now(ffn0)
    in0 = in0.astype(bf16)
    attn0 = reduce_part_now(add_attn0(()))
    out1 = out1_of(attn0).astype(bf16)
    ffn_sum = after_all(join_sections(is_first, ffn0, ffn1), attn0)
    ffn_halves = spread_part(ffn_sum)
    attn_halves = spread_part(join_sections(is_first, attn0, attn1))
    hidden_width = w_up.shape[3]
    grad_up = jnp.stack([half[:hidden_width] for half in ffn_halves])
    down_rows = w_down.shape[1] // 2
    grad_down = joined([half[hidden_width : hidden_width + down_rows] for half in ffn_halves])
    model_width = w_qkv.shape[1]
    grad_qkv = jnp.stack(
        [
            attn_halves[0][:model_width],
            attn_halves[0][model_width:],
            attn_halves[1][:model_width],
        ]
    )
    grad_out = attn_halves[1][model_width:].T

    gain0 = jnp.stack([gain_first0, gain_mid0])
    gain1 = jnp.stack([gain_first1, gain_mid1])
    gain_own = jnp.where(is_first, gain0, gain1)
    gain_sent = jnp.where(is_first, gain1, gain0)
    gain_total = gain_own + swap_section(gain_sent)
    gain_total = sum_tensor(gain_total)
    gain_total = gain_total + swap_core(gain_total)
    gain_total = (
        gain_total
        + around(gain_total, "x", 1)
        + around(gain_total, "x", 2)
        + around(gain_total, "x", 3)
    )
    gain_total = gain_total + around(gain_total, "zlo", 1)

    got_out = swap_section(jnp.where(is_first, out1, out0))
    section_out = jnp.stack(
        [jnp.where(is_first, out0, got_out), jnp.where(is_first, got_out, out1)]
    )
    got_in = swap_section(jnp.where(is_first, in1, in0))
    input_grads = jnp.stack(
        [jnp.where(is_first, in0, got_in), jnp.where(is_first, got_in, in1)]
    )
    return (
        section_out[None],
        input_grads[None],
        gain_total[None],
        jnp.transpose(grad_qkv.astype(f32), (1, 0, 2))[None],
        grad_out.astype(f32)[None],
        jnp.transpose(grad_up.astype(f32), (2, 0, 1))[None],
        grad_down.astype(f32)[None],
    )


def solution(mesh):
    sizes = dict(zip(mesh.axis_names, mesh.devices.shape))
    fine = Mesh(
        mesh.devices.reshape(sizes["section"], 2, sizes["dp"] // 4, 2, sizes["tensor"]),
        ("section", "zlo", "x", "core", "tensor"),
    )
    rows = ("zlo", "x", "core", "tensor")
    in_specs = (
        P(None, rows, None),
        P(None, rows, None),
        P(None, DP, None),
        P("section", None, None),
        P("section", None, None, "tensor"),
        P("section", "tensor", None),
        P("section", None, None, "tensor"),
        P("section", "tensor", None),
    )
    out_specs = (
        P("section", None, rows, None),
        P("section", None, rows, None),
        P("section", None, None),
        P("section", None, None, "tensor"),
        P("section", "tensor", None),
        P("section", None, None, "tensor"),
        P("section", "tensor", None),
    )
    return jax.shard_map(local, mesh=fine, in_specs=in_specs, out_specs=out_specs, check_vma=False)
```

```python
import jax
import jax.numpy as jnp
from jax import lax
from jax.sharding import Mesh
from jax.sharding import PartitionSpec as P

HEAD_DIM = 64
WINDOW = 128

epsilon = 1e-05
bf16 = jnp.bfloat16
f32 = jnp.float32

DP = ("zlo", "x", "core")


def around(block, axis, distance):
    count = lax.axis_size(axis)
    return lax.ppermute(block, axis, [(i, (i + distance) % count) for i in range(count)])


def swap_core(block):
    return lax.ppermute(block, "core", [(0, 1), (1, 0)])


def swap_section(block):
    return lax.ppermute(block, "section", [(0, 1), (1, 0)])


def swap_layer(block):
    return lax.ppermute(block, ("section", "zlo"), [(0, 3), (1, 2), (2, 1), (3, 0)])


def gather_parts(block):
    far = around(block, "tensor", 2)
    ahead = around(block, "tensor", -1)
    behind = around(block, "tensor", 1)
    return [joined([block, ahead, behind]), far]


def scatter_parts(near, far):
    rows = far.shape[0]
    sent_far = around(far.astype(bf16), "tensor", 2)
    sent_ahead = around(near[rows : 2 * rows].astype(bf16), "tensor", 1)
    sent_behind = around(near[2 * rows :].astype(bf16), "tensor", -1)
    kept = near[:rows].astype(f32)
    return kept + sent_far.astype(f32) + sent_ahead.astype(f32) + sent_behind.astype(f32)


def joined(parts, axis=0):
    return jnp.concatenate(parts, axis=axis)


def after_all(values, *others):
    return lax.optimization_barrier((values,) + others)[0]


def sum_tensor(block):
    return (
        block
        + around(block, "tensor", 2)
        + around(block, "tensor", 1)
        + around(block, "tensor", -1)
    )


def layer_norm(values, gain_scale):
    centered = values - jnp.mean(values, axis=-1, keepdims=True)
    variance = jnp.mean(centered * centered, axis=-1, keepdims=True)
    return centered * lax.rsqrt(variance + epsilon) * gain_scale


def doc_layout(doc_lengths, indices):
    doc_ends = jnp.cumsum(doc_lengths)
    passed = indices[:, None] >= doc_ends[None, :]
    doc_ids = jnp.sum(passed.astype(jnp.int32), axis=1)
    starts = jnp.sum(jnp.where(passed, doc_lengths[None, :], 0), axis=1)
    return (doc_ids, indices - starts)


def rope_tables(positions, rope_base):
    half_dim = HEAD_DIM // 2
    inverse = rope_base ** (-2.0 * jnp.arange(half_dim, dtype=f32) / HEAD_DIM)
    angles = positions.astype(f32)[..., None] * inverse
    angles = jnp.concatenate([angles, angles], axis=-1)
    return (jnp.cos(angles), jnp.sin(angles))


def rotate(values, cosine_table, sine_table):
    half_dim = values.shape[-1] // 2
    turned = jnp.concatenate([-values[..., half_dim:], values[..., :half_dim]], axis=-1)
    return values * cosine_table[..., None, :] + turned * sine_table[..., None, :]


def rotate_back(gradients, cosine_table, sine_table):
    half_dim = gradients.shape[-1] // 2
    scaled = gradients * sine_table[..., None, :]
    turned = jnp.concatenate([scaled[..., half_dim:], -scaled[..., :half_dim]], axis=-1)
    return gradients * cosine_table[..., None, :] + turned


def masked_scores(queries, keys_rot, allowed):
    scores = jnp.einsum(
        "qhd,khd->hqk", queries, keys_rot, preferred_element_type=f32
    ) * HEAD_DIM ** (-0.5)
    return jnp.where(allowed[None], scores, -1e30)


def contract_rows(left_rows, right_rows):
    return lax.dot_general(
        left_rows, right_rows, (((0,), (0,)), ((), ())), preferred_element_type=f32
    )


def contract_last(left_rows, weight):
    return lax.dot_general(
        left_rows, weight, (((1,), (1,)), ((), ())), preferred_element_type=f32
    )


def times(left_rows, weight):
    return jnp.dot(left_rows, weight, preferred_element_type=f32)


def gelu_product(first_half, second_half):
    return jax.nn.gelu(first_half, approximate=False) * second_half


def in_turn(work, parts):
    first = work(0, parts[0])
    return first, work(1, after_all(parts[1], first))


def forward_layer(inputs, normed_parts, gain_mid, weights, allowed, tables, late, points):
    w_qkv, w_out = weights[0], weights[1]
    row_count = inputs.shape[0]
    local_width = w_out.shape[0]
    spans = (slice(0, 3 * row_count), slice(3 * row_count, 4 * row_count))

    def project(k, part):
        projected = times(part, w_qkv).reshape(part.shape[0], 3, -1, HEAD_DIM)
        turns = (tables[0][spans[k]], tables[1][spans[k]])
        return (
            rotate(projected[:, 0], *turns).astype(bf16),
            rotate(projected[:, 1], *turns).astype(bf16),
            projected[:, 2].astype(bf16),
        )

    near, far = in_turn(project, normed_parts)
    queries = (near[0], far[0])
    keys_all = joined([near[1], far[1]])
    values_all = joined([near[2], far[2]])

    def attend(k, own_queries):
        scores = masked_scores(own_queries, keys_all, allowed[spans[k]])
        largest = jnp.max(scores, axis=2, keepdims=True)
        exp_scores = jnp.exp(scores - largest)
        totals = jnp.sum(exp_scores, axis=2, keepdims=True)
        soft_weights = (exp_scores / totals).astype(bf16)
        mixed = jnp.einsum("hqk,khd->qhd", soft_weights, values_all, preferred_element_type=f32)
        mixed = mixed.reshape(own_queries.shape[0], local_width).astype(bf16)
        return largest + jnp.log(totals), mixed, times(mixed, w_out).astype(bf16)

    far_logs, far_mixed, far_term = attend(1, queries[1])
    near_logs, near_mixed, near_term = attend(0, after_all(queries[0], far_term))
    resid_mid = inputs + scatter_parts(near_term, far_term)
    points(near_mixed, resid_mid)
    w_up, w_down = weights[2], weights[3]
    mid_parts = gather_parts(layer_norm(resid_mid, gain_mid).astype(bf16))

    def feed(k, part):
        hidden = contract_last(part, w_up)
        local_hidden = hidden.shape[1] // 2
        gelu_in = hidden[:, :local_hidden]
        gate_mult = hidden[:, local_hidden:]
        mixed = gelu_product(gelu_in, gate_mult).astype(bf16)
        return gelu_in, gate_mult, mixed, None if late else times(mixed, w_down).astype(bf16)

    fed = in_turn(feed, mid_parts)
    if late:

        def result(gate):
            held = after_all((fed[0][2], fed[1][2]), gate)
            return [times(mixed, w_down).astype(bf16) for mixed in held]

    else:
        result = resid_mid + scatter_parts(fed[0][3], fed[1][3])
    kept = dict(
        inputs=inputs,
        resid_mid=resid_mid,
        normed=normed_parts,
        queries=joined(queries),
        keys=keys_all,
        values=values_all,
        log_totals=joined([near_logs, far_logs], 1),
        attended=(near_mixed, far_mixed),
        normed_mid=mid_parts,
        gelu_in=(fed[0][0], fed[1][0]),
        gate_mult=(fed[0][1], fed[1][1]),
        mixed=(fed[0][2], fed[1][2]),
    )
    return (result, kept)


def backward_ffn(grad_result, kept, gain_mid, weights):
    w_up, w_down = weights[2], weights[3]
    grad_parts = gather_parts(grad_result.astype(bf16))

    def feed_back(k, part):
        grad_mixed = contract_last(part, w_down)
        unused, pull_gelu = jax.vjp(gelu_product, kept["gelu_in"][k], kept["gate_mult"][k])
        terms = tuple(term.astype(bf16) for term in pull_gelu(grad_mixed))
        return terms[0], terms[1], times(joined(terms, 1), w_up).astype(bf16)

    near, far = in_turn(feed_back, grad_parts)
    grad_normed_mid = scatter_parts(near[2], far[2])
    unused, pull_norm = jax.vjp(layer_norm, kept["resid_mid"], gain_mid)
    grad_resid, grad_gain = pull_norm(grad_normed_mid)

    def weight_grads(gate):
        outer, inner, left, first, second = after_all(
            (grad_parts, kept["mixed"], kept["normed_mid"], (near[0], far[0]), (near[1], far[1])),
            gate,
        )
        outer, inner, left = joined(outer), joined(inner), joined(left)
        first, second = joined(first), joined(second)
        half = inner.shape[1] // 2
        front, back = inner[:, :half], inner[:, half:]
        up = add_core(lambda core: contract_rows(core(first, second), left))
        down = add_core(lambda core: contract_rows(core(front, back), outer))
        rows = up.shape[0] + down.shape[0]
        blank = jnp.zeros((-rows % 128, up.shape[1]), bf16)
        return joined([up, down, blank])

    return (grad_result + grad_resid, weight_grads, grad_gain)


def backward_attn(grad_mid, kept, gain_first, weights, allowed, tables):
    w_qkv, w_out = weights[0], weights[1]
    queries, keys_rot, values_in = kept["queries"], kept["keys"], kept["values"]
    row_count = grad_mid.shape[0]
    grad_parts = gather_parts(grad_mid.astype(bf16))
    near, far = in_turn(lambda k, part: contract_last(part, w_out).astype(bf16), grad_parts)
    grad_attended = joined([near, far]).reshape(queries.shape)
    scores = masked_scores(queries, keys_rot, allowed)
    soft_exact = jnp.exp(scores - kept["log_totals"])
    soft_weights = soft_exact.astype(bf16)
    grad_values = jnp.einsum(
        "hqk,qhd->khd", soft_weights, grad_attended, preferred_element_type=f32
    )
    grad_soft = jnp.einsum("qhd,khd->hqk", grad_attended, values_in, preferred_element_type=f32)
    row_dots = jnp.sum(soft_exact * grad_soft, axis=2, keepdims=True)
    grad_scores = (soft_exact * (grad_soft - row_dots)).astype(bf16)
    grad_queries = jnp.einsum(
        "hqk,khd->qhd", grad_scores, keys_rot, preferred_element_type=f32
    ) * HEAD_DIM ** (-0.5)
    grad_keys = jnp.einsum(
        "hqk,qhd->khd", grad_scores, queries, preferred_element_type=f32
    ) * HEAD_DIM ** (-0.5)
    grad_projected = jnp.stack(
        [
            rotate_back(grad_queries, *tables),
            rotate_back(grad_keys, *tables),
            grad_values,
        ],
        axis=1,
    )
    grad_projected = grad_projected.astype(bf16).reshape(4 * row_count, -1)
    far_term = contract_last(grad_projected[3 * row_count :], w_qkv).astype(bf16)
    near_term = contract_last(grad_projected[: 3 * row_count], w_qkv).astype(bf16)
    grad_normed = scatter_parts(near_term, far_term)
    unused, pull_norm = jax.vjp(layer_norm, kept["inputs"], gain_first)
    grad_resid, grad_gain = pull_norm(grad_normed)

    def gain_before():
        total = 0.0
        for term, normed in zip((near_term, far_term), kept["normed"]):
            total = total + jnp.sum(term.astype(f32) * normed.astype(f32), axis=0)
        return total / gain_first

    def weight_grads(gate, gains):
        outer, inner, left, right = after_all(
            (grad_parts, kept["attended"], kept["normed"], grad_projected), gate
        )
        outer, inner, left = joined(outer), joined(inner), joined(left)
        width = inner.shape[1]
        of_q, of_k, of_v = (right[:, i * width : (i + 1) * width] for i in range(3))
        one = add_core(lambda core: contract_rows(left, core(of_q, of_v)))
        two = add_core(lambda core: contract_rows(core(left, outer), core(of_k, inner)))
        extra = jnp.stack(gains).astype(bf16).reshape(-1, width)
        blank = jnp.zeros((-extra.shape[0] % 128, width), bf16)
        return joined([one, two, extra, blank])

    return (grad_mid + grad_resid, weight_grads, grad_gain, gain_before)


def other_layer(own, after, pair_x, before_x, before_core):
    core_index = lax.axis_index("core")
    parity = lax.axis_index("x") % 2
    own = after_all(own, after)
    rows = own.shape[0]
    if pair_x:
        piece = rows // 4
        sent = lax.dynamic_slice_in_dim(own, (core_index * 2 + parity) * piece, piece)
        got = swap_layer(sent)
        kept = after_all(got, before_x)
        beside = lax.ppermute(kept, "x", [(0, 1), (1, 0), (2, 3), (3, 2)])
        half = in_order(parity, kept, beside)
    else:
        piece = rows // 2
        sent = lax.dynamic_slice_in_dim(own, core_index * piece, piece)
        got = half = swap_layer(sent)
    half = after_all(half, before_core)
    return in_order(core_index, half, swap_core(half)), got


def in_order(index, mine, other):
    low = jnp.where(index == 0, mine, other)
    high = jnp.where(index == 0, other, mine)
    return jnp.concatenate([low, high], axis=0)


def add_core(product):
    is_core0 = lax.axis_index("core") == 0
    sent = product(lambda one, two: jnp.where(is_core0, two, one)).astype(bf16)
    held = product(lambda one, two: jnp.where(is_core0, one, two))
    return (held + swap_core(sent).astype(f32)).astype(bf16)


def reduce_part(grads):
    return lax.psum_scatter(grads, ("zlo", "x"), scatter_dimension=0, tiled=True)


def reduce_part_now(grads):
    pieces = lax.all_to_all(grads, ("zlo", "x"), 0, 0, tiled=True)
    pieces = pieces.reshape(8, -1, pieces.shape[1])
    return jnp.sum(pieces.astype(f32), axis=0).astype(bf16)


def spread_part(part):
    copies = jnp.broadcast_to(part[None], (8,) + part.shape).reshape(-1, part.shape[1])
    half = lax.all_to_all(copies, ("zlo", "x"), 0, 0, tiled=True)
    beside = swap_core(half)
    is_core0 = lax.axis_index("core") == 0
    return jnp.where(is_core0, half, beside), jnp.where(is_core0, beside, half)


def pick_sections(is_first, part_first, part_second):
    own = jnp.where(is_first, part_first, part_second)
    sent = jnp.where(is_first, part_second, part_first)
    return own, sent


def local(tokens, cotangent, lengths, gains, w_qkv, w_out, w_up, w_down):
    section_index = lax.axis_index("section")
    is_first = section_index == 0
    row_count = tokens.shape[1]
    full_rows = row_count * lax.axis_size("tensor")
    start_rows = jnp.where(is_first, tokens[0], tokens[1])
    end_grads = jnp.where(is_first, cotangent[0], cotangent[1])
    start_parts = gather_parts(start_rows)
    gains_other = swap_layer(gains[0])
    gains0 = jnp.where(is_first, gains[0], gains_other)
    gains1 = jnp.where(is_first, gains_other, gains[0])
    first_parts = in_turn(
        lambda k, part: layer_norm(part.astype(f32), gains0[0]).astype(bf16), start_parts
    )
    start_rows = start_rows.astype(f32)
    own = (
        jnp.transpose(w_qkv[0], (1, 0, 2)).reshape(-1, w_qkv.shape[3]),
        w_out[0],
        jnp.transpose(w_up[0], (1, 2, 0)).reshape(-1, w_up.shape[1]),
        w_down[0],
    )
    other_qkv, after = other_layer(own[0], (), False, (), start_parts)
    other_out, after_out = other_layer(own[1], after, False, (), ())
    layer0 = [jnp.where(is_first, own[0], other_qkv), jnp.where(is_first, own[1], other_out)]
    layer1 = [jnp.where(is_first, other_qkv, own[0]), jnp.where(is_first, other_out, own[1])]
    layer0[0] = joined(jnp.split(layer0[0], 3), 1)
    layer1[0] = joined(jnp.split(layer1[0], 3), 1)

    def feed_weights(attended, resid_mid):
        other_up, after = other_layer(own[2], after_out, True, attended, resid_mid)
        other_down, unused = other_layer(own[3], after, False, (), resid_mid)
        layer0.extend([jnp.where(is_first, own[2], other_up), jnp.where(is_first, own[3], other_down)])
        layer1.extend([jnp.where(is_first, other_up, own[2]), jnp.where(is_first, other_down, own[3])])

    doc_lengths = jnp.where(is_first, lengths[0, 0], lengths[1, 0])
    indices = jnp.arange(full_rows, dtype=jnp.int32)
    blocks = jnp.array([0, 1, 3, 2], jnp.int32) + lax.axis_index("tensor")
    indices = (jnp.repeat(blocks, row_count) * row_count + indices % row_count) % full_rows
    doc_ids, positions = doc_layout(doc_lengths, indices)
    same_doc = doc_ids[:, None] == doc_ids[None, :]
    near = jnp.abs(indices[:, None] - indices[None, :]) <= WINDOW // 2
    allowed0 = same_doc & near
    allowed1 = same_doc
    tables0 = rope_tables(positions, 10000.0)
    tables1 = rope_tables(positions, 160000.0)

    out0, kept0 = forward_layer(
        start_rows, first_parts, gains0[1], layer0, allowed0, tables0, False, feed_weights
    )
    out0 = out0.astype(bf16)
    second_rows = out0.astype(f32)
    second_parts = gather_parts(layer_norm(second_rows, gains1[0]).astype(bf16))
    out1_of, kept1 = forward_layer(
        second_rows, second_parts, gains1[1], layer1, allowed1, tables1, True, lambda *points: None
    )
    mid1, ffn_grads1, gain_mid1 = backward_ffn(
        end_grads.astype(f32), kept1, gains1[1], layer1
    )
    in1, attn_grads1, gain_first1, unused = backward_attn(
        mid1, kept1, gains1[0], layer1, allowed1, tables1
    )
    in1 = in1.astype(bf16)
    ffn1 = ffn_grads1(mid1)
    in1, ffn1 = lax.optimization_barrier((in1, ffn1))
    ffn1 = reduce_part(ffn1)
    mid0, ffn_grads0, gain_mid0 = backward_ffn(in1.astype(f32), kept0, gains0[1], layer0)
    attn1 = reduce_part_now(attn_grads1(in1, [gain_first1, gain_mid1]))
    mid0 = after_all(mid0, ffn1, attn1)
    in0, attn_grads0, unused, gain_before = backward_attn(
        mid0, kept0, gains0[0], layer0, allowed0, tables0
    )
    in0 = in0.astype(bf16)
    ffn0 = reduce_part(ffn_grads0(mid0))
    attn_pack0 = attn_grads0((), [gain_before(), gain_mid0])
    attn0 = reduce_part_now(attn_pack0)
    out1_terms = out1_of(attn_pack0)
    attn0, in0 = lax.optimization_barrier((attn0, in0))
    attn_own, attn_sent = pick_sections(is_first, attn0, attn1)
    attn_sent = after_all(attn_sent, out1_terms)
    attn_sum = (attn_own.astype(f32) + swap_section(attn_sent).astype(f32)).astype(bf16)
    out1 = (kept1["resid_mid"] + scatter_parts(*out1_terms)).astype(bf16)
    ffn_own, ffn_sent = pick_sections(is_first, ffn0, ffn1)
    ffn_sum = (ffn_own.astype(f32) + swap_section(ffn_sent).astype(f32)).astype(bf16)
    attn_sum, out1 = lax.optimization_barrier((attn_sum, out1))
    attn_halves = spread_part(attn_sum)
    ffn_halves = spread_part(ffn_sum)
    gain_rows = sum(half[2 * w_qkv.shape[1] :][:8].astype(f32) for half in attn_halves)
    gain_total = sum_tensor(gain_rows).reshape(2, -1)
    hidden_width = w_up.shape[3]
    grad_up = jnp.stack([half[:hidden_width] for half in ffn_halves])
    down_rows = w_down.shape[1] // 2
    grad_down = joined([half[hidden_width : hidden_width + down_rows] for half in ffn_halves])
    model_width = w_qkv.shape[1]
    grad_qkv = jnp.stack(
        [
            attn_halves[0][:model_width],
            attn_halves[0][model_width : 2 * model_width],
            attn_halves[1][:model_width],
        ]
    )
    grad_out = attn_halves[1][model_width : 2 * model_width].T

    got_out = swap_section(jnp.where(is_first, out1, out0))
    section_out = jnp.stack(
        [jnp.where(is_first, out0, got_out), jnp.where(is_first, got_out, out1)]
    )
    got_in = swap_section(jnp.where(is_first, in1, in0))
    input_grads = jnp.stack(
        [jnp.where(is_first, in0, got_in), jnp.where(is_first, got_in, in1)]
    )
    return (
        section_out[None],
        input_grads[None],
        gain_total[None],
        jnp.transpose(grad_qkv.astype(f32), (1, 0, 2))[None],
        grad_out.astype(f32)[None],
        jnp.transpose(grad_up.astype(f32), (2, 0, 1))[None],
        grad_down.astype(f32)[None],
    )


def solution(mesh):
    sizes = dict(zip(mesh.axis_names, mesh.devices.shape))
    fine = Mesh(
        mesh.devices.reshape(sizes["section"], 2, sizes["dp"] // 4, 2, sizes["tensor"]),
        ("section", "zlo", "x", "core", "tensor"),
    )
    rows = ("zlo", "x", "core", "tensor")
    in_specs = (
        P(None, rows, None),
        P(None, rows, None),
        P(None, DP, None),
        P("section", None, None),
        P("section", None, None, "tensor"),
        P("section", "tensor", None),
        P("section", None, None, "tensor"),
        P("section", "tensor", None),
    )
    out_specs = (
        P("section", None, rows, None),
        P("section", None, rows, None),
        P("section", None, None),
        P("section", None, None, "tensor"),
        P("section", "tensor", None),
        P("section", None, None, "tensor"),
        P("section", "tensor", None),
    )
    return jax.shard_map(local, mesh=fine, in_specs=in_specs, out_specs=out_specs, check_vma=False)
```

```python
import jax
import jax.numpy as jnp
from jax import lax
from jax.sharding import Mesh
from jax.sharding import PartitionSpec as P

HEAD_DIM = 64
WINDOW = 128

epsilon = 1e-05
bf16 = jnp.bfloat16
f32 = jnp.float32

DP = ("zlo", "x", "core")


def around(block, axis, distance):
    count = lax.axis_size(axis)
    return lax.ppermute(block, axis, [(i, (i + distance) % count) for i in range(count)])


def swap_core(block):
    return lax.ppermute(block, "core", [(0, 1), (1, 0)])


def swap_section(block):
    return lax.ppermute(block, "section", [(0, 1), (1, 0)])


def swap_layer(block):
    return lax.ppermute(block, ("section", "zlo"), [(0, 3), (1, 2), (2, 1), (3, 0)])


def gather_parts(block):
    far = around(block, "tensor", 2)
    ahead = around(block, "tensor", -1)
    behind = around(block, "tensor", 1)
    return [joined([block, ahead, behind]), far]


def scatter_parts(near, far):
    rows = far.shape[0]
    sent_far = around(far.astype(bf16), "tensor", 2)
    sent_ahead = around(near[rows : 2 * rows].astype(bf16), "tensor", 1)
    sent_behind = around(near[2 * rows :].astype(bf16), "tensor", -1)
    kept = near[:rows].astype(f32)
    return kept + sent_far.astype(f32) + sent_ahead.astype(f32) + sent_behind.astype(f32)


def joined(parts, axis=0):
    return jnp.concatenate(parts, axis=axis)


def after_all(values, *others):
    return lax.optimization_barrier((values,) + others)[0]


def sum_tensor(block):
    return (
        block
        + around(block, "tensor", 2)
        + around(block, "tensor", 1)
        + around(block, "tensor", -1)
    )


def layer_norm(values, gain_scale):
    centered = values - jnp.mean(values, axis=-1, keepdims=True)
    variance = jnp.mean(centered * centered, axis=-1, keepdims=True)
    return centered * lax.rsqrt(variance + epsilon) * gain_scale


def doc_layout(doc_lengths, indices):
    doc_ends = jnp.cumsum(doc_lengths)
    passed = indices[:, None] >= doc_ends[None, :]
    doc_ids = jnp.sum(passed.astype(jnp.int32), axis=1)
    starts = jnp.sum(jnp.where(passed, doc_lengths[None, :], 0), axis=1)
    return (doc_ids, indices - starts)


def rope_tables(positions, rope_base):
    half_dim = HEAD_DIM // 2
    inverse = rope_base ** (-2.0 * jnp.arange(half_dim, dtype=f32) / HEAD_DIM)
    angles = positions.astype(f32)[..., None] * inverse
    angles = jnp.concatenate([angles, angles], axis=-1)
    return (jnp.cos(angles), jnp.sin(angles))


def rotate(values, cosine_table, sine_table):
    half_dim = values.shape[-1] // 2
    turned = jnp.concatenate([-values[..., half_dim:], values[..., :half_dim]], axis=-1)
    return values * cosine_table[..., None, :] + turned * sine_table[..., None, :]


def rotate_back(gradients, cosine_table, sine_table):
    half_dim = gradients.shape[-1] // 2
    scaled = gradients * sine_table[..., None, :]
    turned = jnp.concatenate([scaled[..., half_dim:], -scaled[..., :half_dim]], axis=-1)
    return gradients * cosine_table[..., None, :] + turned


def masked_scores(queries, keys_rot, allowed):
    scores = jnp.einsum(
        "qhd,khd->hqk", queries, keys_rot, preferred_element_type=f32
    ) * HEAD_DIM ** (-0.5)
    return jnp.where(allowed[None], scores, -1e30)


def contract_rows(left_rows, right_rows):
    return lax.dot_general(
        left_rows, right_rows, (((0,), (0,)), ((), ())), preferred_element_type=f32
    )


def contract_last(left_rows, weight):
    return lax.dot_general(
        left_rows, weight, (((1,), (1,)), ((), ())), preferred_element_type=f32
    )


def times(left_rows, weight):
    return jnp.dot(left_rows, weight, preferred_element_type=f32)


def gelu_product(first_half, second_half):
    return jax.nn.gelu(first_half, approximate=False) * second_half


def in_turn(work, parts):
    first = work(0, parts[0])
    return first, work(1, after_all(parts[1], first))


def forward_layer(inputs, normed_parts, gain_mid, weights, allowed, tables, late, points):
    w_qkv = weights[0]
    row_count = inputs.shape[0]
    local_width = w_qkv.shape[1] // 3
    spans = (slice(0, 3 * row_count), slice(3 * row_count, 4 * row_count))

    def project(k, part):
        projected = times(part, w_qkv).reshape(part.shape[0], 3, -1, HEAD_DIM)
        turns = (tables[0][spans[k]], tables[1][spans[k]])
        return (
            rotate(projected[:, 0], *turns).astype(bf16),
            rotate(projected[:, 1], *turns).astype(bf16),
            projected[:, 2].astype(bf16),
        )

    near, far = in_turn(project, normed_parts)
    queries = (near[0], far[0])
    keys_all = joined([near[1], far[1]])
    values_all = joined([near[2], far[2]])
    points[0](values_all)
    w_out = weights[1]

    def attend(k, own_queries):
        scores = masked_scores(own_queries, keys_all, allowed[spans[k]])
        largest = jnp.max(scores, axis=2, keepdims=True)
        exp_scores = jnp.exp(scores - largest)
        totals = jnp.sum(exp_scores, axis=2, keepdims=True)
        soft_weights = (exp_scores / totals).astype(bf16)
        mixed = jnp.einsum("hqk,khd->qhd", soft_weights, values_all, preferred_element_type=f32)
        mixed = mixed.reshape(own_queries.shape[0], local_width).astype(bf16)
        return largest + jnp.log(totals), mixed, times(mixed, w_out).astype(bf16)

    far_logs, far_mixed, far_term = attend(1, queries[1])
    points[1](far_term)
    near_logs, near_mixed, near_term = attend(0, after_all(queries[0], far_term))
    resid_mid = inputs + scatter_parts(near_term, far_term)
    points[2](resid_mid)
    mid_parts = gather_parts(layer_norm(resid_mid, gain_mid).astype(bf16))
    points[3](mid_parts)
    w_up, w_down = weights[2], weights[3]

    def feed(k, part):
        hidden = contract_last(part, w_up)
        local_hidden = hidden.shape[1] // 2
        gelu_in = hidden[:, :local_hidden]
        gate_mult = hidden[:, local_hidden:]
        mixed = gelu_product(gelu_in, gate_mult).astype(bf16)
        return gelu_in, gate_mult, mixed, None if late else times(mixed, w_down).astype(bf16)

    fed = in_turn(feed, mid_parts)
    if late:

        def result(gate):
            held = after_all((fed[0][2], fed[1][2]), gate)
            return [times(mixed, w_down).astype(bf16) for mixed in held]

    else:
        result = resid_mid + scatter_parts(fed[0][3], fed[1][3])
    kept = dict(
        inputs=inputs,
        resid_mid=resid_mid,
        normed=normed_parts,
        queries=joined(queries),
        keys=keys_all,
        values=values_all,
        log_totals=joined([near_logs, far_logs], 1),
        attended=(near_mixed, far_mixed),
        normed_mid=mid_parts,
        gelu_in=(fed[0][0], fed[1][0]),
        gate_mult=(fed[0][1], fed[1][1]),
        mixed=(fed[0][2], fed[1][2]),
    )
    return (result, kept)


def backward_ffn(grad_result, kept, gain_mid, weights):
    w_up, w_down = weights[2], weights[3]
    grad_parts = gather_parts(grad_result.astype(bf16))

    def feed_back(k, part):
        grad_mixed = contract_last(part, w_down)
        unused, pull_gelu = jax.vjp(gelu_product, kept["gelu_in"][k], kept["gate_mult"][k])
        terms = tuple(term.astype(bf16) for term in pull_gelu(grad_mixed))
        return terms[0], terms[1], times(joined(terms, 1), w_up).astype(bf16)

    near, far = in_turn(feed_back, grad_parts)
    grad_normed_mid = scatter_parts(near[2], far[2])
    unused, pull_norm = jax.vjp(layer_norm, kept["resid_mid"], gain_mid)
    grad_resid, grad_gain = pull_norm(grad_normed_mid)

    def weight_grads(gate):
        outer, inner, left, first, second = after_all(
            (grad_parts, kept["mixed"], kept["normed_mid"], (near[0], far[0]), (near[1], far[1])),
            gate,
        )
        outer, inner, left = joined(outer), joined(inner), joined(left)
        first, second = joined(first), joined(second)
        half = inner.shape[1] // 2
        front, back = inner[:, :half], inner[:, half:]
        up = add_core(lambda core: contract_rows(core(first, second), left))
        down = add_core(lambda core: contract_rows(core(front, back), outer))
        rows = up.shape[0] + down.shape[0]
        blank = jnp.zeros((-rows % 128, up.shape[1]), bf16)
        return joined([up, down, blank])

    return (grad_result + grad_resid, weight_grads, grad_gain)


def backward_attn(grad_mid, kept, gain_first, weights, allowed, tables, gate):
    w_qkv, w_out = weights[0], weights[1]
    queries, keys_rot, values_in = kept["queries"], kept["keys"], kept["values"]
    row_count = grad_mid.shape[0]
    grad_parts = gather_parts(grad_mid.astype(bf16))
    near, far = in_turn(lambda k, part: contract_last(part, w_out).astype(bf16), grad_parts)
    grad_attended = after_all(joined([near, far]).reshape(queries.shape), gate)
    scores = masked_scores(queries, keys_rot, allowed)
    soft_exact = jnp.exp(scores - kept["log_totals"])
    soft_weights = soft_exact.astype(bf16)
    grad_values = jnp.einsum(
        "hqk,qhd->khd", soft_weights, grad_attended, preferred_element_type=f32
    )
    grad_soft = jnp.einsum("qhd,khd->hqk", grad_attended, values_in, preferred_element_type=f32)
    row_dots = jnp.sum(soft_exact * grad_soft, axis=2, keepdims=True)
    grad_scores = (soft_exact * (grad_soft - row_dots)).astype(bf16)
    grad_queries = jnp.einsum(
        "hqk,khd->qhd", grad_scores, keys_rot, preferred_element_type=f32
    ) * HEAD_DIM ** (-0.5)
    grad_keys = jnp.einsum(
        "hqk,qhd->khd", grad_scores, queries, preferred_element_type=f32
    ) * HEAD_DIM ** (-0.5)
    grad_projected = jnp.stack(
        [
            rotate_back(grad_queries, *tables),
            rotate_back(grad_keys, *tables),
            grad_values,
        ],
        axis=1,
    )
    grad_projected = grad_projected.astype(bf16).reshape(4 * row_count, -1)
    far_term = contract_last(grad_projected[3 * row_count :], w_qkv).astype(bf16)
    near_term = contract_last(grad_projected[: 3 * row_count], w_qkv).astype(bf16)
    grad_normed = scatter_parts(near_term, far_term)
    unused, pull_norm = jax.vjp(layer_norm, kept["inputs"], gain_first)
    grad_resid, grad_gain = pull_norm(grad_normed)

    def gain_before():
        total = 0.0
        for term, normed in zip((near_term, far_term), kept["normed"]):
            total = total + jnp.sum(term.astype(f32) * normed.astype(f32), axis=0)
        return total / gain_first

    def weight_grads(gate, gains):
        outer, inner, left, right = after_all(
            (grad_parts, kept["attended"], kept["normed"], grad_projected), gate
        )
        outer, inner, left = joined(outer), joined(inner), joined(left)
        width = inner.shape[1]
        of_q, of_k, of_v = (right[:, i * width : (i + 1) * width] for i in range(3))
        one = add_core(lambda core: contract_rows(left, core(of_q, of_v)))
        two = add_core(lambda core: contract_rows(core(left, outer), core(of_k, inner)))
        extra = jnp.stack(gains).astype(bf16).reshape(-1, width)
        blank = jnp.zeros((-extra.shape[0] % 128, width), bf16)
        return joined([one, two, extra, blank])

    return (grad_mid + grad_resid, weight_grads, grad_gain, gain_before)


def fetch_half(own, after):
    piece = own.shape[0] // 2
    start = lax.axis_index("core") * piece
    return swap_layer(lax.dynamic_slice_in_dim(after_all(own, after), start, piece))


def both_halves(half, after=()):
    half = after_all(half, after)
    return in_order(lax.axis_index("core"), half, swap_core(half))


def by_layer(is_first, own, other):
    return jnp.where(is_first, own, other), jnp.where(is_first, other, own)


def in_order(index, mine, other):
    low = jnp.where(index == 0, mine, other)
    high = jnp.where(index == 0, other, mine)
    return jnp.concatenate([low, high], axis=0)


def add_core(product):
    is_core0 = lax.axis_index("core") == 0
    sent = product(lambda one, two: jnp.where(is_core0, two, one)).astype(bf16)
    held = product(lambda one, two: jnp.where(is_core0, one, two))
    return (held + swap_core(sent).astype(f32)).astype(bf16)


def reduce_part(grads):
    return lax.psum_scatter(grads, ("zlo", "x"), scatter_dimension=0, tiled=True)


def reduce_part_now(grads):
    pieces = lax.all_to_all(grads, ("zlo", "x"), 0, 0, tiled=True)
    pieces = pieces.reshape(8, -1, pieces.shape[1])
    return jnp.sum(pieces.astype(f32), axis=0).astype(bf16)


def spread_part(part):
    copies = jnp.broadcast_to(part[None], (8,) + part.shape).reshape(-1, part.shape[1])
    half = lax.all_to_all(copies, ("zlo", "x"), 0, 0, tiled=True)
    beside = swap_core(half)
    is_core0 = lax.axis_index("core") == 0
    return jnp.where(is_core0, half, beside), jnp.where(is_core0, beside, half)


def pick_sections(is_first, part_first, part_second):
    own = jnp.where(is_first, part_first, part_second)
    sent = jnp.where(is_first, part_second, part_first)
    return own, sent


def local(tokens, cotangent, lengths, gains, w_qkv, w_out, w_up, w_down):
    section_index = lax.axis_index("section")
    is_first = section_index == 0
    row_count = tokens.shape[1]
    full_rows = row_count * lax.axis_size("tensor")
    start_rows = jnp.where(is_first, tokens[0], tokens[1])
    end_grads = jnp.where(is_first, cotangent[0], cotangent[1])
    start_parts = gather_parts(start_rows)
    gains_other = swap_layer(gains[0])
    gains0 = jnp.where(is_first, gains[0], gains_other)
    gains1 = jnp.where(is_first, gains_other, gains[0])
    start_rows = start_rows.astype(f32)
    own = (
        jnp.transpose(w_qkv[0], (1, 0, 2)).reshape(-1, w_qkv.shape[3]),
        w_out[0],
        jnp.transpose(w_up[0], (1, 2, 0)).reshape(-1, w_up.shape[1]),
        w_down[0],
    )
    half_qkv = fetch_half(own[0], ())
    start_parts, lengths = after_all((start_parts, lengths), half_qkv)
    first_parts = in_turn(
        lambda k, part: layer_norm(part.astype(f32), gains0[0]).astype(bf16), start_parts
    )
    half_out = fetch_half(own[1], half_qkv)
    qkv0, qkv1 = by_layer(is_first, own[0], both_halves(half_qkv))
    layer0 = [joined(jnp.split(qkv0, 3), 1)]
    layer1 = [joined(jnp.split(qkv1, 3), 1)]
    hidden_width = w_up.shape[3]
    moving = []

    def at_projected(values):
        out0, out1 = by_layer(is_first, own[1], both_halves(half_out, values))
        layer0.append(out0)
        layer1.append(out1)
        moving.append(fetch_half(own[2][:hidden_width], (half_out, values)))

    def at_far_term(far_term):
        moving.append(both_halves(moving[0], far_term))
        moving.append(fetch_half(own[2][hidden_width:], (moving[0], far_term)))

    def at_mid(resid_mid):
        moving.append(both_halves(moving[2], resid_mid))
        moving.append(fetch_half(own[3], (moving[2], resid_mid)))

    def at_gathered(parts):
        up0, up1 = by_layer(is_first, own[2], joined([moving[1], moving[3]]))
        down0, down1 = by_layer(is_first, own[3], both_halves(moving[4], parts))
        layer0.extend([up0, down0])
        layer1.extend([up1, down1])

    points = (at_projected, at_far_term, at_mid, at_gathered)

    doc_lengths = jnp.where(is_first, lengths[0, 0], lengths[1, 0])
    indices = jnp.arange(full_rows, dtype=jnp.int32)
    blocks = jnp.array([0, 1, 3, 2], jnp.int32) + lax.axis_index("tensor")
    indices = (jnp.repeat(blocks, row_count) * row_count + indices % row_count) % full_rows
    doc_ids, positions = doc_layout(doc_lengths, indices)
    same_doc = doc_ids[:, None] == doc_ids[None, :]
    near = jnp.abs(indices[:, None] - indices[None, :]) <= WINDOW // 2
    allowed0 = same_doc & near
    allowed1 = same_doc
    tables0 = rope_tables(positions, 10000.0)
    tables1 = rope_tables(positions, 160000.0)

    out0, kept0 = forward_layer(
        start_rows, first_parts, gains0[1], layer0, allowed0, tables0, False, points
    )
    out0 = out0.astype(bf16)
    second_rows = out0.astype(f32)
    second_parts = gather_parts(layer_norm(second_rows, gains1[0]).astype(bf16))
    out1_of, kept1 = forward_layer(
        second_rows, second_parts, gains1[1], layer1, allowed1, tables1, True, (lambda value: None,) * 4
    )
    mid1, ffn_grads1, gain_mid1 = backward_ffn(
        end_grads.astype(f32), kept1, gains1[1], layer1
    )
    in1, attn_grads1, gain_first1, unused = backward_attn(
        mid1, kept1, gains1[0], layer1, allowed1, tables1, ()
    )
    in1 = in1.astype(bf16)
    ffn1 = ffn_grads1(mid1)
    in1, ffn1 = lax.optimization_barrier((in1, ffn1))
    ffn1 = reduce_part(ffn1)
    mid0, ffn_grads0, gain_mid0 = backward_ffn(in1.astype(f32), kept0, gains0[1], layer0)
    attn1 = reduce_part_now(attn_grads1(in1, [gain_first1, gain_mid1]))
    mid0 = after_all(mid0, ffn1, attn1)
    ffn_pack0 = ffn_grads0(mid0)
    in0, attn_grads0, unused, gain_before = backward_attn(
        mid0, kept0, gains0[0], layer0, allowed0, tables0, ffn_pack0
    )
    in0 = in0.astype(bf16)
    ffn0 = reduce_part(ffn_pack0)
    attn_pack0 = attn_grads0((), [gain_before(), gain_mid0])
    attn0 = reduce_part_now(attn_pack0)
    out1_terms = out1_of(attn_pack0)
    attn0, in0 = lax.optimization_barrier((attn0, in0))
    attn_own, attn_sent = pick_sections(is_first, attn0, attn1)
    attn_sent = after_all(attn_sent, out1_terms)
    attn_sum = (attn_own.astype(f32) + swap_section(attn_sent).astype(f32)).astype(bf16)
    out1 = (kept1["resid_mid"] + scatter_parts(*out1_terms)).astype(bf16)
    ffn_own, ffn_sent = pick_sections(is_first, ffn0, ffn1)
    ffn_sum = (ffn_own.astype(f32) + swap_section(ffn_sent).astype(f32)).astype(bf16)
    attn_sum, out1 = lax.optimization_barrier((attn_sum, out1))
    attn_halves = spread_part(attn_sum)
    ffn_halves = spread_part(ffn_sum)
    gain_rows = sum(half[2 * w_qkv.shape[1] :][:8].astype(f32) for half in attn_halves)
    gain_total = sum_tensor(gain_rows).reshape(2, -1)
    grad_up = jnp.stack([half[:hidden_width] for half in ffn_halves])
    down_rows = w_down.shape[1] // 2
    grad_down = joined([half[hidden_width : hidden_width + down_rows] for half in ffn_halves])
    model_width = w_qkv.shape[1]
    grad_qkv = jnp.stack(
        [
            attn_halves[0][:model_width],
            attn_halves[0][model_width : 2 * model_width],
            attn_halves[1][:model_width],
        ]
    )
    grad_out = attn_halves[1][model_width : 2 * model_width].T

    got_out = swap_section(jnp.where(is_first, out1, out0))
    section_out = jnp.stack(
        [jnp.where(is_first, out0, got_out), jnp.where(is_first, got_out, out1)]
    )
    got_in = swap_section(jnp.where(is_first, in1, in0))
    input_grads = jnp.stack(
        [jnp.where(is_first, in0, got_in), jnp.where(is_first, got_in, in1)]
    )
    return (
        section_out[None],
        input_grads[None],
        gain_total[None],
        jnp.transpose(grad_qkv.astype(f32), (1, 0, 2))[None],
        grad_out.astype(f32)[None],
        jnp.transpose(grad_up.astype(f32), (2, 0, 1))[None],
        grad_down.astype(f32)[None],
    )


def solution(mesh):
    sizes = dict(zip(mesh.axis_names, mesh.devices.shape))
    fine = Mesh(
        mesh.devices.reshape(sizes["section"], 2, sizes["dp"] // 4, 2, sizes["tensor"]),
        ("section", "zlo", "x", "core", "tensor"),
    )
    rows = ("zlo", "x", "core", "tensor")
    in_specs = (
        P(None, rows, None),
        P(None, rows, None),
        P(None, DP, None),
        P("section", None, None),
        P("section", None, None, "tensor"),
        P("section", "tensor", None),
        P("section", None, None, "tensor"),
        P("section", "tensor", None),
    )
    out_specs = (
        P("section", None, rows, None),
        P("section", None, rows, None),
        P("section", None, None),
        P("section", None, None, "tensor"),
        P("section", "tensor", None),
        P("section", None, None, "tensor"),
        P("section", "tensor", None),
    )
    return jax.shard_map(local, mesh=fine, in_specs=in_specs, out_specs=out_specs, check_vma=False)
```

```python
import jax
import jax.numpy as jnp
from jax import lax
from jax.sharding import Mesh
from jax.sharding import PartitionSpec as P

HEAD_DIM = 64
WINDOW = 128

epsilon = 1e-05
bf16 = jnp.bfloat16
f32 = jnp.float32

DP = ("zlo", "x", "core")


def around(block, axis, distance):
    count = lax.axis_size(axis)
    return lax.ppermute(block, axis, [(i, (i + distance) % count) for i in range(count)])


def swap_core(block):
    return lax.ppermute(block, "core", [(0, 1), (1, 0)])


def swap_section(block):
    return lax.ppermute(block, "section", [(0, 1), (1, 0)])


def swap_layer(block):
    return lax.ppermute(block, ("section", "zlo"), [(0, 3), (1, 2), (2, 1), (3, 0)])


def gather_parts(block):
    far = around(block, "tensor", 2)
    ahead = around(block, "tensor", -1)
    behind = around(block, "tensor", 1)
    return [joined([block, ahead, behind]), far]


def scatter_parts(near, far):
    rows = far.shape[0]
    sent_far = around(far.astype(bf16), "tensor", 2)
    sent_ahead = around(near[rows : 2 * rows].astype(bf16), "tensor", 1)
    sent_behind = around(near[2 * rows :].astype(bf16), "tensor", -1)
    kept = near[:rows].astype(f32)
    return kept + sent_far.astype(f32) + sent_ahead.astype(f32) + sent_behind.astype(f32)


def joined(parts, axis=0):
    return jnp.concatenate(parts, axis=axis)


def after_all(values, *others):
    return lax.optimization_barrier((values,) + others)[0]


def sum_tensor(block):
    return (
        block
        + around(block, "tensor", 2)
        + around(block, "tensor", 1)
        + around(block, "tensor", -1)
    )


def layer_norm(values, gain_scale):
    centered = values - jnp.mean(values, axis=-1, keepdims=True)
    variance = jnp.mean(centered * centered, axis=-1, keepdims=True)
    return centered * lax.rsqrt(variance + epsilon) * gain_scale


def doc_layout(doc_lengths, indices):
    doc_ends = jnp.cumsum(doc_lengths)
    passed = indices[:, None] >= doc_ends[None, :]
    doc_ids = jnp.sum(passed.astype(jnp.int32), axis=1)
    starts = jnp.sum(jnp.where(passed, doc_lengths[None, :], 0), axis=1)
    return (doc_ids, indices - starts)


def rope_tables(positions, rope_base):
    half_dim = HEAD_DIM // 2
    inverse = rope_base ** (-2.0 * jnp.arange(half_dim, dtype=f32) / HEAD_DIM)
    angles = positions.astype(f32)[..., None] * inverse
    angles = jnp.concatenate([angles, angles], axis=-1)
    return (jnp.cos(angles), jnp.sin(angles))


def rotate(values, cosine_table, sine_table):
    half_dim = values.shape[-1] // 2
    turned = jnp.concatenate([-values[..., half_dim:], values[..., :half_dim]], axis=-1)
    return values * cosine_table[..., None, :] + turned * sine_table[..., None, :]


def rotate_back(gradients, cosine_table, sine_table):
    half_dim = gradients.shape[-1] // 2
    scaled = gradients * sine_table[..., None, :]
    turned = jnp.concatenate([scaled[..., half_dim:], -scaled[..., :half_dim]], axis=-1)
    return gradients * cosine_table[..., None, :] + turned


def masked_scores(queries, keys_rot, allowed):
    scores = jnp.einsum(
        "qhd,khd->hqk", queries, keys_rot, preferred_element_type=f32
    ) * HEAD_DIM ** (-0.5)
    return jnp.where(allowed[None], scores, -1e30)


def contract_rows(left_rows, right_rows):
    return lax.dot_general(
        left_rows, right_rows, (((0,), (0,)), ((), ())), preferred_element_type=f32
    )


def contract_last(left_rows, weight):
    return lax.dot_general(
        left_rows, weight, (((1,), (1,)), ((), ())), preferred_element_type=f32
    )


def times(left_rows, weight):
    return jnp.dot(left_rows, weight, preferred_element_type=f32)


def gelu_product(first_half, second_half):
    return jax.nn.gelu(first_half, approximate=False) * second_half


def in_turn(work, parts):
    first = work(0, parts[0])
    return first, work(1, after_all(parts[1], first))


def forward_layer(inputs, normed_parts, gain_mid, weights, allowed, tables, late, points):
    w_qkv = weights[0]
    row_count = inputs.shape[0]
    local_width = w_qkv.shape[1] // 3
    spans = (slice(0, 3 * row_count), slice(3 * row_count, 4 * row_count))

    def project(k, part):
        projected = times(part, w_qkv).reshape(part.shape[0], 3, -1, HEAD_DIM)
        turns = (tables[0][spans[k]], tables[1][spans[k]])
        return (
            rotate(projected[:, 0], *turns).astype(bf16),
            rotate(projected[:, 1], *turns).astype(bf16),
            projected[:, 2].astype(bf16),
        )

    near, far = in_turn(project, normed_parts)
    queries = (near[0], far[0])
    keys_all = joined([near[1], far[1]])
    values_all = joined([near[2], far[2]])
    points[0](values_all)
    w_out = weights[1]

    def attend(k, own_queries):
        scores = masked_scores(own_queries, keys_all, allowed[spans[k]])
        largest = jnp.max(scores, axis=2, keepdims=True)
        exp_scores = jnp.exp(scores - largest)
        totals = jnp.sum(exp_scores, axis=2, keepdims=True)
        soft_weights = (exp_scores / totals).astype(bf16)
        mixed = jnp.einsum("hqk,khd->qhd", soft_weights, values_all, preferred_element_type=f32)
        mixed = mixed.reshape(own_queries.shape[0], local_width).astype(bf16)
        return largest + jnp.log(totals), mixed, times(mixed, w_out).astype(bf16)

    far_logs, far_mixed, far_term = attend(1, queries[1])
    points[1](far_term)
    near_logs, near_mixed, near_term = attend(0, after_all(queries[0], far_term))
    resid_mid = inputs + scatter_parts(near_term, far_term)
    points[2](resid_mid)
    mid_parts = gather_parts(layer_norm(resid_mid, gain_mid).astype(bf16))
    points[3](mid_parts)
    w_up, w_down = weights[2], weights[3]

    def feed(k, part):
        hidden = contract_last(part, w_up)
        local_hidden = hidden.shape[1] // 2
        gelu_in = hidden[:, :local_hidden]
        gate_mult = hidden[:, local_hidden:]
        mixed = gelu_product(gelu_in, gate_mult).astype(bf16)
        return gelu_in, gate_mult, mixed, None if late else times(mixed, w_down).astype(bf16)

    fed = in_turn(feed, mid_parts)
    if late:

        def result(gate):
            held = after_all((fed[0][2], fed[1][2]), gate)
            return [times(mixed, w_down).astype(bf16) for mixed in held]

    else:
        result = resid_mid + scatter_parts(fed[0][3], fed[1][3])
    kept = dict(
        inputs=inputs,
        resid_mid=resid_mid,
        normed=normed_parts,
        queries=joined(queries),
        keys=keys_all,
        values=values_all,
        log_totals=joined([near_logs, far_logs], 1),
        attended=(near_mixed, far_mixed),
        normed_mid=mid_parts,
        gelu_in=(fed[0][0], fed[1][0]),
        gate_mult=(fed[0][1], fed[1][1]),
        mixed=(fed[0][2], fed[1][2]),
    )
    return (result, kept)


def backward_ffn(grad_result, kept, gain_mid, weights):
    w_up, w_down = weights[2], weights[3]
    grad_parts = gather_parts(grad_result.astype(bf16))

    def feed_back(k, part):
        grad_mixed = contract_last(part, w_down)
        unused, pull_gelu = jax.vjp(gelu_product, kept["gelu_in"][k], kept["gate_mult"][k])
        terms = tuple(term.astype(bf16) for term in pull_gelu(grad_mixed))
        return terms[0], terms[1], times(joined(terms, 1), w_up).astype(bf16)

    near, far = in_turn(feed_back, grad_parts)
    grad_normed_mid = scatter_parts(near[2], far[2])
    unused, pull_norm = jax.vjp(layer_norm, kept["resid_mid"], gain_mid)
    grad_resid, grad_gain = pull_norm(grad_normed_mid)

    def weight_grads(gate):
        outer, inner, left, first, second = after_all(
            (grad_parts, kept["mixed"], kept["normed_mid"], (near[0], far[0]), (near[1], far[1])),
            gate,
        )
        outer, inner, left = joined(outer), joined(inner), joined(left)
        first, second = joined(first), joined(second)
        half = inner.shape[1] // 2
        front, back = inner[:, :half], inner[:, half:]
        up = add_core(lambda core: contract_rows(core(first, second), left))
        down = add_core(lambda core: contract_rows(core(front, back), outer))
        rows = up.shape[0] + down.shape[0]
        blank = jnp.zeros((-rows % 128, up.shape[1]), bf16)
        return joined([up, down, blank])

    return (grad_result + grad_resid, weight_grads, grad_gain)


def backward_attn(grad_mid, kept, gain_first, weights, allowed, tables, gate):
    w_qkv, w_out = weights[0], weights[1]
    queries, keys_rot, values_in = kept["queries"], kept["keys"], kept["values"]
    row_count = grad_mid.shape[0]
    grad_parts = gather_parts(grad_mid.astype(bf16))
    near, far = in_turn(lambda k, part: contract_last(part, w_out).astype(bf16), grad_parts)
    grad_attended = after_all(joined([near, far]).reshape(queries.shape), gate)
    scores = masked_scores(queries, keys_rot, allowed)
    soft_exact = jnp.exp(scores - kept["log_totals"])
    soft_weights = soft_exact.astype(bf16)
    grad_values = jnp.einsum(
        "hqk,qhd->khd", soft_weights, grad_attended, preferred_element_type=f32
    )
    grad_soft = jnp.einsum("qhd,khd->hqk", grad_attended, values_in, preferred_element_type=f32)
    row_dots = jnp.sum(soft_exact * grad_soft, axis=2, keepdims=True)
    grad_scores = (soft_exact * (grad_soft - row_dots)).astype(bf16)
    grad_queries = jnp.einsum(
        "hqk,khd->qhd", grad_scores, keys_rot, preferred_element_type=f32
    ) * HEAD_DIM ** (-0.5)
    grad_keys = jnp.einsum(
        "hqk,qhd->khd", grad_scores, queries, preferred_element_type=f32
    ) * HEAD_DIM ** (-0.5)
    grad_projected = jnp.stack(
        [
            rotate_back(grad_queries, *tables),
            rotate_back(grad_keys, *tables),
            grad_values,
        ],
        axis=1,
    )
    grad_projected = grad_projected.astype(bf16).reshape(4 * row_count, -1)
    far_term = contract_last(grad_projected[3 * row_count :], w_qkv).astype(bf16)
    near_term = contract_last(grad_projected[: 3 * row_count], w_qkv).astype(bf16)
    grad_normed = scatter_parts(near_term, far_term)
    unused, pull_norm = jax.vjp(layer_norm, kept["inputs"], gain_first)
    grad_resid, grad_gain = pull_norm(grad_normed)

    def gain_before():
        total = 0.0
        for term, normed in zip((near_term, far_term), kept["normed"]):
            total = total + jnp.sum(term.astype(f32) * normed.astype(f32), axis=0)
        return total / gain_first

    def weight_grads(gate, gains):
        outer, inner, left, right = after_all(
            (grad_parts, kept["attended"], kept["normed"], grad_projected), gate
        )
        outer, inner, left = joined(outer), joined(inner), joined(left)
        width = inner.shape[1]
        of_q, of_k, of_v = (right[:, i * width : (i + 1) * width] for i in range(3))
        one = add_core(lambda core: contract_rows(left, core(of_q, of_v)))
        two = add_core(lambda core: contract_rows(core(left, outer), core(of_k, inner)))
        extra = jnp.stack(gains).astype(bf16).reshape(-1, width)
        blank = jnp.zeros((-extra.shape[0] % 128, width), bf16)
        return joined([one, two, extra, blank])

    return (grad_mid + grad_resid, weight_grads, grad_gain, gain_before)


def fetch_half(own, after):
    piece = own.shape[0] // 2
    start = lax.axis_index("core") * piece
    return swap_layer(lax.dynamic_slice_in_dim(after_all(own, after), start, piece))


def both_halves(half, after=()):
    half = after_all(half, after)
    return in_order(lax.axis_index("core"), half, swap_core(half))


def by_layer(is_first, own, other):
    return jnp.where(is_first, own, other), jnp.where(is_first, other, own)


def in_order(index, mine, other):
    low = jnp.where(index == 0, mine, other)
    high = jnp.where(index == 0, other, mine)
    return jnp.concatenate([low, high], axis=0)


def add_core(product):
    is_core0 = lax.axis_index("core") == 0
    sent = product(lambda one, two: jnp.where(is_core0, two, one)).astype(bf16)
    held = product(lambda one, two: jnp.where(is_core0, one, two))
    return (held + swap_core(sent).astype(f32)).astype(bf16)


def reduce_part(grads):
    return lax.psum_scatter(grads, ("zlo", "x"), scatter_dimension=0, tiled=True)


def reduce_part_now(grads):
    pieces = lax.all_to_all(grads, ("zlo", "x"), 0, 0, tiled=True)
    pieces = pieces.reshape(8, -1, pieces.shape[1])
    return jnp.sum(pieces.astype(f32), axis=0).astype(bf16)


def spread_part(part):
    copies = jnp.broadcast_to(part[None], (8,) + part.shape).reshape(-1, part.shape[1])
    return lax.all_to_all(copies, ("zlo", "x"), 0, 0, tiled=True)


def trade_halves(half):
    beside = swap_core(half)
    is_core0 = lax.axis_index("core") == 0
    return jnp.where(is_core0, half, beside), jnp.where(is_core0, beside, half)


def pick_sections(is_first, part_first, part_second):
    own = jnp.where(is_first, part_first, part_second)
    sent = jnp.where(is_first, part_second, part_first)
    return own, sent


def local(tokens, cotangent, lengths, gains, w_qkv, w_out, w_up, w_down):
    section_index = lax.axis_index("section")
    is_first = section_index == 0
    row_count = tokens.shape[1]
    full_rows = row_count * lax.axis_size("tensor")
    start_rows = jnp.where(is_first, tokens[0], tokens[1])
    end_grads = jnp.where(is_first, cotangent[0], cotangent[1])
    start_parts = gather_parts(start_rows)
    gains_other = swap_layer(gains[0])
    gains0 = jnp.where(is_first, gains[0], gains_other)
    gains1 = jnp.where(is_first, gains_other, gains[0])
    start_rows = start_rows.astype(f32)
    own = (
        jnp.transpose(w_qkv[0], (1, 0, 2)).reshape(-1, w_qkv.shape[3]),
        w_out[0],
        jnp.transpose(w_up[0], (1, 2, 0)).reshape(-1, w_up.shape[1]),
        w_down[0],
    )
    half_qkv = fetch_half(own[0], ())
    start_parts, lengths = after_all((start_parts, lengths), half_qkv)
    first_parts = in_turn(
        lambda k, part: layer_norm(part.astype(f32), gains0[0]).astype(bf16), start_parts
    )
    half_out = fetch_half(own[1], half_qkv)
    qkv0, qkv1 = by_layer(is_first, own[0], both_halves(half_qkv))
    layer0 = [joined(jnp.split(qkv0, 3), 1)]
    layer1 = [joined(jnp.split(qkv1, 3), 1)]
    hidden_width = w_up.shape[3]
    moving = []

    def at_projected(values):
        out0, out1 = by_layer(is_first, own[1], both_halves(half_out, values))
        layer0.append(out0)
        layer1.append(out1)
        moving.append(fetch_half(own[2][:hidden_width], (half_out, values)))

    def at_far_term(far_term):
        moving.append(both_halves(moving[0], far_term))
        moving.append(fetch_half(own[2][hidden_width:], (moving[0], far_term)))

    def at_mid(resid_mid):
        moving.append(both_halves(moving[2], resid_mid))
        moving.append(fetch_half(own[3], (moving[2], resid_mid)))

    def at_gathered(parts):
        up0, up1 = by_layer(is_first, own[2], joined([moving[1], moving[3]]))
        down0, down1 = by_layer(is_first, own[3], both_halves(moving[4], parts))
        layer0.extend([up0, down0])
        layer1.extend([up1, down1])

    points = (at_projected, at_far_term, at_mid, at_gathered)

    doc_lengths = jnp.where(is_first, lengths[0, 0], lengths[1, 0])
    indices = jnp.arange(full_rows, dtype=jnp.int32)
    blocks = jnp.array([0, 1, 3, 2], jnp.int32) + lax.axis_index("tensor")
    indices = (jnp.repeat(blocks, row_count) * row_count + indices % row_count) % full_rows
    doc_ids, positions = doc_layout(doc_lengths, indices)
    same_doc = doc_ids[:, None] == doc_ids[None, :]
    near = jnp.abs(indices[:, None] - indices[None, :]) <= WINDOW // 2
    allowed0 = same_doc & near
    allowed1 = same_doc
    tables0 = rope_tables(positions, 10000.0)
    tables1 = rope_tables(positions, 160000.0)

    out0, kept0 = forward_layer(
        start_rows, first_parts, gains0[1], layer0, allowed0, tables0, False, points
    )
    out0 = out0.astype(bf16)
    second_rows = out0.astype(f32)
    second_parts = gather_parts(layer_norm(second_rows, gains1[0]).astype(bf16))
    out1_of, kept1 = forward_layer(
        second_rows, second_parts, gains1[1], layer1, allowed1, tables1, True, (lambda value: None,) * 4
    )
    mid1, ffn_grads1, gain_mid1 = backward_ffn(
        end_grads.astype(f32), kept1, gains1[1], layer1
    )
    in1, attn_grads1, gain_first1, unused = backward_attn(
        mid1, kept1, gains1[0], layer1, allowed1, tables1, ()
    )
    in1 = in1.astype(bf16)
    ffn1 = ffn_grads1(mid1)
    in1, ffn1 = lax.optimization_barrier((in1, ffn1))
    ffn1 = reduce_part(ffn1)
    mid0, ffn_grads0, gain_mid0 = backward_ffn(in1.astype(f32), kept0, gains0[1], layer0)
    attn1 = reduce_part_now(attn_grads1(in1, [gain_first1, gain_mid1]))
    mid0 = after_all(mid0, ffn1, attn1)
    ffn_pack0 = ffn_grads0(mid0)
    in0, attn_grads0, unused, gain_before = backward_attn(
        mid0, kept0, gains0[0], layer0, allowed0, tables0, ffn_pack0
    )
    in0 = in0.astype(bf16)
    ffn0 = reduce_part(ffn_pack0)
    attn_pack0 = attn_grads0((), [gain_before(), gain_mid0])
    attn0 = reduce_part_now(attn_pack0)
    out1_terms = out1_of(attn_pack0)
    ffn_own, ffn_sent = pick_sections(is_first, ffn0, ffn1)
    ffn_sum = (ffn_own.astype(f32) + swap_section(ffn_sent).astype(f32)).astype(bf16)
    attn0, ffn_sum, in0 = lax.optimization_barrier((attn0, ffn_sum, in0))
    attn_own, attn_sent = pick_sections(is_first, attn0, attn1)
    attn_sent = after_all(attn_sent, out1_terms)
    attn_sum = (attn_own.astype(f32) + swap_section(attn_sent).astype(f32)).astype(bf16)
    out1 = (kept1["resid_mid"] + scatter_parts(*out1_terms)).astype(bf16)
    ffn_half = spread_part(ffn_sum)
    attn_sum, out1, ffn_half = lax.optimization_barrier((attn_sum, out1, ffn_half))
    attn_half = spread_part(attn_sum)
    ffn_halves = trade_halves(ffn_half)
    attn_halves = trade_halves(attn_half)
    gain_rows = sum(half[2 * w_qkv.shape[1] :][:8].astype(f32) for half in attn_halves)
    gain_total = sum_tensor(gain_rows).reshape(2, -1)
    grad_up = jnp.stack([half[:hidden_width] for half in ffn_halves])
    down_rows = w_down.shape[1] // 2
    grad_down = joined([half[hidden_width : hidden_width + down_rows] for half in ffn_halves])
    model_width = w_qkv.shape[1]
    grad_qkv = jnp.stack(
        [
            attn_halves[0][:model_width],
            attn_halves[0][model_width : 2 * model_width],
            attn_halves[1][:model_width],
        ]
    )
    grad_out = attn_halves[1][model_width : 2 * model_width].T

    got_out = swap_section(jnp.where(is_first, out1, out0))
    got_out = after_all(got_out, attn_half)
    section_out = jnp.stack(
        [jnp.where(is_first, out0, got_out), jnp.where(is_first, got_out, out1)]
    )
    got_in = swap_section(jnp.where(is_first, in1, in0))
    got_in = after_all(got_in, attn_half)
    input_grads = jnp.stack(
        [jnp.where(is_first, in0, got_in), jnp.where(is_first, got_in, in1)]
    )
    return (
        section_out[None],
        input_grads[None],
        gain_total[None],
        jnp.transpose(grad_qkv.astype(f32), (1, 0, 2))[None],
        grad_out.astype(f32)[None],
        jnp.transpose(grad_up.astype(f32), (2, 0, 1))[None],
        grad_down.astype(f32)[None],
    )


def solution(mesh):
    sizes = dict(zip(mesh.axis_names, mesh.devices.shape))
    fine = Mesh(
        mesh.devices.reshape(sizes["section"], 2, sizes["dp"] // 4, 2, sizes["tensor"]),
        ("section", "zlo", "x", "core", "tensor"),
    )
    rows = ("zlo", "x", "core", "tensor")
    in_specs = (
        P(None, rows, None),
        P(None, rows, None),
        P(None, DP, None),
        P("section", None, None),
        P("section", None, None, "tensor"),
        P("section", "tensor", None),
        P("section", None, None, "tensor"),
        P("section", "tensor", None),
    )
    out_specs = (
        P("section", None, rows, None),
        P("section", None, rows, None),
        P("section", None, None),
        P("section", None, None, "tensor"),
        P("section", "tensor", None),
        P("section", None, None, "tensor"),
        P("section", "tensor", None),
    )
    return jax.shard_map(local, mesh=fine, in_specs=in_specs, out_specs=out_specs, check_vma=False)
```

```python
import functools

import jax
import jax.numpy as jnp
from jax import lax
from jax.experimental import pallas as pl
from jax.experimental.pallas import tpu as pltpu
from jax.sharding import Mesh
from jax.sharding import PartitionSpec as P

HEAD_DIM = 64
WINDOW = 128

epsilon = 1e-05
bf16 = jnp.bfloat16
f32 = jnp.float32

BLOCK = 128

DP = ("zlo", "x", "core")


def around(block, axis, distance):
    count = lax.axis_size(axis)
    return lax.ppermute(block, axis, [(i, (i + distance) % count) for i in range(count)])


def swap_core(block):
    return lax.ppermute(block, "core", [(0, 1), (1, 0)])


def swap_section(block):
    return lax.ppermute(block, "section", [(0, 1), (1, 0)])


def swap_layer(block):
    return lax.ppermute(block, ("section", "zlo"), [(0, 3), (1, 2), (2, 1), (3, 0)])


def gather_parts(block):
    far = around(block, "tensor", 2)
    ahead = around(block, "tensor", -1)
    behind = around(block, "tensor", 1)
    return [joined([block, ahead, behind]), far]


def scatter_parts(near, far):
    rows = far.shape[0]
    sent_far = around(far.astype(bf16), "tensor", 2)
    sent_ahead = around(near[rows : 2 * rows].astype(bf16), "tensor", 1)
    sent_behind = around(near[2 * rows :].astype(bf16), "tensor", -1)
    kept = near[:rows].astype(f32)
    return kept + sent_far.astype(f32) + sent_ahead.astype(f32) + sent_behind.astype(f32)


def joined(parts, axis=0):
    return jnp.concatenate(parts, axis=axis)


def after_all(values, *others):
    return lax.optimization_barrier((values,) + others)[0]


def sum_tensor(block):
    return (
        block
        + around(block, "tensor", 2)
        + around(block, "tensor", 1)
        + around(block, "tensor", -1)
    )


def layer_norm(values, gain_scale):
    centered = values - jnp.mean(values, axis=-1, keepdims=True)
    variance = jnp.mean(centered * centered, axis=-1, keepdims=True)
    return centered * lax.rsqrt(variance + epsilon) * gain_scale


def doc_layout(doc_lengths, indices):
    doc_ends = jnp.cumsum(doc_lengths)
    passed = indices[:, None] >= doc_ends[None, :]
    doc_ids = jnp.sum(passed.astype(jnp.int32), axis=1)
    starts = jnp.sum(jnp.where(passed, doc_lengths[None, :], 0), axis=1)
    return (doc_ids, indices - starts)


def rope_tables(positions, rope_base, heads):
    half_dim = HEAD_DIM // 2
    inverse = rope_base ** (-2.0 * jnp.arange(half_dim, dtype=f32) / HEAD_DIM)
    angles = positions.astype(f32)[:, None] * inverse
    cosine, sine = jnp.cos(angles), jnp.sin(angles)
    cosine = jnp.concatenate([cosine, cosine], axis=-1)
    sine = jnp.concatenate([-sine, sine], axis=-1)
    return (jnp.tile(cosine, (1, heads)), jnp.tile(sine, (1, heads)))


def contract_rows(left_rows, right_rows):
    return lax.dot_general(
        left_rows, right_rows, (((0,), (0,)), ((), ())), preferred_element_type=f32
    )


def contract_last(left_rows, weight):
    return lax.dot_general(
        left_rows, weight, (((1,), (1,)), ((), ())), preferred_element_type=f32
    )


def times(left_rows, weight):
    return jnp.dot(left_rows, weight, preferred_element_type=f32)


def gelu_product(first_half, second_half):
    return jax.nn.gelu(first_half, approximate=False) * second_half


def dot_nt(left, right):
    return lax.dot_general(left, right, (((1,), (1,)), ((), ())), preferred_element_type=f32)


def dot_tn(left, right):
    return lax.dot_general(left, right, (((0,), (0,)), ((), ())), preferred_element_type=f32)


def swap_halves(values):
    width = values.shape[1]
    lanes = lax.broadcasted_iota(jnp.int32, values.shape, 1)
    up = pltpu.roll(values, width - HEAD_DIM // 2, 1)
    down = pltpu.roll(values, HEAD_DIM // 2, 1)
    return jnp.where(lanes % HEAD_DIM < HEAD_DIM // 2, up, down)


def excluded_bias(marks_row, marks_col, start, windowed):
    docs = marks_row[0:1, pl.ds(start, BLOCK)]
    allowed = marks_col[:, 0:1] == docs
    if windowed:
        apart = marks_col[:, 1:2] - marks_row[1:2, pl.ds(start, BLOCK)]
        allowed = allowed & (jnp.abs(apart) <= WINDOW // 2)
    return jnp.where(allowed, 0.0, -1e30)


def attend_kernel(
    windowed,
    near, far, w_qkv, w_out, cosine, sine, marks_row, marks_col,
    queries, keys, values, logs, attended, near_term, far_term,
    projected,
):
    near_rows = near.shape[0]
    width = w_out.shape[0]
    projected[:near_rows] = jnp.dot(near[...], w_qkv[...], preferred_element_type=f32)
    projected[near_rows:] = jnp.dot(far[...], w_qkv[...], preferred_element_type=f32)
    for index, target in ((0, queries), (1, keys)):
        part = projected[:, index * width : (index + 1) * width]
        turned = part * cosine[...] + swap_halves(part) * sine[...]
        target[...] = turned.astype(bf16)
    values[...] = projected[:, 2 * width :].astype(bf16)
    heads = width // HEAD_DIM
    lanes = lax.broadcasted_iota(jnp.int32, (BLOCK, width), 1) // HEAD_DIM

    def step(index, carry):
        start = pl.multiple_of(index * BLOCK, BLOCK)
        bias = excluded_bias(marks_row, marks_col, start, windowed)
        block = queries[pl.ds(start, BLOCK)] * jnp.asarray(HEAD_DIM ** (-0.5), bf16)
        total = jnp.zeros((BLOCK, width), f32)
        for head in range(heads):
            own = jnp.where(lanes == head, block, jnp.zeros_like(block))
            scores = dot_nt(keys[...], own) + bias
            largest = jnp.max(scores, axis=0, keepdims=True)
            powers = jnp.exp(scores - largest)
            sums = jnp.sum(powers, axis=0, keepdims=True)
            soft = (powers * (1.0 / sums)).astype(bf16)
            logs[pl.ds(head, 1), pl.ds(start, BLOCK)] = largest + jnp.log(sums)
            total = jnp.where(lanes == head, dot_tn(soft, values[...]), total)
        attended[pl.ds(start, BLOCK)] = total.astype(bf16)
        return carry

    lax.fori_loop(0, queries.shape[0] // BLOCK, step, 0)
    far_term[...] = jnp.dot(
        attended[near_rows:], w_out[...], preferred_element_type=f32
    ).astype(bf16)
    near_term[...] = jnp.dot(
        attended[:near_rows], w_out[...], preferred_element_type=f32
    ).astype(bf16)


def attend_back_kernel(
    windowed,
    near, far, w_qkv, w_out, cosine, sine, marks_row, marks_col,
    queries, keys, values, logs,
    grad_projected, near_term, far_term,
    grad_attended, grad_queries, grad_keys, grad_values,
):
    near_rows = near.shape[0]
    width = w_out.shape[0]
    grad_attended[:near_rows] = dot_nt(near[...], w_out[...]).astype(bf16)
    grad_attended[near_rows:] = dot_nt(far[...], w_out[...]).astype(bf16)
    grad_keys[...] = jnp.zeros_like(grad_keys)
    grad_values[...] = jnp.zeros_like(grad_values)
    heads = width // HEAD_DIM
    lanes = lax.broadcasted_iota(jnp.int32, (BLOCK, width), 1) // HEAD_DIM
    all_lanes = lax.broadcasted_iota(jnp.int32, queries.shape, 1) // HEAD_DIM

    def step(index, carry):
        start = pl.multiple_of(index * BLOCK, BLOCK)
        bias = excluded_bias(marks_row, marks_col, start, windowed)
        block = queries[pl.ds(start, BLOCK)] * jnp.asarray(HEAD_DIM ** (-0.5), bf16)
        grad_block = grad_attended[pl.ds(start, BLOCK)]
        total = jnp.zeros((BLOCK, width), f32)
        more_keys = jnp.zeros(queries.shape, f32)
        more_values = jnp.zeros(queries.shape, f32)
        for head in range(heads):
            own = jnp.where(lanes == head, block, jnp.zeros_like(block))
            own_grad = jnp.where(lanes == head, grad_block, jnp.zeros_like(grad_block))
            scores = dot_nt(keys[...], own) + bias
            soft = jnp.exp(scores - logs[pl.ds(head, 1), pl.ds(start, BLOCK)])
            grad_soft = dot_nt(values[...], own_grad)
            dots = jnp.sum(soft * grad_soft, axis=0, keepdims=True)
            grad_scores = (soft * (grad_soft - dots)).astype(bf16)
            more_values += jnp.dot(soft.astype(bf16), own_grad, preferred_element_type=f32)
            more_keys += jnp.dot(grad_scores, own, preferred_element_type=f32)
            total = jnp.where(lanes == head, dot_tn(grad_scores, keys[...]), total)
        grad_queries[pl.ds(start, BLOCK)] = total * HEAD_DIM ** (-0.5)
        grad_keys[...] += more_keys
        grad_values[...] += more_values
        return carry

    lax.fori_loop(0, queries.shape[0] // BLOCK, step, 0)
    for index, source in ((0, grad_queries), (1, grad_keys)):
        part = source[...]
        back = part * cosine[...] - swap_halves(part) * sine[...]
        grad_projected[:, index * width : (index + 1) * width] = back.astype(bf16)
    grad_projected[:, 2 * width :] = grad_values[...].astype(bf16)
    far_term[...] = dot_nt(grad_projected[near_rows:], w_qkv[...]).astype(bf16)
    near_term[...] = dot_nt(grad_projected[:near_rows], w_qkv[...]).astype(bf16)


def whole_call(kernel, out_shapes, scratch_shapes, flops, *operands):
    whole = pl.BlockSpec(memory_space=pltpu.VMEM)
    return pl.pallas_call(
        kernel,
        out_shape=[jax.ShapeDtypeStruct(*shape) for shape in out_shapes],
        in_specs=[whole] * len(operands),
        out_specs=[whole] * len(out_shapes),
        scratch_shapes=scratch_shapes,
        compiler_params=pltpu.CompilerParams(vmem_limit_bytes=40 * 1024 * 1024),
        cost_estimate=pl.CostEstimate(flops=flops, bytes_accessed=8 << 20, transcendentals=1 << 20),
    )(*operands)


def in_turn(work, parts):
    first = work(0, parts[0])
    return first, work(1, after_all(parts[1], first))


def forward_layer(inputs, normed_parts, gain_mid, weights, allowed, tables, late, points):
    w_qkv, w_out = weights[0], weights[1]
    near_rows, model_width = normed_parts[0].shape
    far_rows = normed_parts[1].shape[0]
    full_rows = near_rows + far_rows
    width = w_out.shape[0]
    windowed, marks_row, marks_col = allowed
    queries, keys, values, logs, attended, near_term, far_term = whole_call(
        functools.partial(attend_kernel, windowed),
        [((full_rows, width), bf16)] * 3
        + [((8, full_rows), f32), ((full_rows, width), bf16)]
        + [((near_rows, model_width), bf16), ((far_rows, model_width), bf16)],
        [pltpu.VMEM((full_rows, 3 * width), f32)],
        3 << 30,
        *normed_parts, w_qkv, w_out, *tables, marks_row, marks_col,
    )
    points[1](far_term)
    resid_mid = inputs + scatter_parts(near_term, far_term)
    points[2](resid_mid)
    mid_parts = gather_parts(layer_norm(resid_mid, gain_mid).astype(bf16))
    points[3](mid_parts)
    w_up, w_down = weights[2], weights[3]

    def feed(k, part):
        hidden = contract_last(part, w_up)
        local_hidden = hidden.shape[1] // 2
        gelu_in = hidden[:, :local_hidden]
        gate_mult = hidden[:, local_hidden:]
        mixed = gelu_product(gelu_in, gate_mult).astype(bf16)
        return gelu_in, gate_mult, mixed, None if late else times(mixed, w_down).astype(bf16)

    fed = in_turn(feed, mid_parts)
    if late:

        def result(gate):
            held = after_all((fed[0][2], fed[1][2]), gate)
            return [times(mixed, w_down).astype(bf16) for mixed in held]

    else:
        result = resid_mid + scatter_parts(fed[0][3], fed[1][3])
    kept = dict(
        inputs=inputs,
        resid_mid=resid_mid,
        normed=normed_parts,
        queries=queries,
        keys=keys,
        values=values,
        logs=logs,
        attended=attended,
        normed_mid=mid_parts,
        gelu_in=(fed[0][0], fed[1][0]),
        gate_mult=(fed[0][1], fed[1][1]),
        mixed=(fed[0][2], fed[1][2]),
    )
    return (result, kept)


def backward_ffn(grad_result, kept, gain_mid, weights):
    w_up, w_down = weights[2], weights[3]
    grad_parts = gather_parts(grad_result.astype(bf16))

    def feed_back(k, part):
        grad_mixed = contract_last(part, w_down)
        unused, pull_gelu = jax.vjp(gelu_product, kept["gelu_in"][k], kept["gate_mult"][k])
        terms = tuple(term.astype(bf16) for term in pull_gelu(grad_mixed))
        return terms[0], terms[1], times(joined(terms, 1), w_up).astype(bf16)

    near, far = in_turn(feed_back, grad_parts)
    grad_normed_mid = scatter_parts(near[2], far[2])
    unused, pull_norm = jax.vjp(layer_norm, kept["resid_mid"], gain_mid)
    grad_resid, grad_gain = pull_norm(grad_normed_mid)

    def weight_grads(gate):
        outer, inner, left, first, second = after_all(
            (grad_parts, kept["mixed"], kept["normed_mid"], (near[0], far[0]), (near[1], far[1])),
            gate,
        )
        outer, inner, left = joined(outer), joined(inner), joined(left)
        first, second = joined(first), joined(second)
        half = inner.shape[1] // 2
        front, back = inner[:, :half], inner[:, half:]
        up = add_core(lambda core: contract_rows(core(first, second), left))
        down = add_core(lambda core: contract_rows(core(front, back), outer))
        rows = up.shape[0] + down.shape[0]
        blank = jnp.zeros((-rows % 128, up.shape[1]), bf16)
        return joined([up, down, blank])

    return (grad_result + grad_resid, weight_grads, grad_gain)


def backward_attn(grad_mid, kept, gain_first, weights, allowed, tables, gate):
    w_qkv, w_out = weights[0], weights[1]
    grad_parts = gather_parts(grad_mid.astype(bf16))
    near, far = after_all(grad_parts, gate)
    full_rows, width = kept["queries"].shape
    windowed, marks_row, marks_col = allowed
    grad_projected, near_term, far_term = whole_call(
        functools.partial(attend_back_kernel, windowed),
        [((full_rows, 3 * width), bf16), (near.shape, bf16), (far.shape, bf16)],
        [pltpu.VMEM((full_rows, width), bf16)] + [pltpu.VMEM((full_rows, width), f32)] * 3,
        4 << 30,
        near, far, w_qkv, w_out, *tables, marks_row, marks_col,
        kept["queries"], kept["keys"], kept["values"], kept["logs"],
    )
    grad_normed = scatter_parts(near_term, far_term)
    unused, pull_norm = jax.vjp(layer_norm, kept["inputs"], gain_first)
    grad_resid, grad_gain = pull_norm(grad_normed)

    def gain_before():
        total = 0.0
        for term, normed in zip((near_term, far_term), kept["normed"]):
            total = total + jnp.sum(term.astype(f32) * normed.astype(f32), axis=0)
        return total / gain_first

    def weight_grads(gate, gains):
        outer, inner, left, right = after_all(
            (grad_parts, kept["attended"], kept["normed"], grad_projected), gate
        )
        outer, left = joined(outer), joined(left)
        width = inner.shape[1]
        of_q, of_k, of_v = (right[:, i * width : (i + 1) * width] for i in range(3))
        one = add_core(lambda core: contract_rows(left, core(of_q, of_v)))
        two = add_core(lambda core: contract_rows(core(left, outer), core(of_k, inner)))
        extra = jnp.stack(gains).astype(bf16).reshape(-1, width)
        blank = jnp.zeros((-extra.shape[0] % 128, width), bf16)
        return joined([one, two, extra, blank])

    return (grad_mid + grad_resid, weight_grads, grad_gain, gain_before)


def fetch_half(own, after):
    piece = own.shape[0] // 2
    start = lax.axis_index("core") * piece
    return swap_layer(lax.dynamic_slice_in_dim(after_all(own, after), start, piece))


def both_halves(half, after=()):
    half = after_all(half, after)
    return in_order(lax.axis_index("core"), half, swap_core(half))


def by_layer(is_first, own, other):
    return jnp.where(is_first, own, other), jnp.where(is_first, other, own)


def in_order(index, mine, other):
    low = jnp.where(index == 0, mine, other)
    high = jnp.where(index == 0, other, mine)
    return jnp.concatenate([low, high], axis=0)


def add_core(product):
    is_core0 = lax.axis_index("core") == 0
    sent = product(lambda one, two: jnp.where(is_core0, two, one)).astype(bf16)
    held = product(lambda one, two: jnp.where(is_core0, one, two))
    return (held + swap_core(sent).astype(f32)).astype(bf16)


def reduce_part(grads):
    return lax.psum_scatter(grads, ("zlo", "x"), scatter_dimension=0, tiled=True)


def reduce_part_now(grads):
    pieces = lax.all_to_all(grads, ("zlo", "x"), 0, 0, tiled=True)
    pieces = pieces.reshape(8, -1, pieces.shape[1])
    return jnp.sum(pieces.astype(f32), axis=0).astype(bf16)


def spread_part(part):
    copies = jnp.broadcast_to(part[None], (8,) + part.shape).reshape(-1, part.shape[1])
    return lax.all_to_all(copies, ("zlo", "x"), 0, 0, tiled=True)


def trade_halves(half):
    beside = swap_core(half)
    is_core0 = lax.axis_index("core") == 0
    return jnp.where(is_core0, half, beside), jnp.where(is_core0, beside, half)


def pick_sections(is_first, part_first, part_second):
    own = jnp.where(is_first, part_first, part_second)
    sent = jnp.where(is_first, part_second, part_first)
    return own, sent


def local(tokens, cotangent, lengths, gains, w_qkv, w_out, w_up, w_down):
    section_index = lax.axis_index("section")
    is_first = section_index == 0
    row_count = tokens.shape[1]
    full_rows = row_count * lax.axis_size("tensor")
    start_rows = jnp.where(is_first, tokens[0], tokens[1])
    end_grads = jnp.where(is_first, cotangent[0], cotangent[1])
    start_parts = gather_parts(start_rows)
    gains_other = swap_layer(gains[0])
    gains0 = jnp.where(is_first, gains[0], gains_other)
    gains1 = jnp.where(is_first, gains_other, gains[0])
    start_rows = start_rows.astype(f32)
    own = (
        jnp.transpose(w_qkv[0], (1, 0, 2)).reshape(-1, w_qkv.shape[3]),
        w_out[0],
        jnp.transpose(w_up[0], (1, 2, 0)).reshape(-1, w_up.shape[1]),
        w_down[0],
    )
    half_qkv = fetch_half(own[0], ())
    start_parts, lengths = after_all((start_parts, lengths), half_qkv)
    first_parts = in_turn(
        lambda k, part: layer_norm(part.astype(f32), gains0[0]).astype(bf16), start_parts
    )
    half_out = fetch_half(own[1], half_qkv)
    qkv0, qkv1 = by_layer(is_first, own[0], both_halves(half_qkv))
    layer0 = [joined(jnp.split(qkv0, 3), 1)]
    layer1 = [joined(jnp.split(qkv1, 3), 1)]
    hidden_width = w_up.shape[3]
    moving = []

    out0, out1 = by_layer(is_first, own[1], both_halves(half_out))
    layer0.append(out0)
    layer1.append(out1)
    moving.append(fetch_half(own[2][:hidden_width], half_out))

    def at_far_term(far_term):
        moving.append(both_halves(moving[0], far_term))
        moving.append(fetch_half(own[2][hidden_width:], (moving[0], far_term)))

    def at_mid(resid_mid):
        moving.append(both_halves(moving[2], resid_mid))
        moving.append(fetch_half(own[3], (moving[2], resid_mid)))

    def at_gathered(parts):
        up0, up1 = by_layer(is_first, own[2], joined([moving[1], moving[3]]))
        down0, down1 = by_layer(is_first, own[3], both_halves(moving[4], parts))
        layer0.extend([up0, down0])
        layer1.extend([up1, down1])

    points = (None, at_far_term, at_mid, at_gathered)

    doc_lengths = jnp.where(is_first, lengths[0, 0], lengths[1, 0])
    indices = jnp.arange(full_rows, dtype=jnp.int32)
    blocks = jnp.array([0, 1, 3, 2], jnp.int32) + lax.axis_index("tensor")
    indices = (jnp.repeat(blocks, row_count) * row_count + indices % row_count) % full_rows
    doc_ids, positions = doc_layout(doc_lengths, indices)
    marks_row = jnp.stack([doc_ids, indices])
    marks_col = jnp.stack([doc_ids, indices], axis=1)
    allowed0 = (True, marks_row, marks_col)
    allowed1 = (False, marks_row, marks_col)
    heads = w_out.shape[1] // HEAD_DIM
    tables0 = rope_tables(positions, 10000.0, heads)
    tables1 = rope_tables(positions, 160000.0, heads)

    out0, kept0 = forward_layer(
        start_rows, first_parts, gains0[1], layer0, allowed0, tables0, False, points
    )
    out0 = out0.astype(bf16)
    second_rows = out0.astype(f32)
    second_parts = gather_parts(layer_norm(second_rows, gains1[0]).astype(bf16))
    out1_of, kept1 = forward_layer(
        second_rows, second_parts, gains1[1], layer1, allowed1, tables1, True, (lambda value: None,) * 4
    )
    mid1, ffn_grads1, gain_mid1 = backward_ffn(
        end_grads.astype(f32), kept1, gains1[1], layer1
    )
    in1, attn_grads1, gain_first1, unused = backward_attn(
        mid1, kept1, gains1[0], layer1, allowed1, tables1, ()
    )
    in1 = in1.astype(bf16)
    ffn1 = ffn_grads1(mid1)
    in1, ffn1 = lax.optimization_barrier((in1, ffn1))
    ffn1 = reduce_part(ffn1)
    mid0, ffn_grads0, gain_mid0 = backward_ffn(in1.astype(f32), kept0, gains0[1], layer0)
    attn1 = reduce_part_now(attn_grads1(in1, [gain_first1, gain_mid1]))
    mid0 = after_all(mid0, ffn1, attn1)
    ffn_pack0 = ffn_grads0(mid0)
    in0, attn_grads0, unused, gain_before = backward_attn(
        mid0, kept0, gains0[0], layer0, allowed0, tables0, ffn_pack0
    )
    in0 = in0.astype(bf16)
    ffn0 = reduce_part(ffn_pack0)
    attn_pack0 = attn_grads0((), [gain_before(), gain_mid0])
    attn0 = reduce_part_now(attn_pack0)
    out1_terms = out1_of(attn_pack0)
    ffn_own, ffn_sent = pick_sections(is_first, ffn0, ffn1)
    ffn_sum = (ffn_own.astype(f32) + swap_section(ffn_sent).astype(f32)).astype(bf16)
    attn0, ffn_sum, in0 = lax.optimization_barrier((attn0, ffn_sum, in0))
    attn_own, attn_sent = pick_sections(is_first, attn0, attn1)
    attn_sent = after_all(attn_sent, out1_terms)
    attn_sum = (attn_own.astype(f32) + swap_section(attn_sent).astype(f32)).astype(bf16)
    attn_sum, ffn_sum = lax.optimization_barrier((attn_sum, ffn_sum))
    out1 = (kept1["resid_mid"] + scatter_parts(*out1_terms)).astype(bf16)
    ffn_half = spread_part(ffn_sum)
    attn_half = spread_part(attn_sum)
    ffn_halves = trade_halves(ffn_half)
    grad_up = jnp.stack([half[:hidden_width] for half in ffn_halves]).astype(f32)
    down_rows = w_down.shape[1] // 2
    grad_down = joined([half[hidden_width : hidden_width + down_rows] for half in ffn_halves])
    grad_down = grad_down.astype(f32)
    attn_half, grad_up, grad_down, out1 = lax.optimization_barrier(
        (attn_half, grad_up, grad_down, out1)
    )
    attn_halves = trade_halves(attn_half)
    gain_rows = sum(half[2 * w_qkv.shape[1] :][:8].astype(f32) for half in attn_halves)
    gain_total = sum_tensor(gain_rows).reshape(2, -1)
    model_width = w_qkv.shape[1]
    grad_qkv = jnp.stack(
        [
            attn_halves[0][:model_width],
            attn_halves[0][model_width : 2 * model_width],
            attn_halves[1][:model_width],
        ]
    )
    grad_out = attn_halves[1][model_width : 2 * model_width].T

    got_out = swap_section(jnp.where(is_first, out1, out0))
    got_out = after_all(got_out, attn_half)
    section_out = jnp.stack(
        [jnp.where(is_first, out0, got_out), jnp.where(is_first, got_out, out1)]
    )
    got_in = swap_section(jnp.where(is_first, in1, in0))
    got_in = after_all(got_in, attn_half)
    input_grads = jnp.stack(
        [jnp.where(is_first, in0, got_in), jnp.where(is_first, got_in, in1)]
    )
    return (
        section_out[None],
        input_grads[None],
        gain_total[None],
        jnp.transpose(grad_qkv.astype(f32), (1, 0, 2))[None],
        grad_out.astype(f32)[None],
        jnp.transpose(grad_up, (2, 0, 1))[None],
        grad_down[None],
    )


def solution(mesh):
    sizes = dict(zip(mesh.axis_names, mesh.devices.shape))
    fine = Mesh(
        mesh.devices.reshape(sizes["section"], 2, sizes["dp"] // 4, 2, sizes["tensor"]),
        ("section", "zlo", "x", "core", "tensor"),
    )
    rows = ("zlo", "x", "core", "tensor")
    in_specs = (
        P(None, rows, None),
        P(None, rows, None),
        P(None, DP, None),
        P("section", None, None),
        P("section", None, None, "tensor"),
        P("section", "tensor", None),
        P("section", None, None, "tensor"),
        P("section", "tensor", None),
    )
    out_specs = (
        P("section", None, rows, None),
        P("section", None, rows, None),
        P("section", None, None),
        P("section", None, None, "tensor"),
        P("section", "tensor", None),
        P("section", None, None, "tensor"),
        P("section", "tensor", None),
    )
    return jax.shard_map(local, mesh=fine, in_specs=in_specs, out_specs=out_specs, check_vma=False)
```

```python
import functools

import jax
import jax.numpy as jnp
from jax import lax
from jax.experimental import pallas as pl
from jax.experimental.pallas import tpu as pltpu
from jax.sharding import Mesh
from jax.sharding import PartitionSpec as P

HEAD_DIM = 64
WINDOW = 128

epsilon = 1e-05
bf16 = jnp.bfloat16
f32 = jnp.float32

BLOCK = 256

DP = ("zlo", "x", "core")


def around(block, axis, distance):
    count = lax.axis_size(axis)
    return lax.ppermute(block, axis, [(i, (i + distance) % count) for i in range(count)])


def swap_core(block):
    return lax.ppermute(block, "core", [(0, 1), (1, 0)])


def swap_section(block):
    return lax.ppermute(block, "section", [(0, 1), (1, 0)])


def swap_layer(block):
    return lax.ppermute(block, ("section", "zlo"), [(0, 3), (1, 2), (2, 1), (3, 0)])


def gather_parts(block):
    far = around(block, "tensor", 2)
    ahead = around(block, "tensor", -1)
    behind = around(block, "tensor", 1)
    return [joined([block, ahead, behind]), far]


def scatter_parts(near, far):
    rows = far.shape[0]
    sent_far = around(far.astype(bf16), "tensor", 2)
    sent_ahead = around(near[rows : 2 * rows].astype(bf16), "tensor", 1)
    sent_behind = around(near[2 * rows :].astype(bf16), "tensor", -1)
    kept = near[:rows].astype(f32)
    return kept + sent_far.astype(f32) + sent_ahead.astype(f32) + sent_behind.astype(f32)


def joined(parts, axis=0):
    return jnp.concatenate(parts, axis=axis)


def after_all(values, *others):
    return lax.optimization_barrier((values,) + others)[0]


def sum_tensor(block):
    return (
        block
        + around(block, "tensor", 2)
        + around(block, "tensor", 1)
        + around(block, "tensor", -1)
    )


def layer_norm(values, gain_scale):
    centered = values - jnp.mean(values, axis=-1, keepdims=True)
    variance = jnp.mean(centered * centered, axis=-1, keepdims=True)
    return centered * lax.rsqrt(variance + epsilon) * gain_scale


def doc_layout(doc_lengths, indices):
    doc_ends = jnp.cumsum(doc_lengths)
    passed = indices[:, None] >= doc_ends[None, :]
    doc_ids = jnp.sum(passed.astype(jnp.int32), axis=1)
    starts = jnp.sum(jnp.where(passed, doc_lengths[None, :], 0), axis=1)
    return (doc_ids, indices - starts)


def rope_tables(positions, rope_base, heads):
    half_dim = HEAD_DIM // 2
    inverse = rope_base ** (-2.0 * jnp.arange(half_dim, dtype=f32) / HEAD_DIM)
    angles = positions.astype(f32)[:, None] * inverse
    cosine, sine = jnp.cos(angles), jnp.sin(angles)
    cosine = jnp.concatenate([cosine, cosine], axis=-1)
    sine = jnp.concatenate([-sine, sine], axis=-1)
    return (jnp.tile(cosine, (1, heads)), jnp.tile(sine, (1, heads)))


def contract_rows(left_rows, right_rows):
    return lax.dot_general(
        left_rows, right_rows, (((0,), (0,)), ((), ())), preferred_element_type=f32
    )


def contract_last(left_rows, weight):
    return lax.dot_general(
        left_rows, weight, (((1,), (1,)), ((), ())), preferred_element_type=f32
    )


def times(left_rows, weight):
    return jnp.dot(left_rows, weight, preferred_element_type=f32)


def gelu_product(first_half, second_half):
    return jax.nn.gelu(first_half, approximate=False) * second_half


def dot_nt(left, right):
    return lax.dot_general(left, right, (((1,), (1,)), ((), ())), preferred_element_type=f32)


def dot_tn(left, right):
    return lax.dot_general(left, right, (((0,), (0,)), ((), ())), preferred_element_type=f32)


def swap_halves(values):
    width = values.shape[1]
    lanes = lax.broadcasted_iota(jnp.int32, values.shape, 1)
    up = pltpu.roll(values, width - HEAD_DIM // 2, 1)
    down = pltpu.roll(values, HEAD_DIM // 2, 1)
    return jnp.where(lanes % HEAD_DIM < HEAD_DIM // 2, up, down)


def excluded_bias(marks_row, marks_col, start, windowed):
    docs = marks_row[0:1, pl.ds(start, BLOCK)]
    allowed = marks_col[:, 0:1] == docs
    if windowed:
        apart = marks_col[:, 1:2] - marks_row[1:2, pl.ds(start, BLOCK)]
        allowed = allowed & (jnp.abs(apart) <= WINDOW // 2)
    return jnp.where(allowed, 0.0, -1e30)


def attend_kernel(
    windowed,
    near, far, w_qkv, w_out, cosine, sine, marks_row, marks_col,
    queries, keys, values, logs, attended, near_term, far_term,
    projected,
):
    near_rows = near.shape[0]
    width = w_out.shape[0]
    projected[:near_rows] = jnp.dot(near[...], w_qkv[...], preferred_element_type=f32)
    projected[near_rows:] = jnp.dot(far[...], w_qkv[...], preferred_element_type=f32)
    for index, target in ((0, queries), (1, keys)):
        part = projected[:, index * width : (index + 1) * width]
        turned = part * cosine[...] + swap_halves(part) * sine[...]
        target[...] = turned.astype(bf16)
    values[...] = projected[:, 2 * width :].astype(bf16)
    heads = width // HEAD_DIM
    lanes = lax.broadcasted_iota(jnp.int32, (BLOCK, width), 1) // HEAD_DIM

    def step(index, carry):
        start = pl.multiple_of(index * BLOCK, BLOCK)
        bias = excluded_bias(marks_row, marks_col, start, windowed)
        block = queries[pl.ds(start, BLOCK)] * jnp.asarray(HEAD_DIM ** (-0.5), bf16)
        total = jnp.zeros((BLOCK, width), f32)
        for head in range(heads):
            own = jnp.where(lanes == head, block, jnp.zeros_like(block))
            scores = dot_nt(keys[...], own) + bias
            largest = jnp.max(scores, axis=0, keepdims=True)
            powers = jnp.exp(scores - largest)
            sums = jnp.sum(powers, axis=0, keepdims=True)
            soft = (powers * (1.0 / sums)).astype(bf16)
            logs[pl.ds(head, 1), pl.ds(start, BLOCK)] = largest + jnp.log(sums)
            total = jnp.where(lanes == head, dot_tn(soft, values[...]), total)
        attended[pl.ds(start, BLOCK)] = total.astype(bf16)
        return carry

    lax.fori_loop(0, queries.shape[0] // BLOCK, step, 0)
    far_term[...] = jnp.dot(
        attended[near_rows:], w_out[...], preferred_element_type=f32
    ).astype(bf16)
    near_term[...] = jnp.dot(
        attended[:near_rows], w_out[...], preferred_element_type=f32
    ).astype(bf16)


def attend_back_kernel(
    windowed,
    near, far, w_qkv, w_out, cosine, sine, marks_row, marks_col,
    queries, keys, values, logs,
    grad_projected, near_term, far_term,
    grad_attended, grad_queries, grad_keys, grad_values,
):
    near_rows = near.shape[0]
    width = w_out.shape[0]
    grad_attended[:near_rows] = dot_nt(near[...], w_out[...]).astype(bf16)
    grad_attended[near_rows:] = dot_nt(far[...], w_out[...]).astype(bf16)
    grad_keys[...] = jnp.zeros_like(grad_keys)
    grad_values[...] = jnp.zeros_like(grad_values)
    heads = width // HEAD_DIM
    lanes = lax.broadcasted_iota(jnp.int32, (BLOCK, width), 1) // HEAD_DIM
    all_lanes = lax.broadcasted_iota(jnp.int32, queries.shape, 1) // HEAD_DIM

    def step(index, carry):
        start = pl.multiple_of(index * BLOCK, BLOCK)
        bias = excluded_bias(marks_row, marks_col, start, windowed)
        block = queries[pl.ds(start, BLOCK)] * jnp.asarray(HEAD_DIM ** (-0.5), bf16)
        grad_block = grad_attended[pl.ds(start, BLOCK)]
        total = jnp.zeros((BLOCK, width), f32)
        more_keys = jnp.zeros(queries.shape, f32)
        more_values = jnp.zeros(queries.shape, f32)
        for head in range(heads):
            own = jnp.where(lanes == head, block, jnp.zeros_like(block))
            own_grad = jnp.where(lanes == head, grad_block, jnp.zeros_like(grad_block))
            scores = dot_nt(keys[...], own) + bias
            soft = jnp.exp(scores - logs[pl.ds(head, 1), pl.ds(start, BLOCK)])
            grad_soft = dot_nt(values[...], own_grad)
            dots = jnp.sum(soft * grad_soft, axis=0, keepdims=True)
            grad_scores = (soft * (grad_soft - dots)).astype(bf16)
            more_values += jnp.dot(soft.astype(bf16), own_grad, preferred_element_type=f32)
            more_keys += jnp.dot(grad_scores, own, preferred_element_type=f32)
            total = jnp.where(lanes == head, dot_tn(grad_scores, keys[...]), total)
        grad_queries[pl.ds(start, BLOCK)] = total * HEAD_DIM ** (-0.5)
        grad_keys[...] += more_keys
        grad_values[...] += more_values
        return carry

    lax.fori_loop(0, queries.shape[0] // BLOCK, step, 0)
    for index, source in ((0, grad_queries), (1, grad_keys)):
        part = source[...]
        back = part * cosine[...] - swap_halves(part) * sine[...]
        grad_projected[:, index * width : (index + 1) * width] = back.astype(bf16)
    grad_projected[:, 2 * width :] = grad_values[...].astype(bf16)
    far_term[...] = dot_nt(grad_projected[near_rows:], w_qkv[...]).astype(bf16)
    near_term[...] = dot_nt(grad_projected[:near_rows], w_qkv[...]).astype(bf16)


def whole_call(kernel, out_shapes, scratch_shapes, flops, *operands):
    whole = pl.BlockSpec(memory_space=pltpu.VMEM)
    return pl.pallas_call(
        kernel,
        out_shape=[jax.ShapeDtypeStruct(*shape) for shape in out_shapes],
        in_specs=[whole] * len(operands),
        out_specs=[whole] * len(out_shapes),
        scratch_shapes=scratch_shapes,
        compiler_params=pltpu.CompilerParams(vmem_limit_bytes=40 * 1024 * 1024),
        cost_estimate=pl.CostEstimate(flops=flops, bytes_accessed=8 << 20, transcendentals=1 << 20),
    )(*operands)


def in_turn(work, parts):
    first = work(0, parts[0])
    return first, work(1, after_all(parts[1], first))


def forward_layer(inputs, normed_parts, gain_mid, weights, allowed, tables, late, points):
    w_qkv, w_out = weights[0], weights[1]
    near_rows, model_width = normed_parts[0].shape
    far_rows = normed_parts[1].shape[0]
    full_rows = near_rows + far_rows
    width = w_out.shape[0]
    windowed, marks_row, marks_col = allowed
    queries, keys, values, logs, attended, near_term, far_term = whole_call(
        functools.partial(attend_kernel, windowed),
        [((full_rows, width), bf16)] * 3
        + [((8, full_rows), f32), ((full_rows, width), bf16)]
        + [((near_rows, model_width), bf16), ((far_rows, model_width), bf16)],
        [pltpu.VMEM((full_rows, 3 * width), f32)],
        3 << 30,
        *normed_parts, w_qkv, w_out, *tables, marks_row, marks_col,
    )
    points[1](far_term)
    resid_mid = inputs + scatter_parts(near_term, far_term)
    points[2](resid_mid)
    mid_parts = gather_parts(layer_norm(resid_mid, gain_mid).astype(bf16))
    points[3](mid_parts)
    w_up, w_down = weights[2], weights[3]

    def feed(k, part):
        hidden = contract_last(part, w_up)
        local_hidden = hidden.shape[1] // 2
        gelu_in = hidden[:, :local_hidden]
        gate_mult = hidden[:, local_hidden:]
        mixed = gelu_product(gelu_in, gate_mult).astype(bf16)
        return gelu_in, gate_mult, mixed, None if late else times(mixed, w_down).astype(bf16)

    fed = in_turn(feed, mid_parts)
    if late:

        def result(gate):
            held = after_all((fed[0][2], fed[1][2]), gate)
            return [times(mixed, w_down).astype(bf16) for mixed in held]

    else:
        result = resid_mid + scatter_parts(fed[0][3], fed[1][3])
    kept = dict(
        inputs=inputs,
        resid_mid=resid_mid,
        normed=normed_parts,
        queries=queries,
        keys=keys,
        values=values,
        logs=logs,
        attended=attended,
        normed_mid=mid_parts,
        gelu_in=(fed[0][0], fed[1][0]),
        gate_mult=(fed[0][1], fed[1][1]),
        mixed=(fed[0][2], fed[1][2]),
    )
    return (result, kept)


def backward_ffn(grad_result, kept, gain_mid, weights, gate):
    w_up, w_down = weights[2], weights[3]
    grad_parts = after_all(gather_parts(grad_result.astype(bf16)), gate)

    def feed_back(k, part):
        grad_mixed = contract_last(part, w_down)
        unused, pull_gelu = jax.vjp(gelu_product, kept["gelu_in"][k], kept["gate_mult"][k])
        terms = tuple(term.astype(bf16) for term in pull_gelu(grad_mixed))
        return terms[0], terms[1], times(joined(terms, 1), w_up).astype(bf16)

    near, far = in_turn(feed_back, grad_parts)
    grad_normed_mid = scatter_parts(near[2], far[2])
    unused, pull_norm = jax.vjp(layer_norm, kept["resid_mid"], gain_mid)
    grad_resid, grad_gain = pull_norm(grad_normed_mid)

    def weight_grads(gate):
        outer, inner, left, first, second = after_all(
            (grad_parts, kept["mixed"], kept["normed_mid"], (near[0], far[0]), (near[1], far[1])),
            gate,
        )
        outer, inner, left = joined(outer), joined(inner), joined(left)
        first, second = joined(first), joined(second)
        half = inner.shape[1] // 2
        front, back = inner[:, :half], inner[:, half:]
        sent_up, add_up = add_core(lambda core: contract_rows(core(first, second), left))
        sent_down, add_down = add_core(lambda core: contract_rows(core(front, back), outer))

        def pack(gate):
            up, down = add_up(gate), add_down(gate)
            rows = up.shape[0] + down.shape[0]
            blank = jnp.zeros((-rows % 128, up.shape[1]), bf16)
            return joined([up, down, blank])

        return (sent_up, sent_down), pack

    return (grad_result + grad_resid, weight_grads, grad_gain)


def backward_attn(grad_mid, kept, gain_first, weights, allowed, tables, gate, pack):
    w_qkv, w_out = weights[0], weights[1]
    grad_parts = gather_parts(grad_mid.astype(bf16))
    near, far = after_all(grad_parts, gate)
    full_rows, width = kept["queries"].shape
    windowed, marks_row, marks_col = allowed
    grad_projected, near_term, far_term = whole_call(
        functools.partial(attend_back_kernel, windowed),
        [((full_rows, 3 * width), bf16), (near.shape, bf16), (far.shape, bf16)],
        [pltpu.VMEM((full_rows, width), bf16)] + [pltpu.VMEM((full_rows, width), f32)] * 3,
        4 << 30,
        near, far, w_qkv, w_out, *tables, marks_row, marks_col,
        kept["queries"], kept["keys"], kept["values"], kept["logs"],
    )
    packed = pack(grad_projected)
    near_term, far_term = after_all((near_term, far_term), packed)
    grad_normed = scatter_parts(near_term, far_term)
    unused, pull_norm = jax.vjp(layer_norm, kept["inputs"], gain_first)
    grad_resid, grad_gain = pull_norm(grad_normed)

    def gain_before():
        total = 0.0
        for term, normed in zip((near_term, far_term), kept["normed"]):
            total = total + jnp.sum(term.astype(f32) * normed.astype(f32), axis=0)
        return total / gain_first

    def weight_grads(gate, gains):
        outer, inner, left, right = after_all(
            (grad_parts, kept["attended"], kept["normed"], grad_projected), gate
        )
        outer, left = joined(outer), joined(left)
        width = inner.shape[1]
        of_q, of_k, of_v = (right[:, i * width : (i + 1) * width] for i in range(3))
        one = add_core(lambda core: contract_rows(left, core(of_q, of_v)))[1](())
        two = add_core(lambda core: contract_rows(core(left, outer), core(of_k, inner)))[1](())
        extra = jnp.stack(gains).astype(bf16).reshape(-1, width)
        blank = jnp.zeros((-extra.shape[0] % 128, width), bf16)
        return joined([one, two, extra, blank])

    return (grad_mid + grad_resid, weight_grads, grad_gain, gain_before, packed)


def fetch_half(own, after):
    piece = own.shape[0] // 2
    start = lax.axis_index("core") * piece
    return swap_layer(lax.dynamic_slice_in_dim(after_all(own, after), start, piece))


def both_halves(half, after=()):
    half = after_all(half, after)
    return in_order(lax.axis_index("core"), half, swap_core(half))


def by_layer(is_first, own, other):
    return jnp.where(is_first, own, other), jnp.where(is_first, other, own)


def in_order(index, mine, other):
    low = jnp.where(index == 0, mine, other)
    high = jnp.where(index == 0, other, mine)
    return jnp.concatenate([low, high], axis=0)


def add_core(product):
    is_core0 = lax.axis_index("core") == 0
    sent = product(lambda one, two: jnp.where(is_core0, two, one)).astype(bf16)

    def add(gate):
        held = product(lambda one, two: after_all(jnp.where(is_core0, one, two), gate))
        return (held + swap_core(sent).astype(f32)).astype(bf16)

    return sent, add


def reduce_part(grads):
    return lax.psum_scatter(grads, ("zlo", "x"), scatter_dimension=0, tiled=True)


def reduce_part_now(grads):
    pieces = lax.all_to_all(grads, ("zlo", "x"), 0, 0, tiled=True)
    pieces = pieces.reshape(8, -1, pieces.shape[1])
    return jnp.sum(pieces.astype(f32), axis=0).astype(bf16)


def spread_part(part):
    copies = jnp.broadcast_to(part[None], (8,) + part.shape).reshape(-1, part.shape[1])
    return lax.all_to_all(copies, ("zlo", "x"), 0, 0, tiled=True)


def trade_halves(half):
    beside = swap_core(half)
    is_core0 = lax.axis_index("core") == 0
    return jnp.where(is_core0, half, beside), jnp.where(is_core0, beside, half)


def pick_sections(is_first, part_first, part_second):
    own = jnp.where(is_first, part_first, part_second)
    sent = jnp.where(is_first, part_second, part_first)
    return own, sent


def local(tokens, cotangent, lengths, gains, w_qkv, w_out, w_up, w_down):
    section_index = lax.axis_index("section")
    is_first = section_index == 0
    row_count = tokens.shape[1]
    full_rows = row_count * lax.axis_size("tensor")
    start_rows = jnp.where(is_first, tokens[0], tokens[1])
    end_grads = jnp.where(is_first, cotangent[0], cotangent[1])
    start_parts = gather_parts(start_rows)
    gains_other = swap_layer(gains[0])
    gains0 = jnp.where(is_first, gains[0], gains_other)
    gains1 = jnp.where(is_first, gains_other, gains[0])
    start_rows = start_rows.astype(f32)
    own = (
        jnp.transpose(w_qkv[0], (1, 0, 2)).reshape(-1, w_qkv.shape[3]),
        w_out[0],
        jnp.transpose(w_up[0], (1, 2, 0)).reshape(-1, w_up.shape[1]),
        w_down[0],
    )
    half_qkv = fetch_half(own[0], ())
    half_out = fetch_half(own[1], ())
    start_parts, lengths = after_all((start_parts, lengths), (half_qkv, half_out))
    first_parts = in_turn(
        lambda k, part: layer_norm(part.astype(f32), gains0[0]).astype(bf16), start_parts
    )
    qkv0, qkv1 = by_layer(is_first, own[0], both_halves(half_qkv))
    layer0 = [joined(jnp.split(qkv0, 3), 1)]
    layer1 = [joined(jnp.split(qkv1, 3), 1)]
    hidden_width = w_up.shape[3]
    moving = []

    out0, out1 = by_layer(is_first, own[1], both_halves(half_out))
    layer0.append(out0)
    layer1.append(out1)
    moving.append(fetch_half(own[2][:hidden_width], half_out))

    def at_far_term(far_term):
        moving.append(both_halves(moving[0], far_term))
        moving.append(fetch_half(own[2][hidden_width:], (moving[0], far_term)))

    def at_mid(resid_mid):
        moving.append(both_halves(moving[2], resid_mid))
        moving.append(fetch_half(own[3], (moving[2], resid_mid)))

    def at_gathered(parts):
        up0, up1 = by_layer(is_first, own[2], joined([moving[1], moving[3]]))
        down0, down1 = by_layer(is_first, own[3], both_halves(moving[4], parts))
        layer0.extend([up0, down0])
        layer1.extend([up1, down1])

    points = (None, at_far_term, at_mid, at_gathered)

    doc_lengths = jnp.where(is_first, lengths[0, 0], lengths[1, 0])
    indices = jnp.arange(full_rows, dtype=jnp.int32)
    blocks = jnp.array([0, 1, 3, 2], jnp.int32) + lax.axis_index("tensor")
    indices = (jnp.repeat(blocks, row_count) * row_count + indices % row_count) % full_rows
    doc_ids, positions = doc_layout(doc_lengths, indices)
    marks_row = jnp.stack([doc_ids, indices])
    marks_col = jnp.stack([doc_ids, indices], axis=1)
    allowed0 = (True, marks_row, marks_col)
    allowed1 = (False, marks_row, marks_col)
    heads = w_out.shape[1] // HEAD_DIM
    tables0 = rope_tables(positions, 10000.0, heads)
    tables1 = rope_tables(positions, 160000.0, heads)

    out0, kept0 = forward_layer(
        start_rows, first_parts, gains0[1], layer0, allowed0, tables0, False, points
    )
    out0 = out0.astype(bf16)
    second_rows = out0.astype(f32)
    second_parts = gather_parts(layer_norm(second_rows, gains1[0]).astype(bf16))
    out1_of, kept1 = forward_layer(
        second_rows, second_parts, gains1[1], layer1, allowed1, tables1, True, (lambda value: None,) * 4
    )
    mid1, ffn_grads1, gain_mid1 = backward_ffn(
        end_grads.astype(f32), kept1, gains1[1], layer1, ()
    )
    ffn_sent1, ffn_pack1 = ffn_grads1(mid1)
    in1, attn_grads1, gain_first1, unused, unused = backward_attn(
        mid1, kept1, gains1[0], layer1, allowed1, tables1, ffn_sent1, lambda gate: ()
    )
    in1 = in1.astype(bf16)
    ffn_pack1 = ffn_pack1(in1)
    mid0, ffn_grads0, gain_mid0 = backward_ffn(
        in1.astype(f32), kept0, gains0[1], layer0, ffn_pack1
    )
    ffn1 = reduce_part(ffn_pack1)
    mid0 = after_all(mid0, ffn1)
    ffn_sent0, ffn_pack0 = ffn_grads0(mid0)
    in0, attn_grads0, unused, gain_before, ffn_pack0 = backward_attn(
        mid0, kept0, gains0[0], layer0, allowed0, tables0, ffn_sent0, ffn_pack0
    )
    in0 = in0.astype(bf16)
    ffn0 = reduce_part(ffn_pack0)
    attn_pack1 = attn_grads1(in1, [gain_first1, gain_mid1])
    attn_pack0 = attn_grads0((), [gain_before(), gain_mid0])
    packs = [pack.reshape(8, -1, pack.shape[1]) for pack in (attn_pack0, attn_pack1)]
    attn_rows = packs[0].shape[1]
    attn_both = joined(packs, 1).reshape(-1, attn_pack0.shape[1])
    out1_terms = out1_of(attn_both)
    attn_both = reduce_part_now(attn_both)
    out1 = (kept1["resid_mid"] + scatter_parts(*out1_terms)).astype(bf16)
    ffn_own, ffn_sent = pick_sections(is_first, ffn0, ffn1)
    attn_own, attn_sent = pick_sections(is_first, attn_both[:attn_rows], attn_both[attn_rows:])
    model_width = w_qkv.shape[1]
    own_part = joined([ffn_own, attn_own.reshape(-1, model_width)])
    sent_part = joined([ffn_sent, attn_sent.reshape(-1, model_width)])
    part = (own_part.astype(f32) + swap_section(sent_part).astype(f32)).astype(bf16)
    ffn_rows = ffn0.shape[0]
    part_rows = part.shape[0]
    part = joined([part, jnp.zeros((-part_rows % 16, model_width), bf16)])
    halves = [
        half.reshape(8, -1, model_width) for half in trade_halves(spread_part(part))
    ]
    ffn_halves = [half[:, :ffn_rows].reshape(-1, model_width) for half in halves]
    attn_halves = [
        half[:, ffn_rows:part_rows].reshape(-1, attn_pack0.shape[1]) for half in halves
    ]
    grad_up = jnp.stack([half[:hidden_width] for half in ffn_halves]).astype(f32)
    down_rows = w_down.shape[1] // 2
    grad_down = joined([half[hidden_width : hidden_width + down_rows] for half in ffn_halves])
    grad_down = grad_down.astype(f32)
    gain_rows = sum(half[2 * w_qkv.shape[1] :][:8].astype(f32) for half in attn_halves)
    gain_total = sum_tensor(gain_rows).reshape(2, -1)
    grad_qkv = jnp.stack(
        [
            attn_halves[0][:model_width],
            attn_halves[0][model_width : 2 * model_width],
            attn_halves[1][:model_width],
        ]
    )
    grad_out = attn_halves[1][model_width : 2 * model_width].T

    got_out = swap_section(jnp.where(is_first, out1, out0))
    section_out = jnp.stack(
        [jnp.where(is_first, out0, got_out), jnp.where(is_first, got_out, out1)]
    )
    got_in = swap_section(jnp.where(is_first, in1, in0))
    input_grads = jnp.stack(
        [jnp.where(is_first, in0, got_in), jnp.where(is_first, got_in, in1)]
    )
    return (
        section_out[None],
        input_grads[None],
        gain_total[None],
        jnp.transpose(grad_qkv.astype(f32), (1, 0, 2))[None],
        grad_out.astype(f32)[None],
        jnp.transpose(grad_up, (2, 0, 1))[None],
        grad_down[None],
    )


def solution(mesh):
    sizes = dict(zip(mesh.axis_names, mesh.devices.shape))
    fine = Mesh(
        mesh.devices.reshape(sizes["section"], 2, sizes["dp"] // 4, 2, sizes["tensor"]),
        ("section", "zlo", "x", "core", "tensor"),
    )
    rows = ("zlo", "x", "core", "tensor")
    in_specs = (
        P(None, rows, None),
        P(None, rows, None),
        P(None, DP, None),
        P("section", None, None),
        P("section", None, None, "tensor"),
        P("section", "tensor", None),
        P("section", None, None, "tensor"),
        P("section", "tensor", None),
    )
    out_specs = (
        P("section", None, rows, None),
        P("section", None, rows, None),
        P("section", None, None),
        P("section", None, None, "tensor"),
        P("section", "tensor", None),
        P("section", None, None, "tensor"),
        P("section", "tensor", None),
    )
    return jax.shard_map(local, mesh=fine, in_specs=in_specs, out_specs=out_specs, check_vma=False)
```

```python
import functools

import jax
import jax.numpy as jnp
from jax import lax
from jax.experimental import pallas as pl
from jax.experimental.pallas import tpu as pltpu
from jax.sharding import Mesh
from jax.sharding import PartitionSpec as P

HEAD_DIM = 64
WINDOW = 128

epsilon = 1e-05
bf16 = jnp.bfloat16
f32 = jnp.float32

BLOCK = 256

DP = ("zlo", "x", "core")


def around(block, axis, distance):
    count = lax.axis_size(axis)
    return lax.ppermute(block, axis, [(i, (i + distance) % count) for i in range(count)])


def swap_core(block):
    return lax.ppermute(block, "core", [(0, 1), (1, 0)])


def swap_section(block):
    return lax.ppermute(block, "section", [(0, 1), (1, 0)])


def swap_layer(block):
    return lax.ppermute(block, ("section", "zlo"), [(0, 3), (1, 2), (2, 1), (3, 0)])


def gather_parts(block):
    far = around(block, "tensor", 2)
    ahead = around(block, "tensor", -1)
    behind = around(block, "tensor", 1)
    return [joined([block, ahead, behind]), far]


def scatter_parts(near, far):
    rows = far.shape[0]
    sent_far = around(far.astype(bf16), "tensor", 2)
    sent_ahead = around(near[rows : 2 * rows].astype(bf16), "tensor", 1)
    sent_behind = around(near[2 * rows :].astype(bf16), "tensor", -1)
    kept = near[:rows].astype(f32)
    return kept + sent_far.astype(f32) + sent_ahead.astype(f32) + sent_behind.astype(f32)


def joined(parts, axis=0):
    return jnp.concatenate(parts, axis=axis)


def after_all(values, *others):
    return lax.optimization_barrier((values,) + others)[0]


def sum_tensor(block):
    return (
        block
        + around(block, "tensor", 2)
        + around(block, "tensor", 1)
        + around(block, "tensor", -1)
    )


def layer_norm(values, gain_scale):
    centered = values - jnp.mean(values, axis=-1, keepdims=True)
    variance = jnp.mean(centered * centered, axis=-1, keepdims=True)
    return centered * lax.rsqrt(variance + epsilon) * gain_scale


def doc_layout(doc_lengths, indices):
    doc_ends = jnp.cumsum(doc_lengths)
    passed = indices[:, None] >= doc_ends[None, :]
    doc_ids = jnp.sum(passed.astype(jnp.int32), axis=1)
    starts = jnp.sum(jnp.where(passed, doc_lengths[None, :], 0), axis=1)
    return (doc_ids, indices - starts)


def rope_tables(positions, rope_base, heads):
    half_dim = HEAD_DIM // 2
    inverse = rope_base ** (-2.0 * jnp.arange(half_dim, dtype=f32) / HEAD_DIM)
    angles = positions.astype(f32)[:, None] * inverse
    cosine, sine = jnp.cos(angles), jnp.sin(angles)
    cosine = jnp.concatenate([cosine, cosine], axis=-1)
    sine = jnp.concatenate([-sine, sine], axis=-1)
    return (jnp.tile(cosine, (1, heads)), jnp.tile(sine, (1, heads)))


def contract_rows(left_rows, right_rows):
    return lax.dot_general(
        left_rows, right_rows, (((0,), (0,)), ((), ())), preferred_element_type=f32
    )


def contract_last(left_rows, weight):
    return lax.dot_general(
        left_rows, weight, (((1,), (1,)), ((), ())), preferred_element_type=f32
    )


def times(left_rows, weight):
    return jnp.dot(left_rows, weight, preferred_element_type=f32)


def gelu_product(first_half, second_half):
    return jax.nn.gelu(first_half, approximate=False) * second_half


def dot_nt(left, right):
    return lax.dot_general(left, right, (((1,), (1,)), ((), ())), preferred_element_type=f32)


def dot_tn(left, right):
    return lax.dot_general(left, right, (((0,), (0,)), ((), ())), preferred_element_type=f32)


def swap_halves(values):
    width = values.shape[1]
    lanes = lax.broadcasted_iota(jnp.int32, values.shape, 1)
    up = pltpu.roll(values, width - HEAD_DIM // 2, 1)
    down = pltpu.roll(values, HEAD_DIM // 2, 1)
    return jnp.where(lanes % HEAD_DIM < HEAD_DIM // 2, up, down)


def excluded_bias(marks_row, marks_col, start, windowed):
    docs = marks_row[0:1, pl.ds(start, BLOCK)]
    allowed = marks_col[:, 0:1] == docs
    if windowed:
        apart = marks_col[:, 1:2] - marks_row[1:2, pl.ds(start, BLOCK)]
        allowed = allowed & (jnp.abs(apart) <= WINDOW // 2)
    return jnp.where(allowed, 0.0, -1e30)


def attend_kernel(
    windowed,
    near, far, w_qkv, w_out, cosine, sine, marks_row, marks_col,
    queries, keys, values, logs, attended, near_term, far_term,
    projected,
):
    near_rows = near.shape[0]
    width = w_out.shape[0]
    projected[:near_rows] = jnp.dot(near[...], w_qkv[...], preferred_element_type=f32)
    projected[near_rows:] = jnp.dot(far[...], w_qkv[...], preferred_element_type=f32)
    for index, target in ((0, queries), (1, keys)):
        part = projected[:, index * width : (index + 1) * width]
        turned = part * cosine[...] + swap_halves(part) * sine[...]
        target[...] = turned.astype(bf16)
    values[...] = projected[:, 2 * width :].astype(bf16)
    heads = width // HEAD_DIM
    lanes = lax.broadcasted_iota(jnp.int32, (BLOCK, width), 1) // HEAD_DIM

    def step(index, carry):
        start = pl.multiple_of(index * BLOCK, BLOCK)
        bias = excluded_bias(marks_row, marks_col, start, windowed)
        block = queries[pl.ds(start, BLOCK)] * jnp.asarray(HEAD_DIM ** (-0.5), bf16)
        total = jnp.zeros((BLOCK, width), f32)
        for head in range(heads):
            own = jnp.where(lanes == head, block, jnp.zeros_like(block))
            scores = dot_nt(keys[...], own) + bias
            largest = jnp.max(scores, axis=0, keepdims=True)
            powers = jnp.exp(scores - largest)
            sums = jnp.sum(powers, axis=0, keepdims=True)
            soft = (powers * (1.0 / sums)).astype(bf16)
            logs[pl.ds(head, 1), pl.ds(start, BLOCK)] = largest + jnp.log(sums)
            total = jnp.where(lanes == head, dot_tn(soft, values[...]), total)
        attended[pl.ds(start, BLOCK)] = total.astype(bf16)
        return carry

    lax.fori_loop(0, queries.shape[0] // BLOCK, step, 0)
    far_term[...] = jnp.dot(
        attended[near_rows:], w_out[...], preferred_element_type=f32
    ).astype(bf16)
    near_term[...] = jnp.dot(
        attended[:near_rows], w_out[...], preferred_element_type=f32
    ).astype(bf16)


def attend_back_kernel(
    windowed,
    near, far, w_qkv, w_out, cosine, sine, marks_row, marks_col,
    queries, keys, values, logs,
    grad_projected, near_term, far_term,
    grad_attended, grad_queries, grad_keys, grad_values,
):
    near_rows = near.shape[0]
    width = w_out.shape[0]
    grad_attended[:near_rows] = dot_nt(near[...], w_out[...]).astype(bf16)
    grad_attended[near_rows:] = dot_nt(far[...], w_out[...]).astype(bf16)
    grad_keys[...] = jnp.zeros_like(grad_keys)
    grad_values[...] = jnp.zeros_like(grad_values)
    heads = width // HEAD_DIM
    lanes = lax.broadcasted_iota(jnp.int32, (BLOCK, width), 1) // HEAD_DIM
    all_lanes = lax.broadcasted_iota(jnp.int32, queries.shape, 1) // HEAD_DIM

    def step(index, carry):
        start = pl.multiple_of(index * BLOCK, BLOCK)
        bias = excluded_bias(marks_row, marks_col, start, windowed)
        block = queries[pl.ds(start, BLOCK)] * jnp.asarray(HEAD_DIM ** (-0.5), bf16)
        grad_block = grad_attended[pl.ds(start, BLOCK)]
        total = jnp.zeros((BLOCK, width), f32)
        more_keys = jnp.zeros(queries.shape, f32)
        more_values = jnp.zeros(queries.shape, f32)
        for head in range(heads):
            own = jnp.where(lanes == head, block, jnp.zeros_like(block))
            own_grad = jnp.where(lanes == head, grad_block, jnp.zeros_like(grad_block))
            scores = dot_nt(keys[...], own) + bias
            soft = jnp.exp(scores - logs[pl.ds(head, 1), pl.ds(start, BLOCK)])
            grad_soft = dot_nt(values[...], own_grad)
            dots = jnp.sum(soft * grad_soft, axis=0, keepdims=True)
            grad_scores = (soft * (grad_soft - dots)).astype(bf16)
            more_values += jnp.dot(soft.astype(bf16), own_grad, preferred_element_type=f32)
            more_keys += jnp.dot(grad_scores, own, preferred_element_type=f32)
            total = jnp.where(lanes == head, dot_tn(grad_scores, keys[...]), total)
        grad_queries[pl.ds(start, BLOCK)] = total * HEAD_DIM ** (-0.5)
        grad_keys[...] += more_keys
        grad_values[...] += more_values
        return carry

    lax.fori_loop(0, queries.shape[0] // BLOCK, step, 0)
    for index, source in ((0, grad_queries), (1, grad_keys)):
        part = source[...]
        back = part * cosine[...] - swap_halves(part) * sine[...]
        grad_projected[:, index * width : (index + 1) * width] = back.astype(bf16)
    grad_projected[:, 2 * width :] = grad_values[...].astype(bf16)
    far_term[...] = dot_nt(grad_projected[near_rows:], w_qkv[...]).astype(bf16)
    near_term[...] = dot_nt(grad_projected[:near_rows], w_qkv[...]).astype(bf16)


def whole_call(kernel, out_shapes, scratch_shapes, flops, *operands):
    whole = pl.BlockSpec(memory_space=pltpu.VMEM)
    return pl.pallas_call(
        kernel,
        out_shape=[jax.ShapeDtypeStruct(*shape) for shape in out_shapes],
        in_specs=[whole] * len(operands),
        out_specs=[whole] * len(out_shapes),
        scratch_shapes=scratch_shapes,
        compiler_params=pltpu.CompilerParams(vmem_limit_bytes=40 * 1024 * 1024),
        cost_estimate=pl.CostEstimate(flops=flops, bytes_accessed=8 << 20, transcendentals=1 << 20),
    )(*operands)


def in_turn(work, parts):
    first = work(0, parts[0])
    return first, work(1, after_all(parts[1], first))


def forward_layer(inputs, normed_parts, gain_mid, weights, allowed, tables, late, points):
    w_qkv, w_out = weights[0], weights[1]
    near_rows, model_width = normed_parts[0].shape
    far_rows = normed_parts[1].shape[0]
    full_rows = near_rows + far_rows
    width = w_out.shape[0]
    windowed, marks_row, marks_col = allowed
    queries, keys, values, logs, attended, near_term, far_term = whole_call(
        functools.partial(attend_kernel, windowed),
        [((full_rows, width), bf16)] * 3
        + [((8, full_rows), f32), ((full_rows, width), bf16)]
        + [((near_rows, model_width), bf16), ((far_rows, model_width), bf16)],
        [pltpu.VMEM((full_rows, 3 * width), f32)],
        3 << 30,
        *normed_parts, w_qkv, w_out, *tables, marks_row, marks_col,
    )
    points[1](far_term)
    resid_mid = inputs + scatter_parts(near_term, far_term)
    points[2](resid_mid)
    mid_parts = gather_parts(layer_norm(resid_mid, gain_mid).astype(bf16))
    points[3](mid_parts)
    w_up, w_down = weights[2], weights[3]

    def feed(k, part):
        hidden = contract_last(part, w_up)
        local_hidden = hidden.shape[1] // 2
        gelu_in = hidden[:, :local_hidden]
        gate_mult = hidden[:, local_hidden:]
        mixed = gelu_product(gelu_in, gate_mult).astype(bf16)
        return gelu_in, gate_mult, mixed, None if late else times(mixed, w_down).astype(bf16)

    fed = in_turn(feed, mid_parts)
    if late:

        def result(gate):
            held = after_all((fed[0][2], fed[1][2]), gate)
            return [times(mixed, w_down).astype(bf16) for mixed in held]

    else:
        result = resid_mid + scatter_parts(fed[0][3], fed[1][3])
    kept = dict(
        inputs=inputs,
        resid_mid=resid_mid,
        normed=normed_parts,
        queries=queries,
        keys=keys,
        values=values,
        logs=logs,
        attended=attended,
        normed_mid=mid_parts,
        gelu_in=(fed[0][0], fed[1][0]),
        gate_mult=(fed[0][1], fed[1][1]),
        mixed=(fed[0][2], fed[1][2]),
    )
    return (result, kept)


def backward_ffn(grad_result, kept, gain_mid, weights, gate):
    w_up, w_down = weights[2], weights[3]
    grad_parts = after_all(gather_parts(grad_result.astype(bf16)), gate)

    def feed_back(k, part):
        grad_mixed = contract_last(part, w_down)
        unused, pull_gelu = jax.vjp(gelu_product, kept["gelu_in"][k], kept["gate_mult"][k])
        terms = tuple(term.astype(bf16) for term in pull_gelu(grad_mixed))
        return terms[0], terms[1], times(joined(terms, 1), w_up).astype(bf16)

    near, far = in_turn(feed_back, grad_parts)
    grad_normed_mid = scatter_parts(near[2], far[2])
    unused, pull_norm = jax.vjp(layer_norm, kept["resid_mid"], gain_mid)
    grad_resid, grad_gain = pull_norm(grad_normed_mid)

    def weight_grads(gate):
        outer, inner, left, first, second = after_all(
            (grad_parts, kept["mixed"], kept["normed_mid"], (near[0], far[0]), (near[1], far[1])),
            gate,
        )
        outer, inner, left = joined(outer), joined(inner), joined(left)
        first, second = joined(first), joined(second)
        half = inner.shape[1] // 2
        front, back = inner[:, :half], inner[:, half:]
        sent_up, add_up = add_core(lambda core: contract_rows(core(first, second), left))
        sent_down, add_down = add_core(lambda core: contract_rows(core(front, back), outer))

        def pack(gate):
            up, down = add_up(gate), add_down(gate)
            rows = up.shape[0] + down.shape[0]
            blank = jnp.zeros((-rows % 128, up.shape[1]), bf16)
            return joined([up, down, blank])

        return (sent_up, sent_down), pack

    return (grad_result + grad_resid, weight_grads, grad_gain)


def backward_attn(grad_mid, kept, gain_first, weights, allowed, tables, gate, pack):
    w_qkv, w_out = weights[0], weights[1]
    grad_parts = gather_parts(grad_mid.astype(bf16))
    near, far = after_all(grad_parts, gate)
    full_rows, width = kept["queries"].shape
    windowed, marks_row, marks_col = allowed
    grad_projected, near_term, far_term = whole_call(
        functools.partial(attend_back_kernel, windowed),
        [((full_rows, 3 * width), bf16), (near.shape, bf16), (far.shape, bf16)],
        [pltpu.VMEM((full_rows, width), bf16)] + [pltpu.VMEM((full_rows, width), f32)] * 3,
        4 << 30,
        near, far, w_qkv, w_out, *tables, marks_row, marks_col,
        kept["queries"], kept["keys"], kept["values"], kept["logs"],
    )
    packed = pack(grad_projected)
    near_term, far_term = after_all((near_term, far_term), packed)
    grad_normed = scatter_parts(near_term, far_term)
    unused, pull_norm = jax.vjp(layer_norm, kept["inputs"], gain_first)
    grad_resid, grad_gain = pull_norm(grad_normed)

    def gain_before():
        total = 0.0
        for term, normed in zip((near_term, far_term), kept["normed"]):
            total = total + jnp.sum(term.astype(f32) * normed.astype(f32), axis=0)
        return total / gain_first

    def weight_grads(gate, gains):
        outer, inner, left, right = after_all(
            (grad_parts, kept["attended"], kept["normed"], grad_projected), gate
        )
        outer, left = joined(outer), joined(left)
        width = inner.shape[1]
        of_q, of_k, of_v = (right[:, i * width : (i + 1) * width] for i in range(3))
        one = add_core(lambda core: contract_rows(left, core(of_q, of_v)))[1](())
        two = add_core(lambda core: contract_rows(core(left, outer), core(of_k, inner)))[1](())
        extra = jnp.stack(gains).astype(bf16).reshape(-1, width)
        blank = jnp.zeros((-extra.shape[0] % 128, width), bf16)
        return joined([one, two, extra, blank])

    return (grad_mid + grad_resid, weight_grads, grad_gain, gain_before, packed)


def fetch_half(own, after):
    piece = own.shape[0] // 2
    start = lax.axis_index("core") * piece
    return swap_layer(lax.dynamic_slice_in_dim(after_all(own, after), start, piece))


def both_halves(half, after=()):
    half = after_all(half, after)
    return in_order(lax.axis_index("core"), half, swap_core(half))


def by_layer(is_first, own, other):
    return jnp.where(is_first, own, other), jnp.where(is_first, other, own)


def in_order(index, mine, other):
    low = jnp.where(index == 0, mine, other)
    high = jnp.where(index == 0, other, mine)
    return jnp.concatenate([low, high], axis=0)


def add_core(product):
    is_core0 = lax.axis_index("core") == 0
    sent = product(lambda one, two: jnp.where(is_core0, two, one)).astype(bf16)

    def add(gate):
        held = product(lambda one, two: after_all(jnp.where(is_core0, one, two), gate))
        return (held + swap_core(sent).astype(f32)).astype(bf16)

    return sent, add


def reduce_part(grads):
    return lax.psum_scatter(grads, ("zlo", "x"), scatter_dimension=0, tiled=True)


def reduce_part_now(grads):
    pieces = lax.all_to_all(grads, ("zlo", "x"), 0, 0, tiled=True)
    pieces = pieces.reshape(8, -1, pieces.shape[1])
    return jnp.sum(pieces.astype(f32), axis=0).astype(bf16)


def spread_part(part):
    copies = jnp.broadcast_to(part[None], (8,) + part.shape).reshape(-1, part.shape[1])
    return lax.all_to_all(copies, ("zlo", "x"), 0, 0, tiled=True)


def pick_sections(is_first, part_first, part_second):
    own = jnp.where(is_first, part_first, part_second)
    sent = jnp.where(is_first, part_second, part_first)
    return own, sent


def local(tokens, cotangent, lengths, gains, w_qkv, w_out, w_up, w_down):
    section_index = lax.axis_index("section")
    is_first = section_index == 0
    row_count = tokens.shape[1]
    full_rows = row_count * lax.axis_size("tensor")
    start_rows = jnp.where(is_first, tokens[0], tokens[1])
    end_grads = jnp.where(is_first, cotangent[0], cotangent[1])
    start_parts = gather_parts(start_rows)
    gains_other = swap_layer(gains[0])
    gains0 = jnp.where(is_first, gains[0], gains_other)
    gains1 = jnp.where(is_first, gains_other, gains[0])
    start_rows = start_rows.astype(f32)
    own = (
        jnp.transpose(w_qkv[0], (1, 0, 2)).reshape(-1, w_qkv.shape[3]),
        w_out[0],
        jnp.transpose(w_up[0], (1, 2, 0)).reshape(-1, w_up.shape[1]),
        w_down[0],
    )
    half_qkv = fetch_half(own[0], ())
    half_out = fetch_half(own[1], ())
    start_parts, lengths = after_all((start_parts, lengths), (half_qkv, half_out))
    first_parts = in_turn(
        lambda k, part: layer_norm(part.astype(f32), gains0[0]).astype(bf16), start_parts
    )
    qkv0, qkv1 = by_layer(is_first, own[0], both_halves(half_qkv))
    layer0 = [joined(jnp.split(qkv0, 3), 1)]
    layer1 = [joined(jnp.split(qkv1, 3), 1)]
    hidden_width = w_up.shape[3]
    moving = []

    out0, out1 = by_layer(is_first, own[1], both_halves(half_out))
    layer0.append(out0)
    layer1.append(out1)
    moving.append(fetch_half(own[2][:hidden_width], half_out))

    def at_far_term(far_term):
        moving.append(both_halves(moving[0], far_term))
        moving.append(fetch_half(own[2][hidden_width:], (moving[0], far_term)))

    def at_mid(resid_mid):
        moving.append(both_halves(moving[2], resid_mid))
        moving.append(fetch_half(own[3], (moving[2], resid_mid)))

    def at_gathered(parts):
        up0, up1 = by_layer(is_first, own[2], joined([moving[1], moving[3]]))
        down0, down1 = by_layer(is_first, own[3], both_halves(moving[4], parts))
        layer0.extend([up0, down0])
        layer1.extend([up1, down1])

    points = (None, at_far_term, at_mid, at_gathered)

    doc_lengths = jnp.where(is_first, lengths[0, 0], lengths[1, 0])
    indices = jnp.arange(full_rows, dtype=jnp.int32)
    blocks = jnp.array([0, 1, 3, 2], jnp.int32) + lax.axis_index("tensor")
    indices = (jnp.repeat(blocks, row_count) * row_count + indices % row_count) % full_rows
    doc_ids, positions = doc_layout(doc_lengths, indices)
    marks_row = jnp.stack([doc_ids, indices])
    marks_col = jnp.stack([doc_ids, indices], axis=1)
    allowed0 = (True, marks_row, marks_col)
    allowed1 = (False, marks_row, marks_col)
    heads = w_out.shape[1] // HEAD_DIM
    tables0 = rope_tables(positions, 10000.0, heads)
    tables1 = rope_tables(positions, 160000.0, heads)

    out0, kept0 = forward_layer(
        start_rows, first_parts, gains0[1], layer0, allowed0, tables0, False, points
    )
    out0 = out0.astype(bf16)
    second_rows = out0.astype(f32)
    second_parts = gather_parts(layer_norm(second_rows, gains1[0]).astype(bf16))
    out1_of, kept1 = forward_layer(
        second_rows, second_parts, gains1[1], layer1, allowed1, tables1, True, (lambda value: None,) * 4
    )
    mid1, ffn_grads1, gain_mid1 = backward_ffn(
        end_grads.astype(f32), kept1, gains1[1], layer1, ()
    )
    ffn_sent1, ffn_pack1 = ffn_grads1(mid1)
    in1, attn_grads1, gain_first1, unused, unused = backward_attn(
        mid1, kept1, gains1[0], layer1, allowed1, tables1, ffn_sent1, lambda gate: ()
    )
    in1 = in1.astype(bf16)
    ffn_pack1 = ffn_pack1(in1)
    mid0, ffn_grads0, gain_mid0 = backward_ffn(
        in1.astype(f32), kept0, gains0[1], layer0, ffn_pack1
    )
    model_width = w_qkv.shape[1]
    attn_pack1 = attn_grads1(in1, [gain_first1, gain_mid1])
    attn_width = attn_pack1.shape[1]
    pieces = [pack.reshape(8, -1, model_width) for pack in (ffn_pack1, attn_pack1)]
    ffn_rows, attn_rows = pieces[0].shape[1], pieces[1].shape[1]
    part_rows = ffn_rows + attn_rows
    blank = jnp.zeros((8, -part_rows % 16, model_width), bf16)
    part1 = reduce_part(joined(pieces + [blank], 1).reshape(-1, model_width))
    ffn_pack0 = ffn_grads0(mid0)[1](())
    in0, attn_grads0, unused, gain_before, unused = backward_attn(
        mid0, kept0, gains0[0], layer0, allowed0, tables0, (ffn_pack0, part1), lambda gate: ()
    )
    in0 = in0.astype(bf16)
    ffn0 = reduce_part(ffn_pack0)
    attn_pack0 = attn_grads0((), [gain_before(), gain_mid0])
    out1_terms = out1_of(ffn_pack0)
    out1 = (kept1["resid_mid"] + scatter_parts(*out1_terms)).astype(bf16)
    attn0 = reduce_part_now(attn_pack0)
    part0 = joined([ffn0, attn0.reshape(-1, model_width)])
    own_part, sent_part = pick_sections(is_first, part0, part1[:part_rows])
    sent_part = after_all(sent_part, in0, out1)
    part = (own_part.astype(f32) + swap_section(sent_part).astype(f32)).astype(bf16)
    part = joined([part, jnp.zeros((-part_rows % 16, model_width), bf16)])
    half = spread_part(part)
    halves = [both.reshape(8, -1, model_width) for both in (half, swap_core(half))]
    is_core0 = lax.axis_index("core") == 0

    def of_core(core, first_row, rows, width, start, count):
        mine, other = (
            both[:, first_row : first_row + rows].reshape(-1, width)[start : start + count]
            for both in halves
        )
        return jnp.where(is_core0 == (core == 0), mine, other).astype(f32)

    def of_ffn(core, start, count):
        return of_core(core, 0, ffn_rows, model_width, start, count)

    def of_attn(core, start, count):
        return of_core(core, ffn_rows, attn_rows, attn_width, start, count)

    down_rows = w_down.shape[1] // 2
    grad_up = jnp.stack([of_ffn(core, 0, hidden_width) for core in range(2)])
    grad_down = joined([of_ffn(core, hidden_width, down_rows) for core in range(2)])
    gain_rows = sum(of_attn(core, 2 * model_width, 8) for core in range(2))
    gain_total = sum_tensor(gain_rows).reshape(2, -1)
    grad_qkv = jnp.stack(
        [
            of_attn(0, 0, model_width),
            of_attn(0, model_width, model_width),
            of_attn(1, 0, model_width),
        ]
    )
    grad_out = of_attn(1, model_width, model_width).T
    got_out = swap_section(jnp.where(is_first, out1, out0))
    got_out, got_in_sent = after_all((got_out, jnp.where(is_first, in1, in0)), half)
    section_out = jnp.stack(
        [jnp.where(is_first, out0, got_out), jnp.where(is_first, got_out, out1)]
    )
    got_in = swap_section(got_in_sent)
    input_grads = jnp.stack(
        [jnp.where(is_first, in0, got_in), jnp.where(is_first, got_in, in1)]
    )
    return (
        section_out[None],
        input_grads[None],
        gain_total[None],
        jnp.transpose(grad_qkv, (1, 0, 2))[None],
        grad_out[None],
        jnp.transpose(grad_up, (2, 0, 1))[None],
        grad_down[None],
    )


def solution(mesh):
    sizes = dict(zip(mesh.axis_names, mesh.devices.shape))
    fine = Mesh(
        mesh.devices.reshape(sizes["section"], 2, sizes["dp"] // 4, 2, sizes["tensor"]),
        ("section", "zlo", "x", "core", "tensor"),
    )
    rows = ("zlo", "x", "core", "tensor")
    in_specs = (
        P(None, rows, None),
        P(None, rows, None),
        P(None, DP, None),
        P("section", None, None),
        P("section", None, None, "tensor"),
        P("section", "tensor", None),
        P("section", None, None, "tensor"),
        P("section", "tensor", None),
    )
    out_specs = (
        P("section", None, rows, None),
        P("section", None, rows, None),
        P("section", None, None),
        P("section", None, None, "tensor"),
        P("section", "tensor", None),
        P("section", None, None, "tensor"),
        P("section", "tensor", None),
    )
    return jax.shard_map(local, mesh=fine, in_specs=in_specs, out_specs=out_specs, check_vma=False)
```

```python
import functools

import jax
import jax.numpy as jnp
from jax import lax
from jax.experimental import pallas as pl
from jax.experimental.pallas import tpu as pltpu
from jax.sharding import Mesh
from jax.sharding import PartitionSpec as P

HEAD_DIM = 64
WINDOW = 128

epsilon = 1e-05
bf16 = jnp.bfloat16
f32 = jnp.float32

BLOCK = 256

DP = ("zlo", "x", "core")


def around(block, axis, distance):
    count = lax.axis_size(axis)
    return lax.ppermute(block, axis, [(i, (i + distance) % count) for i in range(count)])


def swap_core(block):
    return lax.ppermute(block, "core", [(0, 1), (1, 0)])


def swap_section(block):
    return lax.ppermute(block, "section", [(0, 1), (1, 0)])


def swap_layer(block):
    return lax.ppermute(block, ("section", "zlo"), [(0, 3), (1, 2), (2, 1), (3, 0)])


def gather_parts(block):
    far = around(block, "tensor", 2)
    ahead = around(block, "tensor", -1)
    behind = around(block, "tensor", 1)
    return [joined([block, ahead, behind]), far]


def scatter_parts(near, far):
    rows = far.shape[0]
    sent_far = around(far.astype(bf16), "tensor", 2)
    sent_ahead = around(near[rows : 2 * rows].astype(bf16), "tensor", 1)
    sent_behind = around(near[2 * rows :].astype(bf16), "tensor", -1)
    kept = near[:rows].astype(f32)
    return kept + sent_far.astype(f32) + sent_ahead.astype(f32) + sent_behind.astype(f32)


def joined(parts, axis=0):
    return jnp.concatenate(parts, axis=axis)


def after_all(values, *others):
    return lax.optimization_barrier((values,) + others)[0]


def sum_tensor(block):
    return (
        block
        + around(block, "tensor", 2)
        + around(block, "tensor", 1)
        + around(block, "tensor", -1)
    )


def layer_norm(values, gain_scale):
    centered = values - jnp.mean(values, axis=-1, keepdims=True)
    variance = jnp.mean(centered * centered, axis=-1, keepdims=True)
    return centered * lax.rsqrt(variance + epsilon) * gain_scale


def doc_layout(doc_lengths, indices):
    doc_ends = jnp.cumsum(doc_lengths)
    passed = indices[:, None] >= doc_ends[None, :]
    doc_ids = jnp.sum(passed.astype(jnp.int32), axis=1)
    starts = jnp.sum(jnp.where(passed, doc_lengths[None, :], 0), axis=1)
    return (doc_ids, indices - starts)


def rope_tables(positions, rope_base, heads):
    half_dim = HEAD_DIM // 2
    inverse = rope_base ** (-2.0 * jnp.arange(half_dim, dtype=f32) / HEAD_DIM)
    angles = positions.astype(f32)[:, None] * inverse
    cosine, sine = jnp.cos(angles), jnp.sin(angles)
    cosine = jnp.concatenate([cosine, cosine], axis=-1)
    sine = jnp.concatenate([-sine, sine], axis=-1)
    return (jnp.tile(cosine, (1, heads)), jnp.tile(sine, (1, heads)))


def contract_rows(left_rows, right_rows):
    return lax.dot_general(
        left_rows, right_rows, (((0,), (0,)), ((), ())), preferred_element_type=f32
    )


def contract_last(left_rows, weight):
    return lax.dot_general(
        left_rows, weight, (((1,), (1,)), ((), ())), preferred_element_type=f32
    )


def times(left_rows, weight):
    return jnp.dot(left_rows, weight, preferred_element_type=f32)


def gelu_product(first_half, second_half):
    return jax.nn.gelu(first_half, approximate=False) * second_half


def dot_nt(left, right):
    return lax.dot_general(left, right, (((1,), (1,)), ((), ())), preferred_element_type=f32)


def dot_tn(left, right):
    return lax.dot_general(left, right, (((0,), (0,)), ((), ())), preferred_element_type=f32)


def swap_halves(values):
    width = values.shape[1]
    lanes = lax.broadcasted_iota(jnp.int32, values.shape, 1)
    up = pltpu.roll(values, width - HEAD_DIM // 2, 1)
    down = pltpu.roll(values, HEAD_DIM // 2, 1)
    return jnp.where(lanes % HEAD_DIM < HEAD_DIM // 2, up, down)


def excluded_bias(marks_row, marks_col, start, windowed):
    docs = marks_row[0:1, pl.ds(start, BLOCK)]
    allowed = marks_col[:, 0:1] == docs
    if windowed:
        apart = marks_col[:, 1:2] - marks_row[1:2, pl.ds(start, BLOCK)]
        allowed = allowed & (jnp.abs(apart) <= WINDOW // 2)
    return jnp.where(allowed, 0.0, -1e30)


def attend_kernel(
    windowed,
    near, far, w_qkv, w_out, cosine, sine, marks_row, marks_col,
    queries, keys, values, logs, attended, near_term, far_term,
    projected,
):
    near_rows = near.shape[0]
    width = w_out.shape[0]
    projected[:near_rows] = jnp.dot(near[...], w_qkv[...], preferred_element_type=f32)
    projected[near_rows:] = jnp.dot(far[...], w_qkv[...], preferred_element_type=f32)
    for index, target in ((0, queries), (1, keys)):
        part = projected[:, index * width : (index + 1) * width]
        turned = part * cosine[...] + swap_halves(part) * sine[...]
        target[...] = turned.astype(bf16)
    values[...] = projected[:, 2 * width :].astype(bf16)
    heads = width // HEAD_DIM
    lanes = lax.broadcasted_iota(jnp.int32, (BLOCK, width), 1) // HEAD_DIM

    def step(index, carry):
        start = pl.multiple_of(index * BLOCK, BLOCK)
        bias = excluded_bias(marks_row, marks_col, start, windowed)
        block = queries[pl.ds(start, BLOCK)] * jnp.asarray(HEAD_DIM ** (-0.5), bf16)
        total = jnp.zeros((BLOCK, width), f32)
        for head in range(heads):
            own = jnp.where(lanes == head, block, jnp.zeros_like(block))
            scores = dot_nt(keys[...], own) + bias
            largest = jnp.max(scores, axis=0, keepdims=True)
            powers = jnp.exp(scores - largest)
            sums = jnp.sum(powers, axis=0, keepdims=True)
            soft = (powers * (1.0 / sums)).astype(bf16)
            logs[pl.ds(head, 1), pl.ds(start, BLOCK)] = largest + jnp.log(sums)
            total = jnp.where(lanes == head, dot_tn(soft, values[...]), total)
        attended[pl.ds(start, BLOCK)] = total.astype(bf16)
        return carry

    lax.fori_loop(0, queries.shape[0] // BLOCK, step, 0)
    far_term[...] = jnp.dot(
        attended[near_rows:], w_out[...], preferred_element_type=f32
    ).astype(bf16)
    near_term[...] = jnp.dot(
        attended[:near_rows], w_out[...], preferred_element_type=f32
    ).astype(bf16)


def attend_back_kernel(
    windowed,
    near, far, w_qkv, w_out, cosine, sine, marks_row, marks_col,
    queries, keys, values, logs,
    grad_projected, near_term, far_term,
    grad_attended, grad_queries, grad_keys, grad_values,
):
    near_rows = near.shape[0]
    width = w_out.shape[0]
    grad_attended[:near_rows] = dot_nt(near[...], w_out[...]).astype(bf16)
    grad_attended[near_rows:] = dot_nt(far[...], w_out[...]).astype(bf16)
    grad_keys[...] = jnp.zeros_like(grad_keys)
    grad_values[...] = jnp.zeros_like(grad_values)
    heads = width // HEAD_DIM
    lanes = lax.broadcasted_iota(jnp.int32, (BLOCK, width), 1) // HEAD_DIM
    all_lanes = lax.broadcasted_iota(jnp.int32, queries.shape, 1) // HEAD_DIM

    def step(index, carry):
        start = pl.multiple_of(index * BLOCK, BLOCK)
        bias = excluded_bias(marks_row, marks_col, start, windowed)
        block = queries[pl.ds(start, BLOCK)] * jnp.asarray(HEAD_DIM ** (-0.5), bf16)
        grad_block = grad_attended[pl.ds(start, BLOCK)]
        total = jnp.zeros((BLOCK, width), f32)
        more_keys = jnp.zeros(queries.shape, f32)
        more_values = jnp.zeros(queries.shape, f32)
        for head in range(heads):
            own = jnp.where(lanes == head, block, jnp.zeros_like(block))
            own_grad = jnp.where(lanes == head, grad_block, jnp.zeros_like(grad_block))
            scores = dot_nt(keys[...], own) + bias
            soft = jnp.exp(scores - logs[pl.ds(head, 1), pl.ds(start, BLOCK)])
            grad_soft = dot_nt(values[...], own_grad)
            dots = jnp.sum(soft * grad_soft, axis=0, keepdims=True)
            grad_scores = (soft * (grad_soft - dots)).astype(bf16)
            more_values += jnp.dot(soft.astype(bf16), own_grad, preferred_element_type=f32)
            more_keys += jnp.dot(grad_scores, own, preferred_element_type=f32)
            total = jnp.where(lanes == head, dot_tn(grad_scores, keys[...]), total)
        grad_queries[pl.ds(start, BLOCK)] = total * HEAD_DIM ** (-0.5)
        grad_keys[...] += more_keys
        grad_values[...] += more_values
        return carry

    lax.fori_loop(0, queries.shape[0] // BLOCK, step, 0)
    for index, source in ((0, grad_queries), (1, grad_keys)):
        part = source[...]
        back = part * cosine[...] - swap_halves(part) * sine[...]
        grad_projected[:, index * width : (index + 1) * width] = back.astype(bf16)
    grad_projected[:, 2 * width :] = grad_values[...].astype(bf16)
    far_term[...] = dot_nt(grad_projected[near_rows:], w_qkv[...]).astype(bf16)
    near_term[...] = dot_nt(grad_projected[:near_rows], w_qkv[...]).astype(bf16)


def whole_call(kernel, out_shapes, scratch_shapes, flops, *operands):
    whole = pl.BlockSpec(memory_space=pltpu.VMEM)
    return pl.pallas_call(
        kernel,
        out_shape=[jax.ShapeDtypeStruct(*shape) for shape in out_shapes],
        in_specs=[whole] * len(operands),
        out_specs=[whole] * len(out_shapes),
        scratch_shapes=scratch_shapes,
        compiler_params=pltpu.CompilerParams(vmem_limit_bytes=40 * 1024 * 1024),
        cost_estimate=pl.CostEstimate(flops=flops, bytes_accessed=8 << 20, transcendentals=1 << 20),
    )(*operands)


def in_turn(work, parts):
    first = work(0, parts[0])
    return first, work(1, after_all(parts[1], first))


def forward_layer(inputs, normed_parts, gain_mid, weights, allowed, tables, late, points):
    w_qkv, w_out = weights[0], weights[1]
    near_rows, model_width = normed_parts[0].shape
    far_rows = normed_parts[1].shape[0]
    full_rows = near_rows + far_rows
    width = w_out.shape[0]
    windowed, marks_row, marks_col = allowed
    queries, keys, values, logs, attended, near_term, far_term = whole_call(
        functools.partial(attend_kernel, windowed),
        [((full_rows, width), bf16)] * 3
        + [((8, full_rows), f32), ((full_rows, width), bf16)]
        + [((near_rows, model_width), bf16), ((far_rows, model_width), bf16)],
        [pltpu.VMEM((full_rows, 3 * width), f32)],
        3 << 30,
        *normed_parts, w_qkv, w_out, *tables, marks_row, marks_col,
    )
    points[1](far_term)
    resid_mid = inputs + scatter_parts(near_term, far_term)
    points[2](resid_mid)
    mid_parts = gather_parts(layer_norm(resid_mid, gain_mid).astype(bf16))
    points[3](mid_parts)
    w_up, w_down = weights[2], weights[3]

    def feed(k, part):
        hidden = contract_last(part, w_up)
        local_hidden = hidden.shape[1] // 2
        gelu_in = hidden[:, :local_hidden]
        gate_mult = hidden[:, local_hidden:]
        mixed = gelu_product(gelu_in, gate_mult).astype(bf16)
        return gelu_in, gate_mult, mixed, None if late else times(mixed, w_down).astype(bf16)

    fed = in_turn(feed, mid_parts)
    if late:

        def result(gate):
            held = after_all((fed[0][2], fed[1][2]), gate)
            return [times(mixed, w_down).astype(bf16) for mixed in held]

    else:
        result = resid_mid + scatter_parts(fed[0][3], fed[1][3])
    kept = dict(
        inputs=inputs,
        resid_mid=resid_mid,
        normed=normed_parts,
        queries=queries,
        keys=keys,
        values=values,
        logs=logs,
        attended=attended,
        normed_mid=mid_parts,
        gelu_in=(fed[0][0], fed[1][0]),
        gate_mult=(fed[0][1], fed[1][1]),
        mixed=(fed[0][2], fed[1][2]),
    )
    return (result, kept)


def backward_ffn(grad_result, kept, gain_mid, weights, gate):
    w_up, w_down = weights[2], weights[3]
    grad_parts = after_all(gather_parts(grad_result.astype(bf16)), gate)

    def feed_back(k, part):
        grad_mixed = contract_last(part, w_down)
        unused, pull_gelu = jax.vjp(gelu_product, kept["gelu_in"][k], kept["gate_mult"][k])
        terms = tuple(term.astype(bf16) for term in pull_gelu(grad_mixed))
        return terms[0], terms[1], times(joined(terms, 1), w_up).astype(bf16)

    near, far = in_turn(feed_back, grad_parts)
    grad_normed_mid = scatter_parts(near[2], far[2])
    unused, pull_norm = jax.vjp(layer_norm, kept["resid_mid"], gain_mid)
    grad_resid, grad_gain = pull_norm(grad_normed_mid)

    def weight_grads(gate):
        outer, inner, left, first, second = after_all(
            (grad_parts, kept["mixed"], kept["normed_mid"], (near[0], far[0]), (near[1], far[1])),
            gate,
        )
        outer, inner, left = joined(outer), joined(inner), joined(left)
        first, second = joined(first), joined(second)
        half = inner.shape[1] // 2
        front, back = inner[:, :half], inner[:, half:]
        sent_up, add_up = add_core(lambda core: contract_rows(core(first, second), left))
        sent_down, add_down = add_core(lambda core: contract_rows(core(front, back), outer))

        def pack(gate):
            up, down = add_up(gate), add_down(gate)
            rows = up.shape[0] + down.shape[0]
            blank = jnp.zeros((-rows % 128, up.shape[1]), bf16)
            return joined([up, down, blank])

        return (sent_up, sent_down), pack

    return (grad_result + grad_resid, weight_grads, grad_gain)


def backward_attn(grad_mid, kept, gain_first, weights, allowed, tables, gate, pack):
    w_qkv, w_out = weights[0], weights[1]
    grad_parts = gather_parts(grad_mid.astype(bf16))
    near, far = after_all(grad_parts, gate)
    full_rows, width = kept["queries"].shape
    windowed, marks_row, marks_col = allowed
    grad_projected, near_term, far_term = whole_call(
        functools.partial(attend_back_kernel, windowed),
        [((full_rows, 3 * width), bf16), (near.shape, bf16), (far.shape, bf16)],
        [pltpu.VMEM((full_rows, width), bf16)] + [pltpu.VMEM((full_rows, width), f32)] * 3,
        4 << 30,
        near, far, w_qkv, w_out, *tables, marks_row, marks_col,
        kept["queries"], kept["keys"], kept["values"], kept["logs"],
    )
    packed = pack(grad_projected)
    near_term, far_term = after_all((near_term, far_term), packed)
    grad_normed = scatter_parts(near_term, far_term)
    unused, pull_norm = jax.vjp(layer_norm, kept["inputs"], gain_first)
    grad_resid, grad_gain = pull_norm(grad_normed)

    def gain_before():
        total = 0.0
        for term, normed in zip((near_term, far_term), kept["normed"]):
            total = total + jnp.sum(term.astype(f32) * normed.astype(f32), axis=0)
        return total / gain_first

    def weight_grads(gate, gains):
        outer, inner, left, right = after_all(
            (grad_parts, kept["attended"], kept["normed"], grad_projected), gate
        )
        outer, left = joined(outer), joined(left)
        width = inner.shape[1]
        of_q, of_k, of_v = (right[:, i * width : (i + 1) * width] for i in range(3))
        one = add_core(lambda core: contract_rows(left, core(of_q, of_v)))[1](())
        two = add_core(lambda core: contract_rows(core(left, outer), core(of_k, inner)))[1](())
        extra = jnp.stack(gains).astype(bf16).reshape(-1, width)
        blank = jnp.zeros((-extra.shape[0] % 128, width), bf16)
        return joined([one, two, extra, blank])

    return (grad_mid + grad_resid, weight_grads, grad_gain, gain_before, packed)


def fetch_half(own, after):
    piece = own.shape[0] // 2
    start = lax.axis_index("core") * piece
    return swap_layer(lax.dynamic_slice_in_dim(after_all(own, after), start, piece))


def both_halves(half, after=()):
    half = after_all(half, after)
    return in_order(lax.axis_index("core"), half, swap_core(half))


def by_layer(is_first, own, other):
    return jnp.where(is_first, own, other), jnp.where(is_first, other, own)


def in_order(index, mine, other):
    low = jnp.where(index == 0, mine, other)
    high = jnp.where(index == 0, other, mine)
    return jnp.concatenate([low, high], axis=0)


def add_core(product):
    is_core0 = lax.axis_index("core") == 0
    sent = product(lambda one, two: jnp.where(is_core0, two, one)).astype(bf16)

    def add(gate):
        held = product(lambda one, two: after_all(jnp.where(is_core0, one, two), gate))
        return (held + swap_core(sent).astype(f32)).astype(bf16)

    return sent, add


def reduce_part(grads):
    return lax.psum_scatter(grads, ("zlo", "x"), scatter_dimension=0, tiled=True)


def reduce_part_now(grads):
    pieces = lax.all_to_all(grads, ("zlo", "x"), 0, 0, tiled=True)
    pieces = pieces.reshape(8, -1, pieces.shape[1])
    return jnp.sum(pieces.astype(f32), axis=0).astype(bf16)


def spread_part(part):
    copies = jnp.broadcast_to(part[None], (8,) + part.shape).reshape(-1, part.shape[1])
    return lax.all_to_all(copies, ("zlo", "x"), 0, 0, tiled=True)


def pick_sections(is_first, part_first, part_second):
    own = jnp.where(is_first, part_first, part_second)
    sent = jnp.where(is_first, part_second, part_first)
    return own, sent


def local(tokens, cotangent, lengths, gains, w_qkv, w_out, w_up, w_down):
    section_index = lax.axis_index("section")
    is_first = section_index == 0
    row_count = tokens.shape[1]
    full_rows = row_count * lax.axis_size("tensor")
    start_rows = jnp.where(is_first, tokens[0], tokens[1])
    end_grads = jnp.where(is_first, cotangent[0], cotangent[1])
    start_parts = gather_parts(start_rows)
    gains_other = swap_layer(gains[0])
    gains0 = jnp.where(is_first, gains[0], gains_other)
    gains1 = jnp.where(is_first, gains_other, gains[0])
    start_rows = start_rows.astype(f32)
    own = (
        jnp.transpose(w_qkv[0], (1, 0, 2)).reshape(-1, w_qkv.shape[3]),
        w_out[0],
        jnp.transpose(w_up[0], (1, 2, 0)).reshape(-1, w_up.shape[1]),
        w_down[0],
    )
    half_qkv = fetch_half(own[0], ())
    half_out = fetch_half(own[1], ())
    start_parts, lengths = after_all((start_parts, lengths), (half_qkv, half_out))
    first_parts = in_turn(
        lambda k, part: layer_norm(part.astype(f32), gains0[0]).astype(bf16), start_parts
    )
    qkv0, qkv1 = by_layer(is_first, own[0], both_halves(half_qkv))
    layer0 = [joined(jnp.split(qkv0, 3), 1)]
    layer1 = [joined(jnp.split(qkv1, 3), 1)]
    hidden_width = w_up.shape[3]
    moving = []

    out0, out1 = by_layer(is_first, own[1], both_halves(half_out))
    layer0.append(out0)
    layer1.append(out1)
    moving.append(fetch_half(own[2][:hidden_width], half_out))

    def at_far_term(far_term):
        moving.append(both_halves(moving[0], far_term))
        moving.append(fetch_half(own[2][hidden_width:], (moving[0], far_term)))

    def at_mid(resid_mid):
        moving.append(both_halves(moving[2], resid_mid))
        moving.append(fetch_half(own[3], (moving[2], resid_mid)))

    def at_gathered(parts):
        up0, up1 = by_layer(is_first, own[2], joined([moving[1], moving[3]]))
        down0, down1 = by_layer(is_first, own[3], both_halves(moving[4], parts))
        layer0.extend([up0, down0])
        layer1.extend([up1, down1])

    points = (None, at_far_term, at_mid, at_gathered)

    doc_lengths = jnp.where(is_first, lengths[0, 0], lengths[1, 0])
    indices = jnp.arange(full_rows, dtype=jnp.int32)
    blocks = jnp.array([0, 1, 3, 2], jnp.int32) + lax.axis_index("tensor")
    indices = (jnp.repeat(blocks, row_count) * row_count + indices % row_count) % full_rows
    doc_ids, positions = doc_layout(doc_lengths, indices)
    marks_row = jnp.stack([doc_ids, indices])
    marks_col = jnp.stack([doc_ids, indices], axis=1)
    allowed0 = (True, marks_row, marks_col)
    allowed1 = (False, marks_row, marks_col)
    heads = w_out.shape[1] // HEAD_DIM
    tables0 = rope_tables(positions, 10000.0, heads)
    tables1 = rope_tables(positions, 160000.0, heads)

    out0, kept0 = forward_layer(
        start_rows, first_parts, gains0[1], layer0, allowed0, tables0, False, points
    )
    out0 = out0.astype(bf16)
    second_rows = out0.astype(f32)
    second_parts = gather_parts(layer_norm(second_rows, gains1[0]).astype(bf16))
    out1_of, kept1 = forward_layer(
        second_rows, second_parts, gains1[1], layer1, allowed1, tables1, True, (lambda value: None,) * 4
    )
    mid1, ffn_grads1, gain_mid1 = backward_ffn(
        end_grads.astype(f32), kept1, gains1[1], layer1, ()
    )
    ffn_sent1, ffn_pack1 = ffn_grads1(mid1)
    in1, attn_grads1, gain_first1, unused, unused = backward_attn(
        mid1, kept1, gains1[0], layer1, allowed1, tables1, ffn_sent1, lambda gate: ()
    )
    in1 = in1.astype(bf16)
    ffn_pack1 = ffn_pack1(in1)
    mid0, ffn_grads0, gain_mid0 = backward_ffn(
        in1.astype(f32), kept0, gains0[1], layer0, ffn_pack1
    )
    model_width = w_qkv.shape[1]
    ffn1 = reduce_part(ffn_pack1)
    ffn_pack0 = ffn_grads0(mid0)[1](())
    in0, attn_grads0, unused, gain_before, unused = backward_attn(
        mid0, kept0, gains0[0], layer0, allowed0, tables0, ffn_pack0, lambda gate: ()
    )
    in0 = in0.astype(bf16)
    ffn0 = reduce_part(ffn_pack0)
    attn_pack1 = attn_grads1(in1, [gain_first1, gain_mid1])
    attn_pack0 = attn_grads0((), [gain_before(), gain_mid0])
    out1_terms = out1_of(ffn_pack0)
    out1 = (kept1["resid_mid"] + scatter_parts(*out1_terms)).astype(bf16)
    attn_width = attn_pack0.shape[1]
    packs = [pack.reshape(8, -1, attn_width) for pack in (attn_pack0, attn_pack1)]
    attn_rows = packs[0].shape[1]
    attn_both = reduce_part_now(joined(packs, 1).reshape(-1, attn_width))
    part0 = joined([ffn0, attn_both[:attn_rows].reshape(-1, model_width)])
    part1 = joined([ffn1, attn_both[attn_rows:].reshape(-1, model_width)])
    own_part, sent_part = pick_sections(is_first, part0, part1)
    sent_part = after_all(sent_part, in0, out1)
    part = (own_part.astype(f32) + swap_section(sent_part).astype(f32)).astype(bf16)
    ffn_rows = ffn0.shape[0]
    ffn_half = spread_part(part[:ffn_rows])
    attn_part = after_all(part[ffn_rows:].reshape(-1, attn_width), ffn_half)
    attn_half = spread_part(attn_part)
    is_core0 = lax.axis_index("core") == 0

    def of_core(core, halves, start, count):
        mine, other = (both[start : start + count] for both in halves)
        return jnp.where(is_core0 == (core == 0), mine, other).astype(f32)

    ffn_halves = (ffn_half, swap_core(ffn_half))
    down_rows = w_down.shape[1] // 2
    grad_up = jnp.stack([of_core(core, ffn_halves, 0, hidden_width) for core in range(2)])
    grad_down = joined(
        [of_core(core, ffn_halves, hidden_width, down_rows) for core in range(2)]
    )
    attn_half, grad_up, grad_down = lax.optimization_barrier((attn_half, grad_up, grad_down))
    attn_halves = (attn_half, swap_core(attn_half))
    gain_rows = sum(of_core(core, attn_halves, 2 * model_width, 8) for core in range(2))
    gain_total = sum_tensor(gain_rows).reshape(2, -1)
    grad_qkv = jnp.stack(
        [
            of_core(0, attn_halves, 0, model_width),
            of_core(0, attn_halves, model_width, model_width),
            of_core(1, attn_halves, 0, model_width),
        ]
    )
    grad_out = of_core(1, attn_halves, model_width, model_width).T

    sent_out, sent_in = after_all(
        (jnp.where(is_first, out1, out0), jnp.where(is_first, in1, in0)), ffn_half
    )
    got_out, got_in = swap_section(sent_out), swap_section(sent_in)
    section_out = jnp.stack(
        [jnp.where(is_first, out0, got_out), jnp.where(is_first, got_out, out1)]
    )
    input_grads = jnp.stack(
        [jnp.where(is_first, in0, got_in), jnp.where(is_first, got_in, in1)]
    )
    return (
        section_out[None],
        input_grads[None],
        gain_total[None],
        jnp.transpose(grad_qkv, (1, 0, 2))[None],
        grad_out[None],
        jnp.transpose(grad_up, (2, 0, 1))[None],
        grad_down[None],
    )


def solution(mesh):
    sizes = dict(zip(mesh.axis_names, mesh.devices.shape))
    fine = Mesh(
        mesh.devices.reshape(sizes["section"], 2, sizes["dp"] // 4, 2, sizes["tensor"]),
        ("section", "zlo", "x", "core", "tensor"),
    )
    rows = ("zlo", "x", "core", "tensor")
    in_specs = (
        P(None, rows, None),
        P(None, rows, None),
        P(None, DP, None),
        P("section", None, None),
        P("section", None, None, "tensor"),
        P("section", "tensor", None),
        P("section", None, None, "tensor"),
        P("section", "tensor", None),
    )
    out_specs = (
        P("section", None, rows, None),
        P("section", None, rows, None),
        P("section", None, None),
        P("section", None, None, "tensor"),
        P("section", "tensor", None),
        P("section", None, None, "tensor"),
        P("section", "tensor", None),
    )
    return jax.shard_map(local, mesh=fine, in_specs=in_specs, out_specs=out_specs, check_vma=False)
```

```python
import functools

import jax
import jax.numpy as jnp
from jax import lax
from jax.experimental import pallas as pl
from jax.experimental.pallas import tpu as pltpu
from jax.sharding import Mesh
from jax.sharding import PartitionSpec as P

HEAD_DIM = 64
WINDOW = 128

epsilon = 1e-05
bf16 = jnp.bfloat16
f32 = jnp.float32

BLOCK = 256

DP = ("zlo", "x", "core")


def around(block, axis, distance):
    count = lax.axis_size(axis)
    return lax.ppermute(block, axis, [(i, (i + distance) % count) for i in range(count)])


def swap_core(block):
    return lax.ppermute(block, "core", [(0, 1), (1, 0)])


def swap_section(block):
    return lax.ppermute(block, "section", [(0, 1), (1, 0)])


def swap_layer(block):
    return lax.ppermute(block, ("section", "zlo"), [(0, 3), (1, 2), (2, 1), (3, 0)])


def gather_parts(block):
    far = around(block, "tensor", 2)
    ahead = around(block, "tensor", -1)
    behind = around(block, "tensor", 1)
    return [joined([block, ahead, behind]), far]


def scatter_parts(near, far):
    rows = far.shape[0]
    sent_far = around(far.astype(bf16), "tensor", 2)
    sent_ahead = around(near[rows : 2 * rows].astype(bf16), "tensor", 1)
    sent_behind = around(near[2 * rows :].astype(bf16), "tensor", -1)
    kept = near[:rows].astype(f32)
    return kept + sent_far.astype(f32) + sent_ahead.astype(f32) + sent_behind.astype(f32)


def joined(parts, axis=0):
    return jnp.concatenate(parts, axis=axis)


def after_all(values, *others):
    return lax.optimization_barrier((values,) + others)[0]


def sum_tensor(block):
    return (
        block
        + around(block, "tensor", 2)
        + around(block, "tensor", 1)
        + around(block, "tensor", -1)
    )


def layer_norm(values, gain_scale):
    centered = values - jnp.mean(values, axis=-1, keepdims=True)
    variance = jnp.mean(centered * centered, axis=-1, keepdims=True)
    return centered * lax.rsqrt(variance + epsilon) * gain_scale


def doc_layout(doc_lengths, indices):
    doc_ends = jnp.cumsum(doc_lengths)
    passed = indices[:, None] >= doc_ends[None, :]
    doc_ids = jnp.sum(passed.astype(jnp.int32), axis=1)
    starts = jnp.sum(jnp.where(passed, doc_lengths[None, :], 0), axis=1)
    return (doc_ids, indices - starts)


def rope_tables(positions, rope_base, heads):
    half_dim = HEAD_DIM // 2
    inverse = rope_base ** (-2.0 * jnp.arange(half_dim, dtype=f32) / HEAD_DIM)
    angles = positions.astype(f32)[:, None] * inverse
    cosine, sine = jnp.cos(angles), jnp.sin(angles)
    cosine = jnp.concatenate([cosine, cosine], axis=-1)
    sine = jnp.concatenate([-sine, sine], axis=-1)
    return (jnp.tile(cosine, (1, heads)), jnp.tile(sine, (1, heads)))


def contract_rows(left_rows, right_rows):
    return lax.dot_general(
        left_rows, right_rows, (((0,), (0,)), ((), ())), preferred_element_type=f32
    )


def contract_last(left_rows, weight):
    return lax.dot_general(
        left_rows, weight, (((1,), (1,)), ((), ())), preferred_element_type=f32
    )


def times(left_rows, weight):
    return jnp.dot(left_rows, weight, preferred_element_type=f32)


def gelu_product(first_half, second_half):
    return jax.nn.gelu(first_half, approximate=False) * second_half


def dot_nt(left, right):
    return lax.dot_general(left, right, (((1,), (1,)), ((), ())), preferred_element_type=f32)


def dot_tn(left, right):
    return lax.dot_general(left, right, (((0,), (0,)), ((), ())), preferred_element_type=f32)


def swap_halves(values):
    width = values.shape[1]
    lanes = lax.broadcasted_iota(jnp.int32, values.shape, 1)
    up = pltpu.roll(values, width - HEAD_DIM // 2, 1)
    down = pltpu.roll(values, HEAD_DIM // 2, 1)
    return jnp.where(lanes % HEAD_DIM < HEAD_DIM // 2, up, down)


def excluded_bias(marks_row, marks_col, start, windowed):
    docs = marks_row[0:1, pl.ds(start, BLOCK)]
    allowed = marks_col[:, 0:1] == docs
    if windowed:
        apart = marks_col[:, 1:2] - marks_row[1:2, pl.ds(start, BLOCK)]
        allowed = allowed & (jnp.abs(apart) <= WINDOW // 2)
    return jnp.where(allowed, 0.0, -1e30)


def attend_kernel(
    windowed,
    near, far, w_qkv, w_out, cosine, sine, marks_row, marks_col,
    queries, keys, values, logs, attended, near_term, far_term,
    projected,
):
    near_rows = near.shape[0]
    width = w_out.shape[0]
    projected[:near_rows] = jnp.dot(near[...], w_qkv[...], preferred_element_type=f32)
    projected[near_rows:] = jnp.dot(far[...], w_qkv[...], preferred_element_type=f32)
    for index, target in ((0, queries), (1, keys)):
        part = projected[:, index * width : (index + 1) * width]
        turned = part * cosine[...] + swap_halves(part) * sine[...]
        target[...] = turned.astype(bf16)
    values[...] = projected[:, 2 * width :].astype(bf16)
    heads = width // HEAD_DIM
    lanes = lax.broadcasted_iota(jnp.int32, (BLOCK, width), 1) // HEAD_DIM

    def step(index, carry):
        start = pl.multiple_of(index * BLOCK, BLOCK)
        bias = excluded_bias(marks_row, marks_col, start, windowed)
        block = queries[pl.ds(start, BLOCK)] * jnp.asarray(HEAD_DIM ** (-0.5), bf16)
        total = jnp.zeros((BLOCK, width), f32)
        for head in range(heads):
            own = jnp.where(lanes == head, block, jnp.zeros_like(block))
            scores = dot_nt(keys[...], own) + bias
            largest = jnp.max(scores, axis=0, keepdims=True)
            powers = jnp.exp(scores - largest)
            sums = jnp.sum(powers, axis=0, keepdims=True)
            soft = (powers * (1.0 / sums)).astype(bf16)
            logs[pl.ds(head, 1), pl.ds(start, BLOCK)] = largest + jnp.log(sums)
            total = jnp.where(lanes == head, dot_tn(soft, values[...]), total)
        attended[pl.ds(start, BLOCK)] = total.astype(bf16)
        return carry

    lax.fori_loop(0, queries.shape[0] // BLOCK, step, 0)
    far_term[...] = jnp.dot(
        attended[near_rows:], w_out[...], preferred_element_type=f32
    ).astype(bf16)
    near_term[...] = jnp.dot(
        attended[:near_rows], w_out[...], preferred_element_type=f32
    ).astype(bf16)


def attend_back_kernel(
    windowed,
    near, far, w_qkv, w_out, cosine, sine, marks_row, marks_col,
    queries, keys, values, logs,
    grad_projected, near_term, far_term,
    grad_attended, grad_queries, grad_keys, grad_values,
):
    near_rows = near.shape[0]
    width = w_out.shape[0]
    grad_attended[:near_rows] = dot_nt(near[...], w_out[...]).astype(bf16)
    grad_attended[near_rows:] = dot_nt(far[...], w_out[...]).astype(bf16)
    grad_keys[...] = jnp.zeros_like(grad_keys)
    grad_values[...] = jnp.zeros_like(grad_values)
    heads = width // HEAD_DIM
    lanes = lax.broadcasted_iota(jnp.int32, (BLOCK, width), 1) // HEAD_DIM
    all_lanes = lax.broadcasted_iota(jnp.int32, queries.shape, 1) // HEAD_DIM

    def step(index, carry):
        start = pl.multiple_of(index * BLOCK, BLOCK)
        bias = excluded_bias(marks_row, marks_col, start, windowed)
        block = queries[pl.ds(start, BLOCK)] * jnp.asarray(HEAD_DIM ** (-0.5), bf16)
        grad_block = grad_attended[pl.ds(start, BLOCK)]
        total = jnp.zeros((BLOCK, width), f32)
        more_keys = jnp.zeros(queries.shape, f32)
        more_values = jnp.zeros(queries.shape, f32)
        for head in range(heads):
            own = jnp.where(lanes == head, block, jnp.zeros_like(block))
            own_grad = jnp.where(lanes == head, grad_block, jnp.zeros_like(grad_block))
            scores = dot_nt(keys[...], own) + bias
            soft = jnp.exp(scores - logs[pl.ds(head, 1), pl.ds(start, BLOCK)])
            grad_soft = dot_nt(values[...], own_grad)
            dots = jnp.sum(soft * grad_soft, axis=0, keepdims=True)
            grad_scores = (soft * (grad_soft - dots)).astype(bf16)
            more_values += jnp.dot(soft.astype(bf16), own_grad, preferred_element_type=f32)
            more_keys += jnp.dot(grad_scores, own, preferred_element_type=f32)
            total = jnp.where(lanes == head, dot_tn(grad_scores, keys[...]), total)
        grad_queries[pl.ds(start, BLOCK)] = total * HEAD_DIM ** (-0.5)
        grad_keys[...] += more_keys
        grad_values[...] += more_values
        return carry

    lax.fori_loop(0, queries.shape[0] // BLOCK, step, 0)
    for index, source in ((0, grad_queries), (1, grad_keys)):
        part = source[...]
        back = part * cosine[...] - swap_halves(part) * sine[...]
        grad_projected[:, index * width : (index + 1) * width] = back.astype(bf16)
    grad_projected[:, 2 * width :] = grad_values[...].astype(bf16)
    far_term[...] = dot_nt(grad_projected[near_rows:], w_qkv[...]).astype(bf16)
    near_term[...] = dot_nt(grad_projected[:near_rows], w_qkv[...]).astype(bf16)


def whole_call(kernel, out_shapes, scratch_shapes, flops, *operands):
    whole = pl.BlockSpec(memory_space=pltpu.VMEM)
    return pl.pallas_call(
        kernel,
        out_shape=[jax.ShapeDtypeStruct(*shape) for shape in out_shapes],
        in_specs=[whole] * len(operands),
        out_specs=[whole] * len(out_shapes),
        scratch_shapes=scratch_shapes,
        compiler_params=pltpu.CompilerParams(vmem_limit_bytes=40 * 1024 * 1024),
        cost_estimate=pl.CostEstimate(flops=flops, bytes_accessed=8 << 20, transcendentals=1 << 20),
    )(*operands)


def in_turn(work, parts):
    first = work(0, parts[0])
    return first, work(1, after_all(parts[1], first))


def forward_layer(inputs, normed_parts, gain_mid, weights, allowed, tables, late, points):
    w_qkv, w_out = weights[0], weights[1]
    near_rows, model_width = normed_parts[0].shape
    far_rows = normed_parts[1].shape[0]
    full_rows = near_rows + far_rows
    width = w_out.shape[0]
    windowed, marks_row, marks_col = allowed
    queries, keys, values, logs, attended, near_term, far_term = whole_call(
        functools.partial(attend_kernel, windowed),
        [((full_rows, width), bf16)] * 3
        + [((8, full_rows), f32), ((full_rows, width), bf16)]
        + [((near_rows, model_width), bf16), ((far_rows, model_width), bf16)],
        [pltpu.VMEM((full_rows, 3 * width), f32)],
        3 << 30,
        *normed_parts, w_qkv, w_out, *tables, marks_row, marks_col,
    )
    points[1](far_term)
    resid_mid = inputs + scatter_parts(near_term, far_term)
    points[2](resid_mid)
    mid_parts = gather_parts(layer_norm(resid_mid, gain_mid).astype(bf16))
    points[3](mid_parts)
    w_up, w_down = weights[2], weights[3]

    def feed(k, part):
        hidden = contract_last(part, w_up)
        local_hidden = hidden.shape[1] // 2
        gelu_in = hidden[:, :local_hidden]
        gate_mult = hidden[:, local_hidden:]
        mixed = gelu_product(gelu_in, gate_mult).astype(bf16)
        return gelu_in, gate_mult, mixed, None if late else times(mixed, w_down).astype(bf16)

    fed = in_turn(feed, mid_parts)
    if late:

        def result(gate):
            held = after_all((fed[0][2], fed[1][2]), gate)
            return [times(mixed, w_down).astype(bf16) for mixed in held]

    else:
        result = resid_mid + scatter_parts(fed[0][3], fed[1][3])
    kept = dict(
        inputs=inputs,
        resid_mid=resid_mid,
        normed=normed_parts,
        queries=queries,
        keys=keys,
        values=values,
        logs=logs,
        attended=attended,
        normed_mid=mid_parts,
        gelu_in=(fed[0][0], fed[1][0]),
        gate_mult=(fed[0][1], fed[1][1]),
        mixed=(fed[0][2], fed[1][2]),
    )
    return (result, kept)


def backward_ffn(grad_result, kept, gain_mid, weights, gate):
    w_up, w_down = weights[2], weights[3]
    grad_parts = after_all(gather_parts(grad_result.astype(bf16)), gate)

    def feed_back(k, part):
        grad_mixed = contract_last(part, w_down)
        unused, pull_gelu = jax.vjp(gelu_product, kept["gelu_in"][k], kept["gate_mult"][k])
        terms = tuple(term.astype(bf16) for term in pull_gelu(grad_mixed))
        return terms[0], terms[1], times(joined(terms, 1), w_up).astype(bf16)

    near, far = in_turn(feed_back, grad_parts)
    grad_normed_mid = scatter_parts(near[2], far[2])
    unused, pull_norm = jax.vjp(layer_norm, kept["resid_mid"], gain_mid)
    grad_resid, grad_gain = pull_norm(grad_normed_mid)

    def weight_grads(gate):
        outer, inner, left, first, second = after_all(
            (grad_parts, kept["mixed"], kept["normed_mid"], (near[0], far[0]), (near[1], far[1])),
            gate,
        )
        outer, inner, left = joined(outer), joined(inner), joined(left)
        first, second = joined(first), joined(second)
        half = inner.shape[1] // 2
        front, back = inner[:, :half], inner[:, half:]
        sent_up, add_up = add_core(lambda core: contract_rows(core(first, second), left))
        sent_down, add_down = add_core(lambda core: contract_rows(core(front, back), outer))

        def pack(gate):
            up, down = add_up(gate), add_down(gate)
            rows = up.shape[0] + down.shape[0]
            blank = jnp.zeros((-rows % 128, up.shape[1]), bf16)
            return joined([up, down, blank])

        return (sent_up, sent_down), pack

    return (grad_result + grad_resid, weight_grads, grad_gain)


def backward_attn(grad_mid, kept, gain_first, weights, allowed, tables, gate, pack):
    w_qkv, w_out = weights[0], weights[1]
    grad_parts = gather_parts(grad_mid.astype(bf16))
    near, far = after_all(grad_parts, gate)
    full_rows, width = kept["queries"].shape
    windowed, marks_row, marks_col = allowed
    grad_projected, near_term, far_term = whole_call(
        functools.partial(attend_back_kernel, windowed),
        [((full_rows, 3 * width), bf16), (near.shape, bf16), (far.shape, bf16)],
        [pltpu.VMEM((full_rows, width), bf16)] + [pltpu.VMEM((full_rows, width), f32)] * 3,
        4 << 30,
        near, far, w_qkv, w_out, *tables, marks_row, marks_col,
        kept["queries"], kept["keys"], kept["values"], kept["logs"],
    )
    packed = pack(grad_projected)
    near_term, far_term = after_all((near_term, far_term), packed)
    grad_normed = scatter_parts(near_term, far_term)
    unused, pull_norm = jax.vjp(layer_norm, kept["inputs"], gain_first)
    grad_resid, grad_gain = pull_norm(grad_normed)

    def gain_before():
        total = 0.0
        for term, normed in zip((near_term, far_term), kept["normed"]):
            total = total + jnp.sum(term.astype(f32) * normed.astype(f32), axis=0)
        return total / gain_first

    def weight_grads(gate, gains):
        outer, inner, left, right = after_all(
            (grad_parts, kept["attended"], kept["normed"], grad_projected), gate
        )
        outer, left = joined(outer), joined(left)
        width = inner.shape[1]
        of_q, of_k, of_v = (right[:, i * width : (i + 1) * width] for i in range(3))
        one = add_core(lambda core: contract_rows(left, core(of_q, of_v)))[1](())
        two = add_core(lambda core: contract_rows(core(left, outer), core(of_k, inner)))[1](())
        extra = jnp.stack(gains).astype(bf16).reshape(-1, width)
        blank = jnp.zeros((-extra.shape[0] % 128, width), bf16)
        return joined([one, two, extra, blank])

    return (grad_mid + grad_resid, weight_grads, grad_gain, gain_before, packed)


def fetch_half(own, after):
    piece = own.shape[0] // 2
    start = lax.axis_index("core") * piece
    return swap_layer(lax.dynamic_slice_in_dim(after_all(own, after), start, piece))


def both_halves(half, after=()):
    half = after_all(half, after)
    return in_order(lax.axis_index("core"), half, swap_core(half))


def by_layer(is_first, own, other):
    return jnp.where(is_first, own, other), jnp.where(is_first, other, own)


def in_order(index, mine, other):
    low = jnp.where(index == 0, mine, other)
    high = jnp.where(index == 0, other, mine)
    return jnp.concatenate([low, high], axis=0)


def add_core(product):
    is_core0 = lax.axis_index("core") == 0
    sent = product(lambda one, two: jnp.where(is_core0, two, one)).astype(bf16)

    def add(gate):
        held = product(lambda one, two: after_all(jnp.where(is_core0, one, two), gate))
        return (held + swap_core(sent).astype(f32)).astype(bf16)

    return sent, add


def reduce_part(grads):
    return lax.psum_scatter(grads, ("zlo", "x"), scatter_dimension=0, tiled=True)


def reduce_part_now(grads):
    pieces = lax.all_to_all(grads, ("zlo", "x"), 0, 0, tiled=True)
    pieces = pieces.reshape(8, -1, pieces.shape[1])
    return jnp.sum(pieces.astype(f32), axis=0).astype(bf16)


def spread_part(part):
    copies = jnp.broadcast_to(part[None], (8,) + part.shape).reshape(-1, part.shape[1])
    return lax.all_to_all(copies, ("zlo", "x"), 0, 0, tiled=True)


def pick_sections(is_first, part_first, part_second):
    own = jnp.where(is_first, part_first, part_second)
    sent = jnp.where(is_first, part_second, part_first)
    return own, sent


def local(tokens, cotangent, lengths, gains, w_qkv, w_out, w_up, w_down):
    section_index = lax.axis_index("section")
    is_first = section_index == 0
    row_count = tokens.shape[1]
    full_rows = row_count * lax.axis_size("tensor")
    start_rows = jnp.where(is_first, tokens[0], tokens[1])
    end_grads = jnp.where(is_first, cotangent[0], cotangent[1])
    start_parts = gather_parts(start_rows)
    gains_other = swap_layer(gains[0])
    gains0 = jnp.where(is_first, gains[0], gains_other)
    gains1 = jnp.where(is_first, gains_other, gains[0])
    start_rows = start_rows.astype(f32)
    own = (
        jnp.transpose(w_qkv[0], (1, 0, 2)).reshape(-1, w_qkv.shape[3]),
        w_out[0],
        jnp.transpose(w_up[0], (1, 2, 0)).reshape(-1, w_up.shape[1]),
        w_down[0],
    )
    half_qkv = fetch_half(own[0], ())
    half_out = fetch_half(own[1], ())
    start_parts, lengths = after_all((start_parts, lengths), (half_qkv, half_out))
    first_parts = in_turn(
        lambda k, part: layer_norm(part.astype(f32), gains0[0]).astype(bf16), start_parts
    )
    qkv0, qkv1 = by_layer(is_first, own[0], both_halves(half_qkv))
    layer0 = [joined(jnp.split(qkv0, 3), 1)]
    layer1 = [joined(jnp.split(qkv1, 3), 1)]
    hidden_width = w_up.shape[3]
    moving = []

    out0, out1 = by_layer(is_first, own[1], both_halves(half_out))
    layer0.append(out0)
    layer1.append(out1)
    moving.append(fetch_half(own[2][:hidden_width], half_out))

    def at_far_term(far_term):
        moving.append(both_halves(moving[0], far_term))
        moving.append(fetch_half(own[2][hidden_width:], (moving[0], far_term)))

    def at_mid(resid_mid):
        moving.append(both_halves(moving[2], resid_mid))
        moving.append(fetch_half(own[3], (moving[2], resid_mid)))

    def at_gathered(parts):
        up0, up1 = by_layer(is_first, own[2], joined([moving[1], moving[3]]))
        down0, down1 = by_layer(is_first, own[3], both_halves(moving[4], parts))
        layer0.extend([up0, down0])
        layer1.extend([up1, down1])

    points = (None, at_far_term, at_mid, at_gathered)

    doc_lengths = jnp.where(is_first, lengths[0, 0], lengths[1, 0])
    indices = jnp.arange(full_rows, dtype=jnp.int32)
    blocks = jnp.array([0, 1, 3, 2], jnp.int32) + lax.axis_index("tensor")
    indices = (jnp.repeat(blocks, row_count) * row_count + indices % row_count) % full_rows
    doc_ids, positions = doc_layout(doc_lengths, indices)
    marks_row = jnp.stack([doc_ids, indices])
    marks_col = jnp.stack([doc_ids, indices], axis=1)
    allowed0 = (True, marks_row, marks_col)
    allowed1 = (False, marks_row, marks_col)
    heads = w_out.shape[1] // HEAD_DIM
    tables0 = rope_tables(positions, 10000.0, heads)
    tables1 = rope_tables(positions, 160000.0, heads)

    out0, kept0 = forward_layer(
        start_rows, first_parts, gains0[1], layer0, allowed0, tables0, False, points
    )
    out0 = out0.astype(bf16)
    second_rows = out0.astype(f32)
    second_parts = gather_parts(layer_norm(second_rows, gains1[0]).astype(bf16))
    out1_of, kept1 = forward_layer(
        second_rows, second_parts, gains1[1], layer1, allowed1, tables1, True, (lambda value: None,) * 4
    )
    mid1, ffn_grads1, gain_mid1 = backward_ffn(
        end_grads.astype(f32), kept1, gains1[1], layer1, ()
    )
    ffn_sent1, ffn_pack1 = ffn_grads1(mid1)
    in1, attn_grads1, gain_first1, unused, unused = backward_attn(
        mid1, kept1, gains1[0], layer1, allowed1, tables1, ffn_sent1, lambda gate: ()
    )
    in1 = in1.astype(bf16)
    ffn_pack1 = ffn_pack1(in1)
    mid0, ffn_grads0, gain_mid0 = backward_ffn(
        in1.astype(f32), kept0, gains0[1], layer0, ffn_pack1
    )
    model_width = w_qkv.shape[1]
    ffn1 = reduce_part(ffn_pack1)
    ffn_sent0, ffn_pack0 = ffn_grads0(mid0)
    in0, attn_grads0, unused, gain_before, (ffn_pack0, unused) = backward_attn(
        mid0, kept0, gains0[0], layer0, allowed0, tables0, ffn_sent0,
        lambda gate: (ffn_pack0(gate), ffn1),
    )
    in0 = in0.astype(bf16)
    ffn0 = reduce_part(ffn_pack0)
    attn_pack1 = attn_grads1(in1, [gain_first1, gain_mid1])
    attn_pack0 = attn_grads0((), [gain_before(), gain_mid0])
    out1_terms = out1_of(ffn_pack0)
    out1 = (kept1["resid_mid"] + scatter_parts(*out1_terms)).astype(bf16)
    attn_width = attn_pack0.shape[1]
    packs = [pack.reshape(8, -1, attn_width) for pack in (attn_pack0, attn_pack1)]
    attn_rows = packs[0].shape[1]
    attn_both = reduce_part_now(joined(packs, 1).reshape(-1, attn_width))
    part0 = joined([ffn0, attn_both[:attn_rows].reshape(-1, model_width)])
    part1 = joined([ffn1, attn_both[attn_rows:].reshape(-1, model_width)])
    own_part, sent_part = pick_sections(is_first, part0, part1)
    sent_part = after_all(sent_part, in0, out1)
    part = (own_part.astype(f32) + swap_section(sent_part).astype(f32)).astype(bf16)
    ffn_rows = ffn0.shape[0]
    ffn_half = spread_part(part[:ffn_rows])
    got_out = swap_section(jnp.where(is_first, out1, out0))
    got_in = swap_section(jnp.where(is_first, in1, in0))
    attn_part = part[ffn_rows:].reshape(-1, attn_width)
    gain_start = 2 * model_width % attn_rows
    gain_span = slice(gain_start, gain_start + 8)
    gain_rows = attn_part[gain_span]
    holds_gains = lax.axis_index(("zlo", "x")) == 2 * model_width // attn_rows
    gain_rows = jnp.where(
        holds_gains, sum_tensor(gain_rows.astype(f32)).astype(bf16), gain_rows
    )
    attn_part = joined([attn_part[:gain_start], gain_rows, attn_part[gain_start + 8 :]])
    attn_part, got_out, got_in = after_all((attn_part, got_out, got_in), ffn_half)
    attn_part = after_all(attn_part, got_out, got_in)
    attn_half = spread_part(attn_part)
    is_core0 = lax.axis_index("core") == 0

    def of_core(core, halves, start, count):
        mine, other = (both[start : start + count] for both in halves)
        return jnp.where(is_core0 == (core == 0), mine, other).astype(f32)

    ffn_halves = (ffn_half, swap_core(ffn_half))
    down_rows = w_down.shape[1] // 2
    grad_up = jnp.stack([of_core(core, ffn_halves, 0, hidden_width) for core in range(2)])
    grad_down = joined(
        [of_core(core, ffn_halves, hidden_width, down_rows) for core in range(2)]
    )
    attn_half, grad_up, grad_down = lax.optimization_barrier((attn_half, grad_up, grad_down))
    attn_halves = (attn_half, swap_core(attn_half))
    gain_total = sum(of_core(core, attn_halves, 2 * model_width, 8) for core in range(2))
    gain_total = gain_total.reshape(2, -1)
    grad_qkv = jnp.stack(
        [
            of_core(0, attn_halves, 0, model_width),
            of_core(0, attn_halves, model_width, model_width),
            of_core(1, attn_halves, 0, model_width),
        ]
    )
    grad_out = of_core(1, attn_halves, model_width, model_width).T

    section_out = jnp.stack(
        [jnp.where(is_first, out0, got_out), jnp.where(is_first, got_out, out1)]
    )
    input_grads = jnp.stack(
        [jnp.where(is_first, in0, got_in), jnp.where(is_first, got_in, in1)]
    )
    return (
        section_out[None],
        input_grads[None],
        gain_total[None],
        jnp.transpose(grad_qkv, (1, 0, 2))[None],
        grad_out[None],
        jnp.transpose(grad_up, (2, 0, 1))[None],
        grad_down[None],
    )


def solution(mesh):
    sizes = dict(zip(mesh.axis_names, mesh.devices.shape))
    fine = Mesh(
        mesh.devices.reshape(sizes["section"], 2, sizes["dp"] // 4, 2, sizes["tensor"]),
        ("section", "zlo", "x", "core", "tensor"),
    )
    rows = ("zlo", "x", "core", "tensor")
    in_specs = (
        P(None, rows, None),
        P(None, rows, None),
        P(None, DP, None),
        P("section", None, None),
        P("section", None, None, "tensor"),
        P("section", "tensor", None),
        P("section", None, None, "tensor"),
        P("section", "tensor", None),
    )
    out_specs = (
        P("section", None, rows, None),
        P("section", None, rows, None),
        P("section", None, None),
        P("section", None, None, "tensor"),
        P("section", "tensor", None),
        P("section", None, None, "tensor"),
        P("section", "tensor", None),
    )
    return jax.shard_map(local, mesh=fine, in_specs=in_specs, out_specs=out_specs, check_vma=False)
```

```python
import functools

import jax
import jax.numpy as jnp
from jax import lax
from jax.experimental import pallas as pl
from jax.experimental.pallas import tpu as pltpu
from jax.sharding import Mesh
from jax.sharding import PartitionSpec as P

HEAD_DIM = 64
WINDOW = 128

epsilon = 1e-05
bf16 = jnp.bfloat16
f32 = jnp.float32

BLOCK = 256

DP = ("zlo", "x", "core")


def around(block, axis, distance):
    count = lax.axis_size(axis)
    return lax.ppermute(block, axis, [(i, (i + distance) % count) for i in range(count)])


def swap_core(block):
    return lax.ppermute(block, "core", [(0, 1), (1, 0)])


def swap_section(block):
    return lax.ppermute(block, "section", [(0, 1), (1, 0)])


def swap_layer(block):
    return lax.ppermute(block, ("section", "zlo"), [(0, 3), (1, 2), (2, 1), (3, 0)])


def gather_parts(block):
    far = around(block, "tensor", 2)
    ahead = around(block, "tensor", -1)
    behind = around(block, "tensor", 1)
    return [joined([block, ahead, behind]), far]


def scatter_parts(near, far):
    rows = far.shape[0]
    sent_far = around(far.astype(bf16), "tensor", 2)
    sent_ahead = around(near[rows : 2 * rows].astype(bf16), "tensor", 1)
    sent_behind = around(near[2 * rows :].astype(bf16), "tensor", -1)
    kept = near[:rows].astype(f32)
    return kept + sent_far.astype(f32) + sent_ahead.astype(f32) + sent_behind.astype(f32)


def joined(parts, axis=0):
    return jnp.concatenate(parts, axis=axis)


def after_all(values, *others):
    return lax.optimization_barrier((values,) + others)[0]


def sum_tensor(block):
    return (
        block
        + around(block, "tensor", 2)
        + around(block, "tensor", 1)
        + around(block, "tensor", -1)
    )


def layer_norm(values, gain_scale):
    centered = values - jnp.mean(values, axis=-1, keepdims=True)
    variance = jnp.mean(centered * centered, axis=-1, keepdims=True)
    return centered * lax.rsqrt(variance + epsilon) * gain_scale


def doc_layout(doc_lengths, indices):
    doc_ends = jnp.cumsum(doc_lengths)
    passed = indices[:, None] >= doc_ends[None, :]
    doc_ids = jnp.sum(passed.astype(jnp.int32), axis=1)
    starts = jnp.sum(jnp.where(passed, doc_lengths[None, :], 0), axis=1)
    return (doc_ids, indices - starts)


def rope_tables(positions, rope_base, heads):
    half_dim = HEAD_DIM // 2
    inverse = rope_base ** (-2.0 * jnp.arange(half_dim, dtype=f32) / HEAD_DIM)
    angles = positions.astype(f32)[:, None] * inverse
    cosine, sine = jnp.cos(angles), jnp.sin(angles)
    cosine = jnp.concatenate([cosine, cosine], axis=-1)
    sine = jnp.concatenate([-sine, sine], axis=-1)
    return (jnp.tile(cosine, (1, heads)), jnp.tile(sine, (1, heads)))


def contract_rows(left_rows, right_rows):
    return lax.dot_general(
        left_rows, right_rows, (((0,), (0,)), ((), ())), preferred_element_type=f32
    )


def contract_last(left_rows, weight):
    return lax.dot_general(
        left_rows, weight, (((1,), (1,)), ((), ())), preferred_element_type=f32
    )


def times(left_rows, weight):
    return jnp.dot(left_rows, weight, preferred_element_type=f32)


def gelu_product(first_half, second_half):
    return jax.nn.gelu(first_half, approximate=False) * second_half


def dot_nt(left, right):
    return lax.dot_general(left, right, (((1,), (1,)), ((), ())), preferred_element_type=f32)


def dot_tn(left, right):
    return lax.dot_general(left, right, (((0,), (0,)), ((), ())), preferred_element_type=f32)


def swap_halves(values):
    width = values.shape[1]
    lanes = lax.broadcasted_iota(jnp.int32, values.shape, 1)
    up = pltpu.roll(values, width - HEAD_DIM // 2, 1)
    down = pltpu.roll(values, HEAD_DIM // 2, 1)
    return jnp.where(lanes % HEAD_DIM < HEAD_DIM // 2, up, down)


def excluded_bias(marks_row, marks_col, start, windowed):
    docs = marks_row[0:1, pl.ds(start, BLOCK)]
    allowed = marks_col[:, 0:1] == docs
    if windowed:
        apart = marks_col[:, 1:2] - marks_row[1:2, pl.ds(start, BLOCK)]
        allowed = allowed & (jnp.abs(apart) <= WINDOW // 2)
    return jnp.where(allowed, 0.0, -1e30)


def attend_kernel(
    windowed,
    near, far, w_qkv, w_out, cosine, sine, marks_row, marks_col,
    queries, keys, values, logs, attended, near_term, far_term,
    projected,
):
    near_rows = near.shape[0]
    width = w_out.shape[0]
    projected[:near_rows] = jnp.dot(near[...], w_qkv[...], preferred_element_type=f32)
    projected[near_rows:] = jnp.dot(far[...], w_qkv[...], preferred_element_type=f32)
    for index, target in ((0, queries), (1, keys)):
        part = projected[:, index * width : (index + 1) * width]
        turned = part * cosine[...] + swap_halves(part) * sine[...]
        target[...] = turned.astype(bf16)
    values[...] = projected[:, 2 * width :].astype(bf16)
    heads = width // HEAD_DIM
    lanes = lax.broadcasted_iota(jnp.int32, (BLOCK, width), 1) // HEAD_DIM

    def step(index, carry):
        start = pl.multiple_of(index * BLOCK, BLOCK)
        bias = excluded_bias(marks_row, marks_col, start, windowed)
        block = queries[pl.ds(start, BLOCK)] * jnp.asarray(HEAD_DIM ** (-0.5), bf16)
        total = jnp.zeros((BLOCK, width), f32)
        for head in range(heads):
            own = jnp.where(lanes == head, block, jnp.zeros_like(block))
            scores = dot_nt(keys[...], own) + bias
            largest = jnp.max(scores, axis=0, keepdims=True)
            powers = jnp.exp(scores - largest)
            sums = jnp.sum(powers, axis=0, keepdims=True)
            soft = (powers * (1.0 / sums)).astype(bf16)
            logs[pl.ds(head, 1), pl.ds(start, BLOCK)] = largest + jnp.log(sums)
            total = jnp.where(lanes == head, dot_tn(soft, values[...]), total)
        attended[pl.ds(start, BLOCK)] = total.astype(bf16)
        return carry

    lax.fori_loop(0, queries.shape[0] // BLOCK, step, 0)
    far_term[...] = jnp.dot(
        attended[near_rows:], w_out[...], preferred_element_type=f32
    ).astype(bf16)
    near_term[...] = jnp.dot(
        attended[:near_rows], w_out[...], preferred_element_type=f32
    ).astype(bf16)


def attend_back_kernel(
    windowed,
    near, far, w_qkv, w_out, cosine, sine, marks_row, marks_col,
    queries, keys, values, logs,
    grad_projected, near_term, far_term,
    grad_attended, grad_queries, grad_keys, grad_values,
):
    near_rows = near.shape[0]
    width = w_out.shape[0]
    grad_attended[:near_rows] = dot_nt(near[...], w_out[...]).astype(bf16)
    grad_attended[near_rows:] = dot_nt(far[...], w_out[...]).astype(bf16)
    grad_keys[...] = jnp.zeros_like(grad_keys)
    grad_values[...] = jnp.zeros_like(grad_values)
    heads = width // HEAD_DIM
    lanes = lax.broadcasted_iota(jnp.int32, (BLOCK, width), 1) // HEAD_DIM
    all_lanes = lax.broadcasted_iota(jnp.int32, queries.shape, 1) // HEAD_DIM

    def step(index, carry):
        start = pl.multiple_of(index * BLOCK, BLOCK)
        bias = excluded_bias(marks_row, marks_col, start, windowed)
        block = queries[pl.ds(start, BLOCK)] * jnp.asarray(HEAD_DIM ** (-0.5), bf16)
        grad_block = grad_attended[pl.ds(start, BLOCK)]
        total = jnp.zeros((BLOCK, width), f32)
        more_keys = jnp.zeros(queries.shape, f32)
        more_values = jnp.zeros(queries.shape, f32)
        for head in range(heads):
            own = jnp.where(lanes == head, block, jnp.zeros_like(block))
            own_grad = jnp.where(lanes == head, grad_block, jnp.zeros_like(grad_block))
            scores = dot_nt(keys[...], own) + bias
            soft = jnp.exp(scores - logs[pl.ds(head, 1), pl.ds(start, BLOCK)])
            grad_soft = dot_nt(values[...], own_grad)
            dots = jnp.sum(soft * grad_soft, axis=0, keepdims=True)
            grad_scores = (soft * (grad_soft - dots)).astype(bf16)
            more_values += jnp.dot(soft.astype(bf16), own_grad, preferred_element_type=f32)
            more_keys += jnp.dot(grad_scores, own, preferred_element_type=f32)
            total = jnp.where(lanes == head, dot_tn(grad_scores, keys[...]), total)
        grad_queries[pl.ds(start, BLOCK)] = total * HEAD_DIM ** (-0.5)
        grad_keys[...] += more_keys
        grad_values[...] += more_values
        return carry

    lax.fori_loop(0, queries.shape[0] // BLOCK, step, 0)
    for index, source in ((0, grad_queries), (1, grad_keys)):
        part = source[...]
        back = part * cosine[...] - swap_halves(part) * sine[...]
        grad_projected[:, index * width : (index + 1) * width] = back.astype(bf16)
    grad_projected[:, 2 * width :] = grad_values[...].astype(bf16)
    far_term[...] = dot_nt(grad_projected[near_rows:], w_qkv[...]).astype(bf16)
    near_term[...] = dot_nt(grad_projected[:near_rows], w_qkv[...]).astype(bf16)


def whole_call(kernel, out_shapes, scratch_shapes, flops, *operands):
    whole = pl.BlockSpec(memory_space=pltpu.VMEM)
    return pl.pallas_call(
        kernel,
        out_shape=[jax.ShapeDtypeStruct(*shape) for shape in out_shapes],
        in_specs=[whole] * len(operands),
        out_specs=[whole] * len(out_shapes),
        scratch_shapes=scratch_shapes,
        compiler_params=pltpu.CompilerParams(vmem_limit_bytes=40 * 1024 * 1024),
        cost_estimate=pl.CostEstimate(flops=flops, bytes_accessed=8 << 20, transcendentals=1 << 20),
    )(*operands)


def in_turn(work, parts):
    first = work(0, parts[0])
    return first, work(1, after_all(parts[1], first))


def forward_layer(inputs, normed_parts, gain_mid, weights, allowed, tables, late, points):
    w_qkv, w_out = weights[0], weights[1]
    near_rows, model_width = normed_parts[0].shape
    far_rows = normed_parts[1].shape[0]
    full_rows = near_rows + far_rows
    width = w_out.shape[0]
    windowed, marks_row, marks_col = allowed
    queries, keys, values, logs, attended, near_term, far_term = whole_call(
        functools.partial(attend_kernel, windowed),
        [((full_rows, width), bf16)] * 3
        + [((8, full_rows), f32), ((full_rows, width), bf16)]
        + [((near_rows, model_width), bf16), ((far_rows, model_width), bf16)],
        [pltpu.VMEM((full_rows, 3 * width), f32)],
        3 << 30,
        *normed_parts, w_qkv, w_out, *tables, marks_row, marks_col,
    )
    points[1](far_term)
    resid_mid = inputs + scatter_parts(near_term, far_term)
    points[2](resid_mid)
    mid_parts = gather_parts(layer_norm(resid_mid, gain_mid).astype(bf16))
    points[3](mid_parts)
    w_up, w_down = weights[2], weights[3]

    def feed(k, part):
        hidden = contract_last(part, w_up)
        local_hidden = hidden.shape[1] // 2
        gelu_in = hidden[:, :local_hidden]
        gate_mult = hidden[:, local_hidden:]
        mixed = gelu_product(gelu_in, gate_mult).astype(bf16)
        return gelu_in, gate_mult, mixed, None if late else times(mixed, w_down).astype(bf16)

    fed = in_turn(feed, mid_parts)
    if late:

        def result(gate):
            held = after_all((fed[0][2], fed[1][2]), gate)
            return [times(mixed, w_down).astype(bf16) for mixed in held]

    else:
        result = resid_mid + scatter_parts(fed[0][3], fed[1][3])
    kept = dict(
        inputs=inputs,
        resid_mid=resid_mid,
        normed=normed_parts,
        queries=queries,
        keys=keys,
        values=values,
        logs=logs,
        attended=attended,
        normed_mid=mid_parts,
        gelu_in=(fed[0][0], fed[1][0]),
        gate_mult=(fed[0][1], fed[1][1]),
        mixed=(fed[0][2], fed[1][2]),
    )
    return (result, kept)


def backward_ffn(grad_result, kept, gain_mid, weights, gate):
    w_up, w_down = weights[2], weights[3]
    grad_parts = after_all(gather_parts(grad_result.astype(bf16)), gate)

    def feed_back(k, part):
        grad_mixed = contract_last(part, w_down)
        unused, pull_gelu = jax.vjp(gelu_product, kept["gelu_in"][k], kept["gate_mult"][k])
        terms = tuple(term.astype(bf16) for term in pull_gelu(grad_mixed))
        return terms[0], terms[1], times(joined(terms, 1), w_up).astype(bf16)

    near, far = in_turn(feed_back, grad_parts)
    grad_normed_mid = scatter_parts(near[2], far[2])
    unused, pull_norm = jax.vjp(layer_norm, kept["resid_mid"], gain_mid)
    grad_resid, grad_gain = pull_norm(grad_normed_mid)

    def weight_grads(gate):
        outer, inner, left, first, second = after_all(
            (grad_parts, kept["mixed"], kept["normed_mid"], (near[0], far[0]), (near[1], far[1])),
            gate,
        )
        outer, inner, left = joined(outer), joined(inner), joined(left)
        first, second = joined(first), joined(second)
        half = inner.shape[1] // 2
        front, back = inner[:, :half], inner[:, half:]
        sent_up, add_up = add_core(lambda core: contract_rows(core(first, second), left))
        sent_down, add_down = add_core(lambda core: contract_rows(core(front, back), outer))

        def pack(gate):
            up, down = add_up(gate), add_down(gate)
            rows = up.shape[0] + down.shape[0]
            blank = jnp.zeros((-rows % 128, up.shape[1]), bf16)
            return joined([up, down, blank])

        return (sent_up, sent_down), pack

    return (grad_result + grad_resid, weight_grads, grad_gain)


def backward_attn(grad_mid, kept, gain_first, weights, allowed, tables, gate, pack):
    w_qkv, w_out = weights[0], weights[1]
    grad_parts = gather_parts(grad_mid.astype(bf16))
    near, far = after_all(grad_parts, gate)
    full_rows, width = kept["queries"].shape
    windowed, marks_row, marks_col = allowed
    grad_projected, near_term, far_term = whole_call(
        functools.partial(attend_back_kernel, windowed),
        [((full_rows, 3 * width), bf16), (near.shape, bf16), (far.shape, bf16)],
        [pltpu.VMEM((full_rows, width), bf16)] + [pltpu.VMEM((full_rows, width), f32)] * 3,
        4 << 30,
        near, far, w_qkv, w_out, *tables, marks_row, marks_col,
        kept["queries"], kept["keys"], kept["values"], kept["logs"],
    )
    packed = pack(grad_projected)
    near_term, far_term = after_all((near_term, far_term), packed)
    grad_normed = scatter_parts(near_term, far_term)
    unused, pull_norm = jax.vjp(layer_norm, kept["inputs"], gain_first)
    grad_resid, grad_gain = pull_norm(grad_normed)

    def gain_before():
        total = 0.0
        for term, normed in zip((near_term, far_term), kept["normed"]):
            total = total + jnp.sum(term.astype(f32) * normed.astype(f32), axis=0)
        return total / gain_first

    def weight_grads(gate, gains):
        outer, inner, left, right = after_all(
            (grad_parts, kept["attended"], kept["normed"], grad_projected), gate
        )
        outer, left = joined(outer), joined(left)
        width = inner.shape[1]
        of_q, of_k, of_v = (right[:, i * width : (i + 1) * width] for i in range(3))
        one = add_core(lambda core: contract_rows(left, core(of_q, of_v)))[1](())
        two = add_core(lambda core: contract_rows(core(left, outer), core(of_k, inner)))[1](())
        extra = jnp.stack(gains).astype(bf16).reshape(-1, width)
        blank = jnp.zeros((-extra.shape[0] % 128, width), bf16)
        return joined([one, two, extra, blank])

    return (grad_mid + grad_resid, weight_grads, grad_gain, gain_before, packed)


def fetch_half(own, after):
    piece = own.shape[0] // 2
    start = lax.axis_index("core") * piece
    return swap_layer(lax.dynamic_slice_in_dim(after_all(own, after), start, piece))


def both_halves(half, after=()):
    half = after_all(half, after)
    return in_order(lax.axis_index("core"), half, swap_core(half))


def by_layer(is_first, own, other):
    return jnp.where(is_first, own, other), jnp.where(is_first, other, own)


def in_order(index, mine, other):
    low = jnp.where(index == 0, mine, other)
    high = jnp.where(index == 0, other, mine)
    return jnp.concatenate([low, high], axis=0)


def add_core(product):
    is_core0 = lax.axis_index("core") == 0
    sent = product(lambda one, two: jnp.where(is_core0, two, one)).astype(bf16)

    def add(gate):
        held = product(lambda one, two: after_all(jnp.where(is_core0, one, two), gate))
        return (held + swap_core(sent).astype(f32)).astype(bf16)

    return sent, add


def reduce_part(grads):
    return lax.psum_scatter(grads, ("zlo", "x"), scatter_dimension=0, tiled=True)


def reduce_part_now(grads):
    pieces = lax.all_to_all(grads, ("zlo", "x"), 0, 0, tiled=True)
    pieces = pieces.reshape(8, -1, pieces.shape[1])
    return jnp.sum(pieces.astype(f32), axis=0).astype(bf16)


def spread_part(part):
    copies = jnp.broadcast_to(part[None], (8,) + part.shape).reshape(-1, part.shape[1])
    return lax.all_to_all(copies, ("zlo", "x"), 0, 0, tiled=True)


def pick_sections(is_first, part_first, part_second):
    own = jnp.where(is_first, part_first, part_second)
    sent = jnp.where(is_first, part_second, part_first)
    return own, sent


def local(tokens, cotangent, lengths, gains, w_qkv, w_out, w_up, w_down):
    section_index = lax.axis_index("section")
    is_first = section_index == 0
    row_count = tokens.shape[1]
    full_rows = row_count * lax.axis_size("tensor")
    start_rows = jnp.where(is_first, tokens[0], tokens[1])
    end_grads = jnp.where(is_first, cotangent[0], cotangent[1])
    start_parts = gather_parts(start_rows)
    gains_other = swap_layer(gains[0])
    gains0 = jnp.where(is_first, gains[0], gains_other)
    gains1 = jnp.where(is_first, gains_other, gains[0])
    start_rows = start_rows.astype(f32)
    own = (
        jnp.transpose(w_qkv[0], (1, 0, 2)).reshape(-1, w_qkv.shape[3]),
        w_out[0],
        jnp.transpose(w_up[0], (1, 2, 0)).reshape(-1, w_up.shape[1]),
        w_down[0],
    )
    half_qkv = fetch_half(own[0], ())
    half_out = fetch_half(own[1], ())
    start_parts, lengths = after_all((start_parts, lengths), (half_qkv, half_out))
    first_parts = in_turn(
        lambda k, part: layer_norm(part.astype(f32), gains0[0]).astype(bf16), start_parts
    )
    qkv0, qkv1 = by_layer(is_first, own[0], both_halves(half_qkv))
    layer0 = [joined(jnp.split(qkv0, 3), 1)]
    layer1 = [joined(jnp.split(qkv1, 3), 1)]
    hidden_width = w_up.shape[3]
    moving = []

    out0, out1 = by_layer(is_first, own[1], both_halves(half_out))
    layer0.append(out0)
    layer1.append(out1)
    moving.append(fetch_half(own[2][:hidden_width], half_out))

    def at_far_term(far_term):
        moving.append(both_halves(moving[0], far_term))
        moving.append(fetch_half(own[2][hidden_width:], (moving[0], far_term)))

    def at_mid(resid_mid):
        moving.append(both_halves(moving[2], resid_mid))
        moving.append(fetch_half(own[3], (moving[2], resid_mid)))

    def at_gathered(parts):
        up0, up1 = by_layer(is_first, own[2], joined([moving[1], moving[3]]))
        down0, down1 = by_layer(is_first, own[3], both_halves(moving[4], parts))
        layer0.extend([up0, down0])
        layer1.extend([up1, down1])

    points = (None, at_far_term, at_mid, at_gathered)

    doc_lengths = jnp.where(is_first, lengths[0, 0], lengths[1, 0])
    indices = jnp.arange(full_rows, dtype=jnp.int32)
    blocks = jnp.array([0, 1, 3, 2], jnp.int32) + lax.axis_index("tensor")
    indices = (jnp.repeat(blocks, row_count) * row_count + indices % row_count) % full_rows
    doc_ids, positions = doc_layout(doc_lengths, indices)
    marks_row = jnp.stack([doc_ids, indices])
    marks_col = jnp.stack([doc_ids, indices], axis=1)
    allowed0 = (True, marks_row, marks_col)
    allowed1 = (False, marks_row, marks_col)
    heads = w_out.shape[1] // HEAD_DIM
    tables0 = rope_tables(positions, 10000.0, heads)
    tables1 = rope_tables(positions, 160000.0, heads)

    out0, kept0 = forward_layer(
        start_rows, first_parts, gains0[1], layer0, allowed0, tables0, False, points
    )
    out0 = out0.astype(bf16)
    second_rows = out0.astype(f32)
    second_parts = gather_parts(layer_norm(second_rows, gains1[0]).astype(bf16))
    out1_of, kept1 = forward_layer(
        second_rows, second_parts, gains1[1], layer1, allowed1, tables1, True, (lambda value: None,) * 4
    )
    mid1, ffn_grads1, gain_mid1 = backward_ffn(
        end_grads.astype(f32), kept1, gains1[1], layer1, ()
    )
    ffn_sent1, ffn_pack1 = ffn_grads1(mid1)
    in1, attn_grads1, gain_first1, unused, unused = backward_attn(
        mid1, kept1, gains1[0], layer1, allowed1, tables1, ffn_sent1, lambda gate: ()
    )
    in1 = in1.astype(bf16)
    ffn_pack1 = ffn_pack1(in1)
    mid0, ffn_grads0, gain_mid0 = backward_ffn(
        in1.astype(f32), kept0, gains0[1], layer0, ffn_pack1
    )
    model_width = w_qkv.shape[1]
    ffn1 = reduce_part(ffn_pack1)
    ffn_sent0, ffn_pack0 = ffn_grads0(mid0)
    in0, attn_grads0, unused, gain_before, (ffn_pack0, unused) = backward_attn(
        mid0, kept0, gains0[0], layer0, allowed0, tables0, ffn_sent0,
        lambda gate: (ffn_pack0(gate), ffn1),
    )
    in0 = in0.astype(bf16)
    ffn0 = reduce_part_now(ffn_pack0)
    attn_pack1 = attn_grads1(in1, [gain_first1, gain_mid1])
    attn_pack0 = attn_grads0((), [gain_before(), gain_mid0])
    out1_terms = out1_of(ffn_pack0)
    out1 = (kept1["resid_mid"] + scatter_parts(*out1_terms)).astype(bf16)
    attn_width = attn_pack0.shape[1]
    packs = [pack.reshape(8, -1, attn_width) for pack in (attn_pack0, attn_pack1)]
    attn_rows = packs[0].shape[1]
    attn_both = reduce_part_now(joined(packs, 1).reshape(-1, attn_width))
    gain_start = 2 * model_width % attn_rows
    holds_gains = lax.axis_index(("zlo", "x")) == 2 * model_width // attn_rows
    attn_both = attn_both.reshape(2, attn_rows, attn_width)
    gain_rows = attn_both[:, gain_start : gain_start + 8]
    gain_sums = sum_tensor(gain_rows.astype(f32)).astype(bf16)
    gain_rows = jnp.where(holds_gains, gain_sums, gain_rows)
    attn_both = joined(
        [attn_both[:, :gain_start], gain_rows, attn_both[:, gain_start + 8 :]], 1
    )
    got_out = swap_section(jnp.where(is_first, out1, out0))
    got_in = swap_section(jnp.where(is_first, in1, in0))
    part0 = joined([ffn0, attn_both[0].reshape(-1, model_width)])
    part1 = joined([ffn1, attn_both[1].reshape(-1, model_width)])
    own_part, sent_part = pick_sections(is_first, part0, part1)
    sent_part = after_all(sent_part, got_in, got_out)
    part = (own_part.astype(f32) + swap_section(sent_part).astype(f32)).astype(bf16)
    ffn_rows = ffn0.shape[0]
    ffn_half = spread_part(part[:ffn_rows])
    attn_part = after_all(part[ffn_rows:].reshape(-1, attn_width), ffn_half)
    attn_half = spread_part(attn_part)
    is_core0 = lax.axis_index("core") == 0

    def of_core(core, halves, start, count):
        mine, other = (both[start : start + count] for both in halves)
        return jnp.where(is_core0 == (core == 0), mine, other).astype(f32)

    ffn_halves = (ffn_half, swap_core(ffn_half))
    down_rows = w_down.shape[1] // 2
    grad_up = jnp.stack([of_core(core, ffn_halves, 0, hidden_width) for core in range(2)])
    grad_down = joined(
        [of_core(core, ffn_halves, hidden_width, down_rows) for core in range(2)]
    )
    attn_half, grad_up, grad_down = lax.optimization_barrier((attn_half, grad_up, grad_down))
    attn_halves = (attn_half, swap_core(attn_half))
    gain_total = sum(of_core(core, attn_halves, 2 * model_width, 8) for core in range(2))
    gain_total = gain_total.reshape(2, -1)
    grad_qkv = jnp.stack(
        [
            of_core(0, attn_halves, 0, model_width),
            of_core(0, attn_halves, model_width, model_width),
            of_core(1, attn_halves, 0, model_width),
        ]
    )
    grad_out = of_core(1, attn_halves, model_width, model_width).T

    section_out = jnp.stack(
        [jnp.where(is_first, out0, got_out), jnp.where(is_first, got_out, out1)]
    )
    input_grads = jnp.stack(
        [jnp.where(is_first, in0, got_in), jnp.where(is_first, got_in, in1)]
    )
    return (
        section_out[None],
        input_grads[None],
        gain_total[None],
        jnp.transpose(grad_qkv, (1, 0, 2))[None],
        grad_out[None],
        jnp.transpose(grad_up, (2, 0, 1))[None],
        grad_down[None],
    )


def solution(mesh):
    sizes = dict(zip(mesh.axis_names, mesh.devices.shape))
    fine = Mesh(
        mesh.devices.reshape(sizes["section"], 2, sizes["dp"] // 4, 2, sizes["tensor"]),
        ("section", "zlo", "x", "core", "tensor"),
    )
    rows = ("zlo", "x", "core", "tensor")
    in_specs = (
        P(None, rows, None),
        P(None, rows, None),
        P(None, DP, None),
        P("section", None, None),
        P("section", None, None, "tensor"),
        P("section", "tensor", None),
        P("section", None, None, "tensor"),
        P("section", "tensor", None),
    )
    out_specs = (
        P("section", None, rows, None),
        P("section", None, rows, None),
        P("section", None, None),
        P("section", None, None, "tensor"),
        P("section", "tensor", None),
        P("section", None, None, "tensor"),
        P("section", "tensor", None),
    )
    return jax.shard_map(local, mesh=fine, in_specs=in_specs, out_specs=out_specs, check_vma=False)
```

```python
import functools

import jax
import jax.numpy as jnp
from jax import lax
from jax.experimental import pallas as pl
from jax.experimental.pallas import tpu as pltpu
from jax.sharding import Mesh
from jax.sharding import PartitionSpec as P

HEAD_DIM = 64
WINDOW = 128

epsilon = 1e-05
bf16 = jnp.bfloat16
f32 = jnp.float32

BLOCK = 256

DP = ("zlo", "x", "core")


def around(block, axis, distance):
    count = lax.axis_size(axis)
    return lax.ppermute(block, axis, [(i, (i + distance) % count) for i in range(count)])


def swap_core(block):
    return lax.ppermute(block, "core", [(0, 1), (1, 0)])


def swap_section(block):
    return lax.ppermute(block, "section", [(0, 1), (1, 0)])


def swap_layer(block):
    return lax.ppermute(block, ("section", "zlo"), [(0, 3), (1, 2), (2, 1), (3, 0)])


def gather_parts(block):
    far = around(block, "tensor", 2)
    ahead = around(block, "tensor", -1)
    behind = around(block, "tensor", 1)
    return [joined([block, ahead, behind]), far]


def scatter_parts(near, far):
    rows = far.shape[0]
    sent_far = around(far.astype(bf16), "tensor", 2)
    sent_ahead = around(near[rows : 2 * rows].astype(bf16), "tensor", 1)
    sent_behind = around(near[2 * rows :].astype(bf16), "tensor", -1)
    kept = near[:rows].astype(f32)
    return kept + sent_far.astype(f32) + sent_ahead.astype(f32) + sent_behind.astype(f32)


def joined(parts, axis=0):
    return jnp.concatenate(parts, axis=axis)


def after_all(values, *others):
    return lax.optimization_barrier((values,) + others)[0]


def sum_tensor(block):
    return (
        block
        + around(block, "tensor", 2)
        + around(block, "tensor", 1)
        + around(block, "tensor", -1)
    )


def layer_norm(values, gain_scale):
    centered = values - jnp.mean(values, axis=-1, keepdims=True)
    variance = jnp.mean(centered * centered, axis=-1, keepdims=True)
    return centered * lax.rsqrt(variance + epsilon) * gain_scale


def doc_layout(doc_lengths, indices):
    doc_ends = jnp.cumsum(doc_lengths)
    passed = indices[:, None] >= doc_ends[None, :]
    doc_ids = jnp.sum(passed.astype(jnp.int32), axis=1)
    starts = jnp.sum(jnp.where(passed, doc_lengths[None, :], 0), axis=1)
    return (doc_ids, indices - starts)


def rope_tables(positions, rope_base, heads):
    half_dim = HEAD_DIM // 2
    inverse = rope_base ** (-2.0 * jnp.arange(half_dim, dtype=f32) / HEAD_DIM)
    angles = positions.astype(f32)[:, None] * inverse
    cosine, sine = jnp.cos(angles), jnp.sin(angles)
    cosine = jnp.concatenate([cosine, cosine], axis=-1)
    sine = jnp.concatenate([-sine, sine], axis=-1)
    return (jnp.tile(cosine, (1, heads)), jnp.tile(sine, (1, heads)))


def contract_rows(left_rows, right_rows):
    return lax.dot_general(
        left_rows, right_rows, (((0,), (0,)), ((), ())), preferred_element_type=f32
    )


def contract_last(left_rows, weight):
    return lax.dot_general(
        left_rows, weight, (((1,), (1,)), ((), ())), preferred_element_type=f32
    )


def times(left_rows, weight):
    return jnp.dot(left_rows, weight, preferred_element_type=f32)


def gelu_product(first_half, second_half):
    return jax.nn.gelu(first_half, approximate=False) * second_half


def dot_nt(left, right):
    return lax.dot_general(left, right, (((1,), (1,)), ((), ())), preferred_element_type=f32)


def dot_tn(left, right):
    return lax.dot_general(left, right, (((0,), (0,)), ((), ())), preferred_element_type=f32)


def swap_halves(values):
    width = values.shape[1]
    lanes = lax.broadcasted_iota(jnp.int32, values.shape, 1)
    up = pltpu.roll(values, width - HEAD_DIM // 2, 1)
    down = pltpu.roll(values, HEAD_DIM // 2, 1)
    return jnp.where(lanes % HEAD_DIM < HEAD_DIM // 2, up, down)


def excluded_bias(marks_row, marks_col, start, windowed):
    docs = marks_row[0:1, pl.ds(start, BLOCK)]
    allowed = marks_col[:, 0:1] == docs
    if windowed:
        apart = marks_col[:, 1:2] - marks_row[1:2, pl.ds(start, BLOCK)]
        allowed = allowed & (jnp.abs(apart) <= WINDOW // 2)
    return jnp.where(allowed, 0.0, -1e30)


def attend_kernel(
    windowed,
    near, far, w_qkv, w_out, cosine, sine, marks_row, marks_col,
    queries, keys, values, logs, attended, near_term, far_term,
    projected,
):
    near_rows = near.shape[0]
    width = w_out.shape[0]
    projected[:near_rows] = jnp.dot(near[...], w_qkv[...], preferred_element_type=f32)
    projected[near_rows:] = jnp.dot(far[...], w_qkv[...], preferred_element_type=f32)
    for index, target in ((0, queries), (1, keys)):
        part = projected[:, index * width : (index + 1) * width]
        turned = part * cosine[...] + swap_halves(part) * sine[...]
        target[...] = turned.astype(bf16)
    values[...] = projected[:, 2 * width :].astype(bf16)
    heads = width // HEAD_DIM
    lanes = lax.broadcasted_iota(jnp.int32, (BLOCK, width), 1) // HEAD_DIM

    def step(index, carry):
        start = pl.multiple_of(index * BLOCK, BLOCK)
        bias = excluded_bias(marks_row, marks_col, start, windowed)
        block = queries[pl.ds(start, BLOCK)] * jnp.asarray(HEAD_DIM ** (-0.5), bf16)
        total = jnp.zeros((BLOCK, width), f32)
        for head in range(heads):
            own = jnp.where(lanes == head, block, jnp.zeros_like(block))
            scores = dot_nt(keys[...], own) + bias
            largest = jnp.max(scores, axis=0, keepdims=True)
            powers = jnp.exp(scores - largest)
            sums = jnp.sum(powers, axis=0, keepdims=True)
            soft = (powers * (1.0 / sums)).astype(bf16)
            logs[pl.ds(head, 1), pl.ds(start, BLOCK)] = largest + jnp.log(sums)
            total = jnp.where(lanes == head, dot_tn(soft, values[...]), total)
        attended[pl.ds(start, BLOCK)] = total.astype(bf16)
        return carry

    lax.fori_loop(0, queries.shape[0] // BLOCK, step, 0)
    far_term[...] = jnp.dot(
        attended[near_rows:], w_out[...], preferred_element_type=f32
    ).astype(bf16)
    near_term[...] = jnp.dot(
        attended[:near_rows], w_out[...], preferred_element_type=f32
    ).astype(bf16)


def attend_back_kernel(
    windowed,
    near, far, w_qkv, w_out, cosine, sine, marks_row, marks_col,
    queries, keys, values, logs,
    grad_projected, near_term, far_term,
    grad_attended, grad_queries, grad_keys, grad_values,
):
    near_rows = near.shape[0]
    width = w_out.shape[0]
    grad_attended[:near_rows] = dot_nt(near[...], w_out[...]).astype(bf16)
    grad_attended[near_rows:] = dot_nt(far[...], w_out[...]).astype(bf16)
    grad_keys[...] = jnp.zeros_like(grad_keys)
    grad_values[...] = jnp.zeros_like(grad_values)
    heads = width // HEAD_DIM
    lanes = lax.broadcasted_iota(jnp.int32, (BLOCK, width), 1) // HEAD_DIM
    all_lanes = lax.broadcasted_iota(jnp.int32, queries.shape, 1) // HEAD_DIM

    def step(index, carry):
        start = pl.multiple_of(index * BLOCK, BLOCK)
        bias = excluded_bias(marks_row, marks_col, start, windowed)
        block = queries[pl.ds(start, BLOCK)] * jnp.asarray(HEAD_DIM ** (-0.5), bf16)
        grad_block = grad_attended[pl.ds(start, BLOCK)]
        total = jnp.zeros((BLOCK, width), f32)
        more_keys = jnp.zeros(queries.shape, f32)
        more_values = jnp.zeros(queries.shape, f32)
        for head in range(heads):
            own = jnp.where(lanes == head, block, jnp.zeros_like(block))
            own_grad = jnp.where(lanes == head, grad_block, jnp.zeros_like(grad_block))
            scores = dot_nt(keys[...], own) + bias
            soft = jnp.exp(scores - logs[pl.ds(head, 1), pl.ds(start, BLOCK)])
            grad_soft = dot_nt(values[...], own_grad)
            dots = jnp.sum(soft * grad_soft, axis=0, keepdims=True)
            grad_scores = (soft * (grad_soft - dots)).astype(bf16)
            more_values += jnp.dot(soft.astype(bf16), own_grad, preferred_element_type=f32)
            more_keys += jnp.dot(grad_scores, own, preferred_element_type=f32)
            total = jnp.where(lanes == head, dot_tn(grad_scores, keys[...]), total)
        grad_queries[pl.ds(start, BLOCK)] = total * HEAD_DIM ** (-0.5)
        grad_keys[...] += more_keys
        grad_values[...] += more_values
        return carry

    lax.fori_loop(0, queries.shape[0] // BLOCK, step, 0)
    for index, source in ((0, grad_queries), (1, grad_keys)):
        part = source[...]
        back = part * cosine[...] - swap_halves(part) * sine[...]
        grad_projected[:, index * width : (index + 1) * width] = back.astype(bf16)
    grad_projected[:, 2 * width :] = grad_values[...].astype(bf16)
    far_term[...] = dot_nt(grad_projected[near_rows:], w_qkv[...]).astype(bf16)
    near_term[...] = dot_nt(grad_projected[:near_rows], w_qkv[...]).astype(bf16)


def whole_call(kernel, out_shapes, scratch_shapes, flops, *operands):
    whole = pl.BlockSpec(memory_space=pltpu.VMEM)
    return pl.pallas_call(
        kernel,
        out_shape=[jax.ShapeDtypeStruct(*shape) for shape in out_shapes],
        in_specs=[whole] * len(operands),
        out_specs=[whole] * len(out_shapes),
        scratch_shapes=scratch_shapes,
        compiler_params=pltpu.CompilerParams(vmem_limit_bytes=40 * 1024 * 1024),
        cost_estimate=pl.CostEstimate(flops=flops, bytes_accessed=8 << 20, transcendentals=1 << 20),
    )(*operands)


def in_turn(work, parts):
    first = work(0, parts[0])
    return first, work(1, after_all(parts[1], first))


def forward_layer(inputs, normed_parts, gain_mid, weights, allowed, tables, late, points):
    w_qkv, w_out = weights[0], weights[1]
    near_rows, model_width = normed_parts[0].shape
    far_rows = normed_parts[1].shape[0]
    full_rows = near_rows + far_rows
    width = w_out.shape[0]
    windowed, marks_row, marks_col = allowed
    queries, keys, values, logs, attended, near_term, far_term = whole_call(
        functools.partial(attend_kernel, windowed),
        [((full_rows, width), bf16)] * 3
        + [((8, full_rows), f32), ((full_rows, width), bf16)]
        + [((near_rows, model_width), bf16), ((far_rows, model_width), bf16)],
        [pltpu.VMEM((full_rows, 3 * width), f32)],
        3 << 30,
        *normed_parts, w_qkv, w_out, *tables, marks_row, marks_col,
    )
    points[1](far_term)
    resid_mid = inputs + scatter_parts(near_term, far_term)
    points[2](resid_mid)
    mid_parts = gather_parts(layer_norm(resid_mid, gain_mid).astype(bf16))
    points[3](mid_parts)
    w_up, w_down = weights[2], weights[3]

    def feed(k, part):
        hidden = contract_last(part, w_up)
        local_hidden = hidden.shape[1] // 2
        gelu_in = hidden[:, :local_hidden]
        gate_mult = hidden[:, local_hidden:]
        mixed = gelu_product(gelu_in, gate_mult).astype(bf16)
        return gelu_in, gate_mult, mixed, None if late else times(mixed, w_down).astype(bf16)

    fed = in_turn(feed, mid_parts)
    if late:

        def result(gate):
            held = after_all((fed[0][2], fed[1][2]), gate)
            return [times(mixed, w_down).astype(bf16) for mixed in held]

    else:
        result = resid_mid + scatter_parts(fed[0][3], fed[1][3])
    kept = dict(
        inputs=inputs,
        resid_mid=resid_mid,
        normed=normed_parts,
        queries=queries,
        keys=keys,
        values=values,
        logs=logs,
        attended=attended,
        normed_mid=mid_parts,
        gelu_in=(fed[0][0], fed[1][0]),
        gate_mult=(fed[0][1], fed[1][1]),
        mixed=(fed[0][2], fed[1][2]),
    )
    return (result, kept)


def backward_ffn(grad_result, kept, gain_mid, weights, gate):
    w_up, w_down = weights[2], weights[3]
    grad_parts = after_all(gather_parts(grad_result.astype(bf16)), gate)

    def feed_back(k, part):
        grad_mixed = contract_last(part, w_down)
        unused, pull_gelu = jax.vjp(gelu_product, kept["gelu_in"][k], kept["gate_mult"][k])
        terms = tuple(term.astype(bf16) for term in pull_gelu(grad_mixed))
        return terms[0], terms[1], times(joined(terms, 1), w_up).astype(bf16)

    near, far = in_turn(feed_back, grad_parts)
    grad_normed_mid = scatter_parts(near[2], far[2])
    unused, pull_norm = jax.vjp(layer_norm, kept["resid_mid"], gain_mid)
    grad_resid, grad_gain = pull_norm(grad_normed_mid)

    def weight_grads(gate):
        outer, inner, left, first, second = after_all(
            (grad_parts, kept["mixed"], kept["normed_mid"], (near[0], far[0]), (near[1], far[1])),
            gate,
        )
        outer, inner, left = joined(outer), joined(inner), joined(left)
        first, second = joined(first), joined(second)
        half = inner.shape[1] // 2
        front, back = inner[:, :half], inner[:, half:]
        sent_up, add_up = add_core(lambda core: contract_rows(core(first, second), left))
        sent_down, add_down = add_core(lambda core: contract_rows(core(front, back), outer))

        def pack(gate):
            up, down = add_up(gate), add_down(gate)
            rows = up.shape[0] + down.shape[0]
            blank = jnp.zeros((-rows % 128, up.shape[1]), bf16)
            return joined([up, down, blank])

        return (sent_up, sent_down), pack

    return (grad_result + grad_resid, weight_grads, grad_gain)


def backward_attn(grad_mid, kept, gain_first, weights, allowed, tables, gate, pack):
    w_qkv, w_out = weights[0], weights[1]
    grad_parts = gather_parts(grad_mid.astype(bf16))
    near, far = after_all(grad_parts, gate)
    full_rows, width = kept["queries"].shape
    windowed, marks_row, marks_col = allowed
    grad_projected, near_term, far_term = whole_call(
        functools.partial(attend_back_kernel, windowed),
        [((full_rows, 3 * width), bf16), (near.shape, bf16), (far.shape, bf16)],
        [pltpu.VMEM((full_rows, width), bf16)] + [pltpu.VMEM((full_rows, width), f32)] * 3,
        4 << 30,
        near, far, w_qkv, w_out, *tables, marks_row, marks_col,
        kept["queries"], kept["keys"], kept["values"], kept["logs"],
    )
    packed = pack(grad_projected)
    near_term, far_term = after_all((near_term, far_term), packed)
    grad_normed = scatter_parts(near_term, far_term)
    unused, pull_norm = jax.vjp(layer_norm, kept["inputs"], gain_first)
    grad_resid, grad_gain = pull_norm(grad_normed)

    def gain_before():
        total = 0.0
        for term, normed in zip((near_term, far_term), kept["normed"]):
            total = total + jnp.sum(term.astype(f32) * normed.astype(f32), axis=0)
        return total / gain_first

    def weight_grads(gate, gains):
        outer, inner, left, right = after_all(
            (grad_parts, kept["attended"], kept["normed"], grad_projected), gate
        )
        outer, left = joined(outer), joined(left)
        width = inner.shape[1]
        of_q, of_k, of_v = (right[:, i * width : (i + 1) * width] for i in range(3))
        one = add_core(lambda core: contract_rows(left, core(of_q, of_v)))[1](())
        two = add_core(lambda core: contract_rows(core(left, outer), core(of_k, inner)))[1](())
        extra = jnp.stack(gains).astype(bf16).reshape(-1, width)
        blank = jnp.zeros((-extra.shape[0] % 128, width), bf16)
        return joined([one, two, extra, blank])

    return (grad_mid + grad_resid, weight_grads, grad_gain, gain_before, packed)


def fetch_half(own, after):
    piece = own.shape[0] // 2
    start = lax.axis_index("core") * piece
    return swap_layer(lax.dynamic_slice_in_dim(after_all(own, after), start, piece))


def both_halves(half, after=()):
    half = after_all(half, after)
    return in_order(lax.axis_index("core"), half, swap_core(half))


def by_layer(is_first, own, other):
    return jnp.where(is_first, own, other), jnp.where(is_first, other, own)


def in_order(index, mine, other):
    low = jnp.where(index == 0, mine, other)
    high = jnp.where(index == 0, other, mine)
    return jnp.concatenate([low, high], axis=0)


def add_core(product):
    is_core0 = lax.axis_index("core") == 0
    sent = product(lambda one, two: jnp.where(is_core0, two, one)).astype(bf16)

    def add(gate):
        held = product(lambda one, two: after_all(jnp.where(is_core0, one, two), gate))
        return (held + swap_core(sent).astype(f32)).astype(bf16)

    return sent, add


def reduce_part(grads):
    return lax.psum_scatter(grads, ("zlo", "x"), scatter_dimension=0, tiled=True)


def reduce_part_now(grads):
    pieces = lax.all_to_all(grads, ("zlo", "x"), 0, 0, tiled=True)
    pieces = pieces.reshape(8, -1, pieces.shape[1])
    return jnp.sum(pieces.astype(f32), axis=0).astype(bf16)


def spread_part(part):
    copies = jnp.broadcast_to(part[None], (8,) + part.shape).reshape(-1, part.shape[1])
    return lax.all_to_all(copies, ("zlo", "x"), 0, 0, tiled=True)


def pick_sections(is_first, part_first, part_second):
    own = jnp.where(is_first, part_first, part_second)
    sent = jnp.where(is_first, part_second, part_first)
    return own, sent


def local(tokens, cotangent, lengths, gains, w_qkv, w_out, w_up, w_down):
    section_index = lax.axis_index("section")
    is_first = section_index == 0
    row_count = tokens.shape[1]
    full_rows = row_count * lax.axis_size("tensor")
    start_rows = jnp.where(is_first, tokens[0], tokens[1])
    end_grads = jnp.where(is_first, cotangent[0], cotangent[1])
    start_parts = gather_parts(start_rows)
    gains_other = swap_layer(gains[0])
    gains0 = jnp.where(is_first, gains[0], gains_other)
    gains1 = jnp.where(is_first, gains_other, gains[0])
    start_rows = start_rows.astype(f32)
    own = (
        jnp.transpose(w_qkv[0], (1, 0, 2)).reshape(-1, w_qkv.shape[3]),
        w_out[0],
        jnp.transpose(w_up[0], (1, 2, 0)).reshape(-1, w_up.shape[1]),
        w_down[0],
    )
    half_qkv = fetch_half(own[0], ())
    half_out = fetch_half(own[1], ())
    start_parts, lengths = after_all((start_parts, lengths), (half_qkv, half_out))
    first_parts = in_turn(
        lambda k, part: layer_norm(part.astype(f32), gains0[0]).astype(bf16), start_parts
    )
    qkv0, qkv1 = by_layer(is_first, own[0], both_halves(half_qkv))
    layer0 = [joined(jnp.split(qkv0, 3), 1)]
    layer1 = [joined(jnp.split(qkv1, 3), 1)]
    hidden_width = w_up.shape[3]
    moving = []

    out0, out1 = by_layer(is_first, own[1], both_halves(half_out))
    layer0.append(out0)
    layer1.append(out1)
    moving.append(fetch_half(own[2][:hidden_width], half_out))

    def at_far_term(far_term):
        moving.append(both_halves(moving[0], far_term))
        moving.append(fetch_half(own[2][hidden_width:], (moving[0], far_term)))

    def at_mid(resid_mid):
        moving.append(both_halves(moving[2], resid_mid))
        moving.append(fetch_half(own[3], (moving[2], resid_mid)))

    def at_gathered(parts):
        up0, up1 = by_layer(is_first, own[2], joined([moving[1], moving[3]]))
        down0, down1 = by_layer(is_first, own[3], both_halves(moving[4], parts))
        layer0.extend([up0, down0])
        layer1.extend([up1, down1])

    points = (None, at_far_term, at_mid, at_gathered)

    doc_lengths = jnp.where(is_first, lengths[0, 0], lengths[1, 0])
    indices = jnp.arange(full_rows, dtype=jnp.int32)
    blocks = jnp.array([0, 1, 3, 2], jnp.int32) + lax.axis_index("tensor")
    indices = (jnp.repeat(blocks, row_count) * row_count + indices % row_count) % full_rows
    doc_ids, positions = doc_layout(doc_lengths, indices)
    marks_row = jnp.stack([doc_ids, indices])
    marks_col = jnp.stack([doc_ids, indices], axis=1)
    allowed0 = (True, marks_row, marks_col)
    allowed1 = (False, marks_row, marks_col)
    heads = w_out.shape[1] // HEAD_DIM
    tables0 = rope_tables(positions, 10000.0, heads)
    tables1 = rope_tables(positions, 160000.0, heads)

    out0, kept0 = forward_layer(
        start_rows, first_parts, gains0[1], layer0, allowed0, tables0, False, points
    )
    out0 = out0.astype(bf16)
    second_rows = out0.astype(f32)
    second_parts = gather_parts(layer_norm(second_rows, gains1[0]).astype(bf16))
    out1_of, kept1 = forward_layer(
        second_rows, second_parts, gains1[1], layer1, allowed1, tables1, True, (lambda value: None,) * 4
    )
    mid1, ffn_grads1, gain_mid1 = backward_ffn(
        end_grads.astype(f32), kept1, gains1[1], layer1, ()
    )
    ffn_sent1, ffn_pack1 = ffn_grads1(mid1)
    in1, attn_grads1, gain_first1, unused, unused = backward_attn(
        mid1, kept1, gains1[0], layer1, allowed1, tables1, ffn_sent1, lambda gate: ()
    )
    in1 = in1.astype(bf16)
    ffn_pack1 = ffn_pack1(in1)
    mid0, ffn_grads0, gain_mid0 = backward_ffn(
        in1.astype(f32), kept0, gains0[1], layer0, ffn_pack1
    )
    model_width = w_qkv.shape[1]
    ffn1 = reduce_part(ffn_pack1)
    ffn_sent0, ffn_pack0 = ffn_grads0(mid0)
    in0, attn_grads0, unused, gain_before, (ffn_pack0, unused) = backward_attn(
        mid0, kept0, gains0[0], layer0, allowed0, tables0, ffn_sent0,
        lambda gate: (ffn_pack0(gate), ffn1),
    )
    in0 = in0.astype(bf16)
    ffn0 = reduce_part_now(ffn_pack0)
    attn_pack1 = attn_grads1(in1, [gain_first1, gain_mid1])
    attn_pack0 = attn_grads0((), [gain_before(), gain_mid0])
    out1_terms = out1_of(ffn_pack0)
    out1 = (kept1["resid_mid"] + scatter_parts(*out1_terms)).astype(bf16)
    attn_width = attn_pack0.shape[1]
    packs = [pack.reshape(8, -1, attn_width) for pack in (attn_pack0, attn_pack1)]
    attn_rows = packs[0].shape[1]
    attn_both = after_all(joined(packs, 1).reshape(-1, attn_width), in0, out1)
    attn_both = reduce_part_now(attn_both)
    gain_start = 2 * model_width % attn_rows
    holds_gains = lax.axis_index(("zlo", "x")) == 2 * model_width // attn_rows
    attn_both = attn_both.reshape(2, attn_rows, attn_width)
    gain_rows = attn_both[:, gain_start : gain_start + 8]
    gain_sums = sum_tensor(gain_rows.astype(f32)).astype(bf16)
    gain_rows = jnp.where(holds_gains, gain_sums, gain_rows)
    attn_both = joined(
        [attn_both[:, :gain_start], gain_rows, attn_both[:, gain_start + 8 :]], 1
    )
    got_out = swap_section(jnp.where(is_first, out1, out0))
    got_in = swap_section(jnp.where(is_first, in1, in0))
    part0 = joined([ffn0, attn_both[0].reshape(-1, model_width)])
    part1 = joined([ffn1, attn_both[1].reshape(-1, model_width)])
    own_part, sent_part = pick_sections(is_first, part0, part1)
    sent_part = after_all(sent_part, got_in, got_out)
    part = (own_part.astype(f32) + swap_section(sent_part).astype(f32)).astype(bf16)
    ffn_rows = ffn0.shape[0]
    ffn_half = spread_part(part[:ffn_rows])
    attn_part = after_all(part[ffn_rows:].reshape(-1, attn_width), ffn_half)
    attn_half = spread_part(attn_part)
    is_core0 = lax.axis_index("core") == 0

    def of_core(core, halves, start, count):
        mine, other = (both[start : start + count] for both in halves)
        return jnp.where(is_core0 == (core == 0), mine, other).astype(f32)

    ffn_halves = (ffn_half, swap_core(ffn_half))
    down_rows = w_down.shape[1] // 2
    grad_up = jnp.stack([of_core(core, ffn_halves, 0, hidden_width) for core in range(2)])
    grad_down = joined(
        [of_core(core, ffn_halves, hidden_width, down_rows) for core in range(2)]
    )
    attn_half, grad_up, grad_down = lax.optimization_barrier((attn_half, grad_up, grad_down))
    attn_halves = (attn_half, swap_core(attn_half))
    gain_total = sum(of_core(core, attn_halves, 2 * model_width, 8) for core in range(2))
    gain_total = gain_total.reshape(2, -1)
    grad_qkv = jnp.stack(
        [
            of_core(0, attn_halves, 0, model_width),
            of_core(0, attn_halves, model_width, model_width),
            of_core(1, attn_halves, 0, model_width),
        ]
    )
    grad_out = of_core(1, attn_halves, model_width, model_width).T

    section_out = jnp.stack(
        [jnp.where(is_first, out0, got_out), jnp.where(is_first, got_out, out1)]
    )
    input_grads = jnp.stack(
        [jnp.where(is_first, in0, got_in), jnp.where(is_first, got_in, in1)]
    )
    return (
        section_out[None],
        input_grads[None],
        gain_total[None],
        jnp.transpose(grad_qkv, (1, 0, 2))[None],
        grad_out[None],
        jnp.transpose(grad_up, (2, 0, 1))[None],
        grad_down[None],
    )


def solution(mesh):
    sizes = dict(zip(mesh.axis_names, mesh.devices.shape))
    fine = Mesh(
        mesh.devices.reshape(sizes["section"], 2, sizes["dp"] // 4, 2, sizes["tensor"]),
        ("section", "zlo", "x", "core", "tensor"),
    )
    rows = ("zlo", "x", "core", "tensor")
    in_specs = (
        P(None, rows, None),
        P(None, rows, None),
        P(None, DP, None),
        P("section", None, None),
        P("section", None, None, "tensor"),
        P("section", "tensor", None),
        P("section", None, None, "tensor"),
        P("section", "tensor", None),
    )
    out_specs = (
        P("section", None, rows, None),
        P("section", None, rows, None),
        P("section", None, None),
        P("section", None, None, "tensor"),
        P("section", "tensor", None),
        P("section", None, None, "tensor"),
        P("section", "tensor", None),
    )
    return jax.shard_map(local, mesh=fine, in_specs=in_specs, out_specs=out_specs, check_vma=False)
```

```python
import functools

import jax
import jax.numpy as jnp
from jax import lax
from jax.experimental import pallas as pl
from jax.experimental.pallas import tpu as pltpu
from jax.sharding import Mesh
from jax.sharding import PartitionSpec as P

HEAD_DIM = 64
WINDOW = 128

epsilon = 1e-05
bf16 = jnp.bfloat16
f32 = jnp.float32

BLOCK = 256

DP = ("zlo", "x", "core")


def around(block, axis, distance):
    count = lax.axis_size(axis)
    return lax.ppermute(block, axis, [(i, (i + distance) % count) for i in range(count)])


def swap_core(block):
    return lax.ppermute(block, "core", [(0, 1), (1, 0)])


def swap_section(block):
    return lax.ppermute(block, "section", [(0, 1), (1, 0)])


def swap_layer(block):
    return lax.ppermute(block, ("section", "zlo"), [(0, 3), (1, 2), (2, 1), (3, 0)])


def gather_parts(block):
    far = around(block, "tensor", 2)
    ahead = around(block, "tensor", -1)
    behind = around(block, "tensor", 1)
    return [joined([block, ahead, behind]), far]


def scatter_parts(near, far):
    rows = far.shape[0]
    sent_far = around(far.astype(bf16), "tensor", 2)
    sent_ahead = around(near[rows : 2 * rows].astype(bf16), "tensor", 1)
    sent_behind = around(near[2 * rows :].astype(bf16), "tensor", -1)
    kept = near[:rows].astype(f32)
    return kept + sent_far.astype(f32) + sent_ahead.astype(f32) + sent_behind.astype(f32)


def joined(parts, axis=0):
    return jnp.concatenate(parts, axis=axis)


def after_all(values, *others):
    return lax.optimization_barrier((values,) + others)[0]


def sum_tensor(block):
    return (
        block
        + around(block, "tensor", 2)
        + around(block, "tensor", 1)
        + around(block, "tensor", -1)
    )


def layer_norm(values, gain_scale):
    centered = values - jnp.mean(values, axis=-1, keepdims=True)
    variance = jnp.mean(centered * centered, axis=-1, keepdims=True)
    return centered * lax.rsqrt(variance + epsilon) * gain_scale


def doc_layout(doc_lengths, indices):
    doc_ends = jnp.cumsum(doc_lengths)
    passed = indices[:, None] >= doc_ends[None, :]
    doc_ids = jnp.sum(passed.astype(jnp.int32), axis=1)
    starts = jnp.sum(jnp.where(passed, doc_lengths[None, :], 0), axis=1)
    return (doc_ids, indices - starts)


def rope_tables(positions, rope_base, heads):
    half_dim = HEAD_DIM // 2
    inverse = rope_base ** (-2.0 * jnp.arange(half_dim, dtype=f32) / HEAD_DIM)
    angles = positions.astype(f32)[:, None] * inverse
    cosine, sine = jnp.cos(angles), jnp.sin(angles)
    cosine = jnp.concatenate([cosine, cosine], axis=-1)
    sine = jnp.concatenate([-sine, sine], axis=-1)
    return (jnp.tile(cosine, (1, heads)), jnp.tile(sine, (1, heads)))


def contract_rows(left_rows, right_rows):
    return lax.dot_general(
        left_rows, right_rows, (((0,), (0,)), ((), ())), preferred_element_type=f32
    )


def contract_last(left_rows, weight):
    return lax.dot_general(
        left_rows, weight, (((1,), (1,)), ((), ())), preferred_element_type=f32
    )


def times(left_rows, weight):
    return jnp.dot(left_rows, weight, preferred_element_type=f32)


def gelu_product(first_half, second_half):
    return jax.nn.gelu(first_half, approximate=False) * second_half


def dot_nt(left, right):
    return lax.dot_general(left, right, (((1,), (1,)), ((), ())), preferred_element_type=f32)


def dot_tn(left, right):
    return lax.dot_general(left, right, (((0,), (0,)), ((), ())), preferred_element_type=f32)


def swap_halves(values):
    width = values.shape[1]
    lanes = lax.broadcasted_iota(jnp.int32, values.shape, 1)
    up = pltpu.roll(values, width - HEAD_DIM // 2, 1)
    down = pltpu.roll(values, HEAD_DIM // 2, 1)
    return jnp.where(lanes % HEAD_DIM < HEAD_DIM // 2, up, down)


def excluded_bias(marks_row, marks_col, start, windowed):
    docs = marks_row[0:1, pl.ds(start, BLOCK)]
    allowed = marks_col[:, 0:1] == docs
    if windowed:
        apart = marks_col[:, 1:2] - marks_row[1:2, pl.ds(start, BLOCK)]
        allowed = allowed & (jnp.abs(apart) <= WINDOW // 2)
    return jnp.where(allowed, 0.0, -1e30)


def attend_kernel(
    windowed,
    near, far, w_qkv, w_out, cosine, sine, marks_row, marks_col,
    queries, keys, values, logs, attended, near_term, far_term,
    projected,
):
    near_rows = near.shape[0]
    width = w_out.shape[0]
    projected[:near_rows] = jnp.dot(near[...], w_qkv[...], preferred_element_type=f32)
    projected[near_rows:] = jnp.dot(far[...], w_qkv[...], preferred_element_type=f32)
    for index, target in ((0, queries), (1, keys)):
        part = projected[:, index * width : (index + 1) * width]
        turned = part * cosine[...] + swap_halves(part) * sine[...]
        target[...] = turned.astype(bf16)
    values[...] = projected[:, 2 * width :].astype(bf16)
    heads = width // HEAD_DIM
    lanes = lax.broadcasted_iota(jnp.int32, (BLOCK, width), 1) // HEAD_DIM

    def step(index, carry):
        start = pl.multiple_of(index * BLOCK, BLOCK)
        bias = excluded_bias(marks_row, marks_col, start, windowed)
        block = queries[pl.ds(start, BLOCK)] * jnp.asarray(HEAD_DIM ** (-0.5), bf16)
        total = jnp.zeros((BLOCK, width), f32)
        for head in range(heads):
            own = jnp.where(lanes == head, block, jnp.zeros_like(block))
            scores = dot_nt(keys[...], own) + bias
            largest = jnp.max(scores, axis=0, keepdims=True)
            powers = jnp.exp(scores - largest)
            sums = jnp.sum(powers, axis=0, keepdims=True)
            soft = (powers * (1.0 / sums)).astype(bf16)
            logs[pl.ds(head, 1), pl.ds(start, BLOCK)] = largest + jnp.log(sums)
            total = jnp.where(lanes == head, dot_tn(soft, values[...]), total)
        attended[pl.ds(start, BLOCK)] = total.astype(bf16)
        return carry

    lax.fori_loop(0, queries.shape[0] // BLOCK, step, 0)
    far_term[...] = jnp.dot(
        attended[near_rows:], w_out[...], preferred_element_type=f32
    ).astype(bf16)
    near_term[...] = jnp.dot(
        attended[:near_rows], w_out[...], preferred_element_type=f32
    ).astype(bf16)


def attend_back_kernel(
    windowed,
    near, far, w_qkv, w_out, cosine, sine, marks_row, marks_col,
    queries, keys, values, logs,
    grad_projected, near_term, far_term,
    grad_attended, grad_queries, grad_keys, grad_values,
):
    near_rows = near.shape[0]
    width = w_out.shape[0]
    grad_attended[:near_rows] = dot_nt(near[...], w_out[...]).astype(bf16)
    grad_attended[near_rows:] = dot_nt(far[...], w_out[...]).astype(bf16)
    grad_keys[...] = jnp.zeros_like(grad_keys)
    grad_values[...] = jnp.zeros_like(grad_values)
    heads = width // HEAD_DIM
    lanes = lax.broadcasted_iota(jnp.int32, (BLOCK, width), 1) // HEAD_DIM
    all_lanes = lax.broadcasted_iota(jnp.int32, queries.shape, 1) // HEAD_DIM

    def step(index, carry):
        start = pl.multiple_of(index * BLOCK, BLOCK)
        bias = excluded_bias(marks_row, marks_col, start, windowed)
        block = queries[pl.ds(start, BLOCK)] * jnp.asarray(HEAD_DIM ** (-0.5), bf16)
        grad_block = grad_attended[pl.ds(start, BLOCK)]
        total = jnp.zeros((BLOCK, width), f32)
        more_keys = jnp.zeros(queries.shape, f32)
        more_values = jnp.zeros(queries.shape, f32)
        for head in range(heads):
            own = jnp.where(lanes == head, block, jnp.zeros_like(block))
            own_grad = jnp.where(lanes == head, grad_block, jnp.zeros_like(grad_block))
            scores = dot_nt(keys[...], own) + bias
            soft = jnp.exp(scores - logs[pl.ds(head, 1), pl.ds(start, BLOCK)])
            grad_soft = dot_nt(values[...], own_grad)
            dots = jnp.sum(soft * grad_soft, axis=0, keepdims=True)
            grad_scores = (soft * (grad_soft - dots)).astype(bf16)
            more_values += jnp.dot(soft.astype(bf16), own_grad, preferred_element_type=f32)
            more_keys += jnp.dot(grad_scores, own, preferred_element_type=f32)
            total = jnp.where(lanes == head, dot_tn(grad_scores, keys[...]), total)
        grad_queries[pl.ds(start, BLOCK)] = total * HEAD_DIM ** (-0.5)
        grad_keys[...] += more_keys
        grad_values[...] += more_values
        return carry

    lax.fori_loop(0, queries.shape[0] // BLOCK, step, 0)
    for index, source in ((0, grad_queries), (1, grad_keys)):
        part = source[...]
        back = part * cosine[...] - swap_halves(part) * sine[...]
        grad_projected[:, index * width : (index + 1) * width] = back.astype(bf16)
    grad_projected[:, 2 * width :] = grad_values[...].astype(bf16)
    far_term[...] = dot_nt(grad_projected[near_rows:], w_qkv[...]).astype(bf16)
    near_term[...] = dot_nt(grad_projected[:near_rows], w_qkv[...]).astype(bf16)


def whole_call(kernel, out_shapes, scratch_shapes, flops, *operands):
    whole = pl.BlockSpec(memory_space=pltpu.VMEM)
    return pl.pallas_call(
        kernel,
        out_shape=[jax.ShapeDtypeStruct(*shape) for shape in out_shapes],
        in_specs=[whole] * len(operands),
        out_specs=[whole] * len(out_shapes),
        scratch_shapes=scratch_shapes,
        compiler_params=pltpu.CompilerParams(vmem_limit_bytes=40 * 1024 * 1024),
        cost_estimate=pl.CostEstimate(flops=flops, bytes_accessed=8 << 20, transcendentals=1 << 20),
    )(*operands)


def in_turn(work, parts):
    first = work(0, parts[0])
    return first, work(1, after_all(parts[1], first))


def forward_layer(inputs, normed_parts, gain_mid, weights, allowed, tables, late, points):
    w_qkv, w_out = weights[0], weights[1]
    near_rows, model_width = normed_parts[0].shape
    far_rows = normed_parts[1].shape[0]
    full_rows = near_rows + far_rows
    width = w_out.shape[0]
    windowed, marks_row, marks_col = allowed
    queries, keys, values, logs, attended, near_term, far_term = whole_call(
        functools.partial(attend_kernel, windowed),
        [((full_rows, width), bf16)] * 3
        + [((8, full_rows), f32), ((full_rows, width), bf16)]
        + [((near_rows, model_width), bf16), ((far_rows, model_width), bf16)],
        [pltpu.VMEM((full_rows, 3 * width), f32)],
        3 << 30,
        *normed_parts, w_qkv, w_out, *tables, marks_row, marks_col,
    )
    points[1](far_term)
    resid_mid = inputs + scatter_parts(near_term, far_term)
    points[2](resid_mid)
    mid_parts = gather_parts(layer_norm(resid_mid, gain_mid).astype(bf16))
    points[3](mid_parts)
    w_up, w_down = weights[2], weights[3]

    def feed(k, part):
        hidden = contract_last(part, w_up)
        local_hidden = hidden.shape[1] // 2
        gelu_in = hidden[:, :local_hidden]
        gate_mult = hidden[:, local_hidden:]
        mixed = gelu_product(gelu_in, gate_mult).astype(bf16)
        return gelu_in, gate_mult, mixed, None if late else times(mixed, w_down).astype(bf16)

    fed = in_turn(feed, mid_parts)
    if late:

        def result(gate):
            held = after_all((fed[0][2], fed[1][2]), gate)
            return [times(mixed, w_down).astype(bf16) for mixed in held]

    else:
        result = resid_mid + scatter_parts(fed[0][3], fed[1][3])
    kept = dict(
        inputs=inputs,
        resid_mid=resid_mid,
        normed=normed_parts,
        queries=queries,
        keys=keys,
        values=values,
        logs=logs,
        attended=attended,
        normed_mid=mid_parts,
        gelu_in=(fed[0][0], fed[1][0]),
        gate_mult=(fed[0][1], fed[1][1]),
        mixed=(fed[0][2], fed[1][2]),
    )
    return (result, kept)


def backward_ffn(grad_result, kept, gain_mid, weights, gate):
    w_up, w_down = weights[2], weights[3]
    grad_parts = after_all(gather_parts(grad_result.astype(bf16)), gate)

    def feed_back(k, part):
        grad_mixed = contract_last(part, w_down)
        unused, pull_gelu = jax.vjp(gelu_product, kept["gelu_in"][k], kept["gate_mult"][k])
        terms = tuple(term.astype(bf16) for term in pull_gelu(grad_mixed))
        return terms[0], terms[1], times(joined(terms, 1), w_up).astype(bf16)

    near, far = in_turn(feed_back, grad_parts)
    grad_normed_mid = scatter_parts(near[2], far[2])
    unused, pull_norm = jax.vjp(layer_norm, kept["resid_mid"], gain_mid)
    grad_resid, grad_gain = pull_norm(grad_normed_mid)

    def weight_grads(gate):
        outer, inner, left, first, second = after_all(
            (grad_parts, kept["mixed"], kept["normed_mid"], (near[0], far[0]), (near[1], far[1])),
            gate,
        )
        outer, inner, left = joined(outer), joined(inner), joined(left)
        first, second = joined(first), joined(second)
        half = inner.shape[1] // 2
        front, back = inner[:, :half], inner[:, half:]
        sent_up, add_up = add_core(lambda core: contract_rows(core(first, second), left))
        sent_down, add_down = add_core(lambda core: contract_rows(core(front, back), outer))

        def pack(gate):
            up, down = add_up(gate), add_down(gate)
            rows = up.shape[0] + down.shape[0]
            blank = jnp.zeros((-rows % 128, up.shape[1]), bf16)
            return joined([up, down, blank])

        return (sent_up, sent_down), pack

    return (grad_result + grad_resid, weight_grads, grad_gain)


def backward_attn(grad_mid, kept, gain_first, weights, allowed, tables, gate, pack):
    w_qkv, w_out = weights[0], weights[1]
    grad_parts = gather_parts(grad_mid.astype(bf16))
    near, far = after_all(grad_parts, gate)
    full_rows, width = kept["queries"].shape
    windowed, marks_row, marks_col = allowed
    grad_projected, near_term, far_term = whole_call(
        functools.partial(attend_back_kernel, windowed),
        [((full_rows, 3 * width), bf16), (near.shape, bf16), (far.shape, bf16)],
        [pltpu.VMEM((full_rows, width), bf16)] + [pltpu.VMEM((full_rows, width), f32)] * 3,
        4 << 30,
        near, far, w_qkv, w_out, *tables, marks_row, marks_col,
        kept["queries"], kept["keys"], kept["values"], kept["logs"],
    )
    packed = pack(grad_projected)
    near_term, far_term = after_all((near_term, far_term), packed)
    grad_normed = scatter_parts(near_term, far_term)
    unused, pull_norm = jax.vjp(layer_norm, kept["inputs"], gain_first)
    grad_resid, grad_gain = pull_norm(grad_normed)

    def gain_before():
        total = 0.0
        for term, normed in zip((near_term, far_term), kept["normed"]):
            total = total + jnp.sum(term.astype(f32) * normed.astype(f32), axis=0)
        return total / gain_first

    def weight_grads(gate, gains):
        outer, inner, left, right = after_all(
            (grad_parts, kept["attended"], kept["normed"], grad_projected), gate
        )
        outer, left = joined(outer), joined(left)
        width = inner.shape[1]
        of_q, of_k, of_v = (right[:, i * width : (i + 1) * width] for i in range(3))
        one = add_core(lambda core: contract_rows(left, core(of_q, of_v)))[1](())
        two = add_core(lambda core: contract_rows(core(left, outer), core(of_k, inner)))[1](())
        extra = jnp.stack(gains).astype(bf16).reshape(-1, width)
        blank = jnp.zeros((-extra.shape[0] % 128, width), bf16)
        return joined([one, two, extra, blank])

    return (grad_mid + grad_resid, weight_grads, grad_gain, gain_before, packed)


def fetch_half(own, after):
    piece = own.shape[0] // 2
    start = lax.axis_index("core") * piece
    return swap_layer(lax.dynamic_slice_in_dim(after_all(own, after), start, piece))


def both_halves(half, after=()):
    half = after_all(half, after)
    return in_order(lax.axis_index("core"), half, swap_core(half))


def by_layer(is_first, own, other):
    return jnp.where(is_first, own, other), jnp.where(is_first, other, own)


def in_order(index, mine, other):
    low = jnp.where(index == 0, mine, other)
    high = jnp.where(index == 0, other, mine)
    return jnp.concatenate([low, high], axis=0)


def add_core(product):
    is_core0 = lax.axis_index("core") == 0
    sent = product(lambda one, two: jnp.where(is_core0, two, one)).astype(bf16)

    def add(gate):
        held = product(lambda one, two: after_all(jnp.where(is_core0, one, two), gate))
        return (held + swap_core(sent).astype(f32)).astype(bf16)

    return sent, add


def reduce_part(grads):
    return lax.psum_scatter(grads, ("zlo", "x"), scatter_dimension=0, tiled=True)


def reduce_part_now(grads):
    pieces = lax.all_to_all(grads, ("zlo", "x"), 0, 0, tiled=True)
    pieces = pieces.reshape(8, -1, pieces.shape[1])
    return jnp.sum(pieces.astype(f32), axis=0).astype(bf16)


def spread_part(part):
    copies = jnp.broadcast_to(part[None], (8,) + part.shape).reshape(-1, part.shape[1])
    return lax.all_to_all(copies, ("zlo", "x"), 0, 0, tiled=True)


def pick_sections(is_first, part_first, part_second):
    own = jnp.where(is_first, part_first, part_second)
    sent = jnp.where(is_first, part_second, part_first)
    return own, sent


def local(tokens, cotangent, lengths, gains, w_qkv, w_out, w_up, w_down):
    section_index = lax.axis_index("section")
    is_first = section_index == 0
    row_count = tokens.shape[1]
    full_rows = row_count * lax.axis_size("tensor")
    start_rows = jnp.where(is_first, tokens[0], tokens[1])
    end_grads = jnp.where(is_first, cotangent[0], cotangent[1])
    start_parts = gather_parts(start_rows)
    gains_other = swap_layer(gains[0])
    gains0 = jnp.where(is_first, gains[0], gains_other)
    gains1 = jnp.where(is_first, gains_other, gains[0])
    start_rows = start_rows.astype(f32)
    own = (
        jnp.transpose(w_qkv[0], (1, 0, 2)).reshape(-1, w_qkv.shape[3]),
        w_out[0],
        jnp.transpose(w_up[0], (1, 2, 0)).reshape(-1, w_up.shape[1]),
        w_down[0],
    )
    half_qkv = fetch_half(own[0], ())
    half_out = fetch_half(own[1], ())
    start_parts, lengths = after_all((start_parts, lengths), (half_qkv, half_out))
    first_parts = in_turn(
        lambda k, part: layer_norm(part.astype(f32), gains0[0]).astype(bf16), start_parts
    )
    qkv0, qkv1 = by_layer(is_first, own[0], both_halves(half_qkv))
    layer0 = [joined(jnp.split(qkv0, 3), 1)]
    layer1 = [joined(jnp.split(qkv1, 3), 1)]
    hidden_width = w_up.shape[3]
    moving = []

    out0, out1 = by_layer(is_first, own[1], both_halves(half_out))
    layer0.append(out0)
    layer1.append(out1)
    moving.append(fetch_half(own[2][:hidden_width], half_out))

    def at_far_term(far_term):
        moving.append(both_halves(moving[0], far_term))
        moving.append(fetch_half(own[2][hidden_width:], (moving[0], far_term)))

    def at_mid(resid_mid):
        moving.append(both_halves(moving[2], resid_mid))
        moving.append(fetch_half(own[3], (moving[2], resid_mid)))

    def at_gathered(parts):
        up0, up1 = by_layer(is_first, own[2], joined([moving[1], moving[3]]))
        down0, down1 = by_layer(is_first, own[3], both_halves(moving[4], parts))
        layer0.extend([up0, down0])
        layer1.extend([up1, down1])

    points = (None, at_far_term, at_mid, at_gathered)

    doc_lengths = jnp.where(is_first, lengths[0, 0], lengths[1, 0])
    indices = jnp.arange(full_rows, dtype=jnp.int32)
    blocks = jnp.array([0, 1, 3, 2], jnp.int32) + lax.axis_index("tensor")
    indices = (jnp.repeat(blocks, row_count) * row_count + indices % row_count) % full_rows
    doc_ids, positions = doc_layout(doc_lengths, indices)
    marks_row = jnp.stack([doc_ids, indices])
    marks_col = jnp.stack([doc_ids, indices], axis=1)
    allowed0 = (True, marks_row, marks_col)
    allowed1 = (False, marks_row, marks_col)
    heads = w_out.shape[1] // HEAD_DIM
    tables0 = rope_tables(positions, 10000.0, heads)
    tables1 = rope_tables(positions, 160000.0, heads)

    out0, kept0 = forward_layer(
        start_rows, first_parts, gains0[1], layer0, allowed0, tables0, False, points
    )
    out0 = out0.astype(bf16)
    second_rows = out0.astype(f32)
    second_parts = gather_parts(layer_norm(second_rows, gains1[0]).astype(bf16))
    out1_of, kept1 = forward_layer(
        second_rows, second_parts, gains1[1], layer1, allowed1, tables1, True, (lambda value: None,) * 4
    )
    mid1, ffn_grads1, gain_mid1 = backward_ffn(
        end_grads.astype(f32), kept1, gains1[1], layer1, ()
    )
    ffn_sent1, ffn_pack1 = ffn_grads1(mid1)
    in1, attn_grads1, gain_first1, unused, unused = backward_attn(
        mid1, kept1, gains1[0], layer1, allowed1, tables1, ffn_sent1, lambda gate: ()
    )
    in1 = in1.astype(bf16)
    ffn_pack1 = ffn_pack1(in1)
    mid0, ffn_grads0, gain_mid0 = backward_ffn(
        in1.astype(f32), kept0, gains0[1], layer0, ffn_pack1
    )
    model_width = w_qkv.shape[1]
    ffn1 = reduce_part(ffn_pack1)
    ffn_sent0, ffn_pack0 = ffn_grads0(mid0)
    in0, attn_grads0, unused, gain_before, (ffn_pack0, unused) = backward_attn(
        mid0, kept0, gains0[0], layer0, allowed0, tables0, ffn_sent0,
        lambda gate: (ffn_pack0(gate), ffn1),
    )
    in0 = in0.astype(bf16)
    ffn0 = reduce_part_now(ffn_pack0)
    attn_pack1 = attn_grads1(in1, [gain_first1, gain_mid1])
    attn_pack0 = attn_grads0((), [gain_before(), gain_mid0])
    out1_terms = out1_of(ffn_pack0)
    out1 = (kept1["resid_mid"] + scatter_parts(*out1_terms)).astype(bf16)
    attn_width = attn_pack0.shape[1]
    packs = [pack.reshape(8, -1, attn_width) for pack in (attn_pack0, attn_pack1)]
    attn_rows = packs[0].shape[1]
    attn_both = after_all(joined(packs, 1).reshape(-1, attn_width), in0)
    attn_both = reduce_part_now(attn_both)
    gain_start = 2 * model_width % attn_rows
    holds_gains = lax.axis_index(("zlo", "x")) == 2 * model_width // attn_rows
    attn_both = attn_both.reshape(2, attn_rows, attn_width)
    gain_rows = attn_both[:, gain_start : gain_start + 8]
    gain_sums = sum_tensor(gain_rows.astype(f32)).astype(bf16)
    gain_rows = jnp.where(holds_gains, gain_sums, gain_rows)
    attn_both = joined(
        [attn_both[:, :gain_start], gain_rows, attn_both[:, gain_start + 8 :]], 1
    )
    got_out = swap_section(jnp.where(is_first, out1, out0))
    got_in = swap_section(jnp.where(is_first, in1, in0))
    part0 = joined([ffn0, attn_both[0].reshape(-1, model_width)])
    part1 = joined([ffn1, attn_both[1].reshape(-1, model_width)])
    own_part, sent_part = pick_sections(is_first, part0, part1)
    sent_part = after_all(sent_part, got_in, got_out)
    part = (own_part.astype(f32) + swap_section(sent_part).astype(f32)).astype(bf16)
    ffn_rows = ffn0.shape[0]
    ffn_half = spread_part(part[:ffn_rows])
    attn_part = after_all(part[ffn_rows:].reshape(-1, attn_width), ffn_half)
    attn_half = spread_part(attn_part)
    is_core0 = lax.axis_index("core") == 0

    def of_core(core, halves, start, count):
        mine, other = (both[start : start + count] for both in halves)
        return jnp.where(is_core0 == (core == 0), mine, other).astype(f32)

    ffn_halves = (ffn_half, swap_core(ffn_half))
    down_rows = w_down.shape[1] // 2
    grad_up = jnp.stack([of_core(core, ffn_halves, 0, hidden_width) for core in range(2)])
    grad_down = joined(
        [of_core(core, ffn_halves, hidden_width, down_rows) for core in range(2)]
    )
    attn_half, grad_up, grad_down = lax.optimization_barrier((attn_half, grad_up, grad_down))
    attn_halves = (attn_half, swap_core(attn_half))
    gain_total = sum(of_core(core, attn_halves, 2 * model_width, 8) for core in range(2))
    gain_total = gain_total.reshape(2, -1)
    grad_qkv = jnp.stack(
        [
            of_core(0, attn_halves, 0, model_width),
            of_core(0, attn_halves, model_width, model_width),
            of_core(1, attn_halves, 0, model_width),
        ]
    )
    grad_out = of_core(1, attn_halves, model_width, model_width).T

    section_out = jnp.stack(
        [jnp.where(is_first, out0, got_out), jnp.where(is_first, got_out, out1)]
    )
    input_grads = jnp.stack(
        [jnp.where(is_first, in0, got_in), jnp.where(is_first, got_in, in1)]
    )
    return (
        section_out[None],
        input_grads[None],
        gain_total[None],
        jnp.transpose(grad_qkv, (1, 0, 2))[None],
        grad_out[None],
        jnp.transpose(grad_up, (2, 0, 1))[None],
        grad_down[None],
    )


def solution(mesh):
    sizes = dict(zip(mesh.axis_names, mesh.devices.shape))
    fine = Mesh(
        mesh.devices.reshape(sizes["section"], 2, sizes["dp"] // 4, 2, sizes["tensor"]),
        ("section", "zlo", "x", "core", "tensor"),
    )
    rows = ("zlo", "x", "core", "tensor")
    in_specs = (
        P(None, rows, None),
        P(None, rows, None),
        P(None, DP, None),
        P("section", None, None),
        P("section", None, None, "tensor"),
        P("section", "tensor", None),
        P("section", None, None, "tensor"),
        P("section", "tensor", None),
    )
    out_specs = (
        P("section", None, rows, None),
        P("section", None, rows, None),
        P("section", None, None),
        P("section", None, None, "tensor"),
        P("section", "tensor", None),
        P("section", None, None, "tensor"),
        P("section", "tensor", None),
    )
    return jax.shard_map(local, mesh=fine, in_specs=in_specs, out_specs=out_specs, check_vma=False)
```
